512 devices in a mesh: req: 8 (over z_lo, core), ctx: 16 (over x, z_hi), tp: 4 (over y).
Axes of the slice: x: 4, y: 4, z: 16 (z_hi: 4, z_lo: 4; z = z_hi * 4 + z_lo), core: 2. Of those that a mesh axis runs over, the one named last changes fastest.
Arguments:
- queries: bfloat16 [64, 256, 64, 128], P('req', 'ctx', 'tp'), may hold values from -16 to 16
- kv_pool: bfloat16 [2, 8, 768, 8, 8, 128], P(None, 'req', 'ctx', None, 'tp'), may hold values from -16 to 16
- new_kv: bfloat16 [2, 64, 256, 8, 128], P(None, 'req', 'ctx', 'tp'), may hold values from -6 to 6
- block_table: int32 [8, 16, 48], P('req', 'ctx'), may hold values from 0 to 47, each once within a row
- cached_len: int32 [8, 8], P('req'), may hold values from 1 to 768, 3840 in all within a row
- new_len: int32 [8, 8], P('req'), may hold values from 1 to 256, 1536 in all within a row
- mamba_x: bfloat16 [64, 256, 8192], P('req', 'ctx', 'tp'), may hold values from -6 to 6
- conv_state: bfloat16 [64, 3, 8192], P('req', None, 'tp'), may hold values from -6 to 6
- conv_weight: float32 [4, 8192], P(None, 'tp'), may hold values from -3 to 3
- conv_bias: float32 [8192], P('tp'), may hold values from -3 to 3
- x_proj: bfloat16 [32, 8192], P(None, 'tp'), may hold values from -0.0625 to 0.0625
- dt_raw: bfloat16 [64, 256, 8192], P('req', 'ctx', 'tp'), may hold values from -6 to 4
- a_log: float32 [16, 8192], P(None, 'tp'), may hold values from -3 to 0.5
- skip_gain: float32 [8192], P('tp'), may hold values from 0.5 to 1.5
- ssm_state: bfloat16 [64, 16, 8192], P('req', None, 'tp'), may hold values from -6 to 6
- target_group: int32 [8, 8], P('req'), may hold values from 0 to 7, as said below
Outputs:
- attended: bfloat16 [64, 256, 64, 128], P('req', 'ctx', 'tp')
- mixed: bfloat16 [64, 256, 8192], P('req', 'ctx', 'tp')
The draws below stay inside these ranges and needn't reach their ends.
Inputs may be any that keep to these rules, and one draw needn't show every extreme that they name: `target_group`: each row names every group exactly 1 times.
All inputs are finite; a program needn't handle non-finite values.
Results may differ from the reference program's by a relative error of at most 0.013.
Values may be sent and summed in bfloat16 or wider, within the bound.
A program may use at most 128 MiB of HBM per device.

```python
import math
import jax
import jax.numpy as jnp
import numpy as np
from jax import lax

HEADS = 64
KVH = 8
HD = 128
STATE = 16
CONV = 4
MCH = 8192
REQ_GRP = 8
PAGE = 8
CACHE_DEV = 48
NEW = 256
CACHE = 768
REQS = 64
PAGES = 48
N_REQ = 8
N_CTX = 16


def draw_queries(key, part):
    key = jax.random.fold_in(key, 3)
    tensor_extents = (REQS, NEW, HEADS, HD)
    values = jnp.clip(jax.random.normal(key, tensor_extents, jnp.float32), -6.0, 6.0)
    return values.astype(jnp.bfloat16)


def draw_kv_pool(key, part):
    key = jax.random.fold_in(key, 4)
    groups = REQS // REQ_GRP
    blocks = CACHE // CACHE_DEV
    tensor_extents = (2, groups, blocks * PAGES, PAGE, KVH, HD)
    values = jnp.clip(jax.random.normal(key, tensor_extents, jnp.float32), -6.0, 6.0)
    return values.astype(jnp.bfloat16)


def draw_dt_raw(key, part):
    key = jax.random.fold_in(key, 5)
    tensor_extents = (REQS, NEW, MCH)
    starting_displacement = -3.0 + 0.5 * jnp.clip(jax.random.normal(key, tensor_extents, jnp.float32), -4.0, 4.0)
    spots = jax.random.randint(jax.random.fold_in(key, 1), (REQS, 3), 0, NEW)
    equality_detected = jnp.any(jnp.arange(NEW, dtype=jnp.int32)[None, :, None] == spots[:, None, :], axis=-1)
    contiguous_lines = 3.0 + 0.3 * jax.random.uniform(jax.random.fold_in(key, 2), tensor_extents, jnp.float32)
    return jnp.where(equality_detected[:, :, None], contiguous_lines, starting_displacement).astype(jnp.bfloat16)


def draw_a_log(key, part):
    key = jax.random.fold_in(key, 7)
    slow = jax.random.randint(jax.random.fold_in(key, 1), (1, MCH), 0, 2) == 0
    slow_rate = jax.random.uniform(jax.random.fold_in(key, 2), (STATE, MCH), jnp.float32, 0.07, 0.15)
    fast_rate = jax.random.uniform(jax.random.fold_in(key, 3), (STATE, MCH), jnp.float32, 0.5, 1.5)
    return jnp.log(jnp.where(slow, slow_rate, fast_rate)).astype(jnp.float32)


def draw_target_group(key, part):
    key = jax.random.fold_in(key, 9)
    groups = REQS // REQ_GRP
    keys = jax.random.split(key, groups)
    orders = jax.vmap(lambda one: jax.random.permutation(one, REQ_GRP))(keys)
    return (orders % groups).astype(jnp.int32)


def block_scale(stream_key, dims, cuts, low, high):
    factor_of = 1.0
    for axis_at, parts in cuts:
        steps = jax.random.uniform(jax.random.fold_in(jax.random.fold_in(stream_key, 6), axis_at), (parts,), jnp.float32, low / len(cuts), high / len(cuts))
        factor_of = factor_of * jnp.repeat(jnp.exp(steps), dims[axis_at] // parts).reshape((-1,) + (1,) * (len(dims) - 1 - axis_at))
    return factor_of


def length_profile(count, total, reach, slope):
    portions = [(1 << 20) // math.isqrt(rank ** slope) + 1 for rank in range(2, count + 1)]
    surplus, holding = total - reach - (count - 1), [1] * (count - 1)
    while surplus > 0:
        movable = [i for i in range(count - 1) if holding[i] < reach]
        whole, remaining = sum([portions[i] for i in movable]), surplus
        for i in movable:
            addition = min(reach - holding[i], max(1, remaining * portions[i] // whole), surplus)
            holding[i] = holding[i] + addition
            surplus = surplus - addition
    return np.array([reach] + holding)


def ragged_sizes(key, number_of, total, bound, lean):
    if number_of == 2:
        one = jax.random.randint(key, (), max(1, total - bound), min(bound, total - 1) + 1)
        return jnp.stack([one, total - one])
    lengths = jnp.asarray(length_profile(number_of, total, bound, lean), jnp.int32)
    pairs = (number_of - 1) // 2
    giver, sink = lengths[1:1 + 2 * pairs:2], lengths[2:2 + 2 * pairs:2]
    room = jnp.minimum(giver - 1, bound - sink)
    passed = jax.random.randint(jax.random.fold_in(key, 1), (pairs,), 0, 1 << 20) % (room + 1)
    lengths = lengths.at[1:1 + 2 * pairs:2].set(giver - passed).at[2:2 + 2 * pairs:2].set(sink + passed)
    return lengths[jax.random.permutation(jax.random.fold_in(key, 2), number_of)]


def gaussian(rng, shape, deviation, reach, pieces=(), held_as=jnp.bfloat16):
    values = deviation * jax.random.normal(rng, shape, jnp.float32)
    if pieces:
        values = values * block_scale(rng, shape, pieces, -0.22, 0.18)
    return jnp.clip(values, -reach, reach).astype(held_as)


def setup_inputs(seed: int = 0) -> dict:
    streams_of = jax.random.split(jax.random.key(seed), 17)
    queries = draw_queries(jax.random.fold_in(streams_of[16], 71), 0)
    kv_pool = draw_kv_pool(jax.random.fold_in(streams_of[16], 71), 0)
    new_kv = gaussian(streams_of[2], (2, REQS, NEW, KVH, HD), 1.0, 6.0, ((1, 8), (2, 16), (3, 4)))
    block_table = jax.vmap(lambda own: jax.random.permutation(own, PAGES))(jax.random.split(streams_of[3], N_REQ * N_CTX)).reshape((N_REQ, N_CTX, PAGES)).astype(jnp.int32)
    cached_len = jax.vmap(lambda own: ragged_sizes(own, REQ_GRP, 5 * CACHE, CACHE, 2))(jax.random.split(streams_of[4], N_REQ)).reshape((N_REQ, REQ_GRP)).astype(jnp.int32)
    new_len = jax.vmap(lambda own: ragged_sizes(own, REQ_GRP, 6 * NEW, NEW, 1))(jax.random.split(streams_of[5], N_REQ)).reshape((N_REQ, REQ_GRP)).astype(jnp.int32)
    mamba_x = gaussian(streams_of[6], (REQS, NEW, MCH), 1.0, 6.0, ((0, 8), (1, 16), (2, 4)))
    conv_state = gaussian(streams_of[7], (REQS, CONV - 1, MCH), 1.0, 6.0, ((0, 8), (2, 4)))
    conv_weight = gaussian(streams_of[8], (CONV, MCH), CONV ** -0.5, 3.0, ((1, 4),), jnp.float32)
    conv_bias = gaussian(streams_of[9], (MCH,), 0.5, 3.0, ((0, 4),), jnp.float32)
    x_proj = gaussian(streams_of[10], (2 * STATE, MCH), MCH ** -0.5, 0.0625, ((1, 4),))
    dt_raw = draw_dt_raw(jax.random.fold_in(streams_of[16], 71), 0)
    a_log = draw_a_log(jax.random.fold_in(streams_of[16], 71), 0)
    skip_gain = jnp.clip(1.0 + 0.1 * jax.random.normal(streams_of[13], (MCH,), jnp.float32), 0.5, 1.5)
    ssm_state = gaussian(streams_of[14], (REQS, STATE, MCH), 1.0, 6.0, ((0, 8), (2, 4)))
    target_group = draw_target_group(jax.random.fold_in(streams_of[16], 71), 0)
    return dict(queries=queries, kv_pool=kv_pool, new_kv=new_kv, block_table=block_table, cached_len=cached_len, new_len=new_len, mamba_x=mamba_x, conv_state=conv_state, conv_weight=conv_weight, conv_bias=conv_bias, x_proj=x_proj, dt_raw=dt_raw, a_log=a_log, skip_gain=skip_gain, ssm_state=ssm_state, target_group=target_group)


def cache_of(kv_pool, block_table):
    groups = kv_pool.shape[1]
    offsets = (jnp.arange(N_CTX, dtype=jnp.int32) * PAGES)[:, None]
    indices = (block_table + offsets[None]).reshape(groups, N_CTX * PAGES).astype(jnp.int32)
    pools = jnp.moveaxis(kv_pool, 1, 0)
    picked = jax.vmap(lambda pool, where_idx: jnp.take(pool, where_idx, axis=1))(pools, indices)
    picked = picked.reshape(groups, 2, N_CTX, REQ_GRP, CACHE_DEV, KVH, HD)
    picked = picked.transpose(1, 0, 3, 2, 4, 5, 6)
    return picked.reshape(2, REQS, CACHE, KVH, HD)


def attend_one(items):
    query, cached_key_pages, cache_v, fresh_k, new_value_rows, clen, nlen = items
    keys = jnp.concatenate([cached_key_pages, fresh_k], axis=0).astype(jnp.float32)
    values = jnp.concatenate([cache_v, new_value_rows], axis=0).astype(jnp.float32)
    groups = HEADS // KVH
    grouped = query.reshape(NEW, KVH, groups, HD).astype(jnp.float32)
    scores = jnp.einsum("tkgd,nkd->kgtn", grouped, keys) * (HD ** -0.5)
    token_location = jnp.arange(CACHE + NEW, dtype=jnp.int32)
    tpos = jnp.arange(NEW, dtype=jnp.int32)
    fresh_pos = token_location - CACHE
    fresh_ok = (fresh_pos[None, :] <= tpos[:, None]) & (fresh_pos[None, :] < nlen)
    stored_entry_usable = jnp.broadcast_to((token_location < clen)[None, :], (NEW, CACHE + NEW))
    valid = jnp.where((token_location < CACHE)[None, :], stored_entry_usable, fresh_ok)
    scores = jnp.where(valid[None, None], scores, -1e30)
    top = jnp.max(scores, axis=-1, keepdims=True)
    weight = jnp.where(valid[None, None], jnp.exp(scores - top), 0.0)
    total = jnp.sum(weight, axis=-1)
    weight_b = weight.astype(jnp.bfloat16).astype(jnp.float32)
    summed = jnp.einsum("kgtn,nkd->kgtd", weight_b, values) / total[..., None]
    summed = summed.transpose(2, 0, 1, 3).reshape(NEW, HEADS, HD)
    live = tpos < nlen
    return jnp.where(live[:, None, None], summed, 0.0).astype(jnp.bfloat16)


def reference(queries, kv_pool, new_kv, block_table, cached_len, new_len, mamba_x, conv_state, conv_weight, conv_bias, x_proj, dt_raw, a_log, skip_gain, ssm_state, target_group):
    cache_kv = cache_of(kv_pool, block_table)
    clens = cached_len.reshape(REQS)
    nlens = new_len.reshape(REQS)
    attention_all = lax.map(attend_one, (queries, cache_kv[0], cache_kv[1], new_kv[0], new_kv[1], clens, nlens))

    padded = jnp.concatenate([conv_state, mamba_x], axis=1).astype(jnp.float32)
    summed = conv_weight[0] * padded[:, 0:NEW]
    for tap in range(1, CONV):
        summed = summed + conv_weight[tap] * padded[:, tap:tap + NEW]
    x_conv = jax.nn.silu(summed + conv_bias).astype(jnp.bfloat16)
    proj = jnp.einsum("rtc,sc->rts", x_conv.astype(jnp.float32), x_proj.astype(jnp.float32))
    in_vec = proj[..., :STATE]
    out_vec = proj[..., STATE:]
    step_size = jax.nn.softplus(dt_raw.astype(jnp.float32))
    rates = -jnp.exp(a_log)
    values = x_conv.astype(jnp.float32)

    def advance(state, item):
        step, into, out, value = item
        state = jnp.exp(step[:, None, :] * rates[None]) * state + (step * value)[:, None, :] * into[:, :, None]
        return state, jnp.sum(out[:, :, None] * state, axis=1) + skip_gain * value

    sequence = (step_size.transpose(1, 0, 2), in_vec.transpose(1, 0, 2), out_vec.transpose(1, 0, 2), values.transpose(1, 0, 2))
    final_state, outputs = lax.scan(advance, ssm_state.astype(jnp.float32), sequence)
    mixed_all = outputs.transpose(1, 0, 2)
    live = jnp.arange(NEW, dtype=jnp.int32)[None, :] < nlens[:, None]
    mixed_all = jnp.where(live[:, :, None], mixed_all, 0.0).astype(jnp.bfloat16)

    ordering = target_group.reshape(REQS).astype(jnp.int32) * REQS + jnp.arange(REQS, dtype=jnp.int32)
    order = jnp.argsort(ordering, stable=True).astype(jnp.int32)
    return jnp.take(attention_all, order, axis=0), jnp.take(mixed_all, order, axis=0)
```

```python
import math

import jax
import jax.numpy as jnp
from jax import lax
from jax.experimental import pallas as pl
from jax.experimental.pallas import tpu as pltpu
from jax.sharding import PartitionSpec as P

MESH = pl.DeviceIdType.MESH
F32 = jnp.float32
BF16 = jnp.bfloat16
LOG2E = math.log2(math.e)
NREQ, NCTX, NTP = 8, 16, 4
R, T, C, S = 8, 16, 2048, 16
HD = 128
SPAN = 48
TILES = C // 128
Q, KV, ST, AO, PF = range(5)


def wrap(a, n):
    return lax.rem(a + n, n)


def tile_lanes(j):
    return pl.ds(pl.multiple_of(j * 128, 128), 128)


def copy_to(axis, peer, src, dst, send_sem, recv_sem):
    return pltpu.make_async_remote_copy(
        src_ref=src,
        dst_ref=dst,
        send_sem=send_sem,
        recv_sem=recv_sem,
        device_id={axis: peer},
        device_id_type=MESH,
    )


def kernel(
    qs, kvs, rs, xt, dtt, cwb, cs, xp, a2, a2o, s0, thr, nlr, meta,
    att, mix,
    qr, kvr, rr, rf, xc, xcb, dts, pp, pr, bb, cb, av, yl, yr,
    st_s, st_r, pf_s, pf_r, ao_s, ao_r, y_s, o_s, y_all, o_all,
    ctx_send, ctx_recv, rim_send, rim_recv, tp_send, tp_recv, req_send, req_recv,
):
    g, c, p = lax.axis_index("req"), lax.axis_index("ctx"), lax.axis_index("tp")

    barrier = pltpu.get_barrier_semaphore()
    for axis, me, n in (("ctx", c, NCTX), ("tp", p, NTP), ("req", g, NREQ)):

        def greet(k, carry, axis=axis, me=me, n=n):
            pl.semaphore_signal(
                barrier, inc=1, device_id={axis: wrap(me + k, n)}, device_id_type=MESH
            )
            return carry

        lax.fori_loop(1, n, greet, 0)
    pl.semaphore_wait(barrier, NCTX + NTP + NREQ - 3)

    def ctx_copy(kind, k, src, dst):
        return copy_to(
            "ctx", wrap(c + k, NCTX), src, dst, ctx_send.at[kind, k], ctx_recv.at[kind, k]
        )

    def ctx_wait_recv(kind, dst):
        def one(k, carry):
            slot = dst.at[wrap(c - k, NCTX)]
            ctx_copy(kind, k, slot, slot).wait_recv()
            return carry

        lax.fori_loop(1, NCTX, one, 0)

    def ctx_wait_send(kind, src):
        def one(k, carry):
            slot = src.at[wrap(c + k, NCTX)]
            ctx_copy(kind, k, slot, slot).wait_send()
            return carry

        lax.fori_loop(1, NCTX, one, 0)

    rim = copy_to("ctx", wrap(c + 1, NCTX), rs, rr, rim_send, rim_recv)
    rim.start()

    def send_qkv(k, carry):
        peer = wrap(c + k, NCTX)
        ctx_copy(KV, k, kvs.at[peer], kvr.at[c]).start()
        ctx_copy(Q, k, qs.at[peer], qr.at[c]).start()
        return carry

    lax.fori_loop(1, NCTX, send_qkv, 0)
    qr[c] = qs[c]
    kvr[c] = kvs[c]

    def soften(j, carry):
        lanes = tile_lanes(j)
        d = dtt[:, lanes].astype(F32)
        dts[:, lanes] = jnp.maximum(d, 0.0) + jnp.log1p(jnp.exp(-jnp.abs(d)))
        return carry

    lax.fori_loop(0, TILES, soften, 0)

    rim.wait_recv()
    first = c == 0
    for k in range(3):
        got = rr[k].astype(F32)
        for half in range(2):
            cols = slice(half * 1024, half * 1024 + 1024)
            rows = slice(k * R, k * R + R)
            rf[rows, cols] = jnp.where(first, cs[rows, cols], got[half * R : half * R + R])

    def convolve(j, carry):
        lanes = tile_lanes(j)
        padded = jnp.concatenate([rf[:, lanes], xt[:, lanes].astype(F32)], axis=0)
        total = cwb[0:1, lanes] * padded[0 : T * R]
        for k in range(1, 4):
            total = total + cwb[k : k + 1, lanes] * padded[k * R : k * R + T * R]
        total = total + cwb[4:5, lanes]
        rounded = (total / (1.0 + jnp.exp(-total))).astype(BF16)
        xcb[:, lanes] = rounded
        xc[:, lanes] = rounded.astype(F32)
        return carry

    lax.fori_loop(0, TILES, convolve, 0)

    pp[...] = jnp.dot(xcb[...], xp[...], preferred_element_type=F32)
    for k in range(1, NTP):
        copy_to("tp", wrap(p + k, NTP), pp, pr.at[k - 1], tp_send.at[k], tp_recv.at[k]).start()
    for k in range(1, NTP):
        copy_to("tp", wrap(p + k, NTP), pp, pr.at[k - 1], tp_send.at[k], tp_recv.at[k]).wait()
    pp[...] = (pp[...] + pr[0]) + (pr[1] + pr[2])

    def spread(t, carry):
        rows = pp[pl.ds(pl.multiple_of(t * R, R), R), :]
        for s in range(S):
            bb[t * S + s] = jnp.broadcast_to(rows[:, s : s + 1], (R, 128))
            cb[t * S + s] = jnp.broadcast_to(rows[:, S + s : S + s + 1], (R, 128))
        return carry

    lax.fori_loop(0, T, spread, 0)

    def scan_tile(k, carry):
        j = wrap(c + k, NCTX)
        lanes = tile_lanes(j)
        rate = [jnp.broadcast_to(a2[s : s + 1, lanes], (R, 128)) for s in range(S)]
        gain = jnp.broadcast_to(cwb[5:6, lanes], (R, 128))

        def step(t, carry):
            elapsed, state = carry[0], carry[1:]
            rows = pl.ds(pl.multiple_of(t * R, R), R)
            d, x = dts[rows, lanes], xc[rows, lanes]
            u = d * x
            parts = [gain * x, None]
            new = []
            for s in range(S):
                decay = jnp.exp2(d * rate[s])
                av[j * (T * S) + t * S + s] = decay
                h = decay * state[s] + u * bb[t * S + s]
                new.append(h)
                y = cb[t * S + s] * h
                parts[s % 2] = y if parts[s % 2] is None else parts[s % 2] + y
            yl[rows, lanes] = parts[0] + parts[1]
            return (elapsed + d, *new)

        zero = jnp.zeros((R, 128), F32)
        last = lax.fori_loop(0, T, step, (zero,) * (S + 1))
        high = last[0].astype(BF16).astype(F32)
        packed = jnp.concatenate([*last[1:], high, last[0] - high], axis=0).astype(BF16)
        st_s[j] = packed

        @pl.when(k > 0)
        def _():
            ctx_copy(ST, k, st_s.at[j], st_r.at[c]).start()

        @pl.when(k == 0)
        def _():
            st_r[c] = packed

        return carry

    lax.fori_loop(0, NCTX, scan_tile, 0)

    ctx_wait_recv(KV, kvr)
    ctx_wait_recv(Q, qr)
    own_len = meta[R]
    factor = HD**-0.5 * LOG2E

    def attend(k, carry):
        b = wrap(c // 2 + k, NCTX // 2)
        q = qr[pl.ds(2 * b, 2)].reshape(2 * T * R, HD)
        keys = kvr[:, 0:64, :].reshape(NCTX * 64, HD)
        values = kvr[:, 64:128, :].reshape(NCTX * 64, HD)
        scores = lax.dot_general(
            q, keys, (((1,), (1,)), ((), ())), preferred_element_type=F32
        )
        row = lax.broadcasted_iota(jnp.int32, (2 * T * R, 1), 0)
        when = b * (2 * T) + row // R
        scores = jnp.where(when >= thr[...], scores, -1e30)
        top = jnp.max(scores, axis=1, keepdims=True)
        weight = jnp.exp2((scores - top) * factor)
        total = jnp.sum(weight, axis=1, keepdims=True)
        out = jnp.dot(weight.astype(BF16), values, preferred_element_type=F32) / total
        out = jnp.where(when < own_len, out, 0.0).astype(BF16)
        for half in range(2):
            peer = 2 * b + half
            part = out[half * T * R : (half + 1) * T * R]
            ao_s[peer] = part

            @pl.when(peer != c)
            def _():
                ctx_copy(
                    AO, wrap(peer - c, NCTX), ao_s.at[peer], ao_r.at[c]
                ).start()

            @pl.when(peer == c)
            def _():
                ao_r[c] = part

        return carry

    lax.fori_loop(0, NCTX // 2, attend, 0)

    ctx_wait_recv(ST, st_r)

    def advance(b, state):
        pf_s[b] = state.astype(BF16)
        item = st_r[b].astype(F32)
        elapsed = item[S * R : S * R + R] + item[S * R + R :]
        return jnp.exp2(a2o[...] * jnp.concatenate([elapsed] * S, axis=0)) * state + item[: S * R]

    lax.fori_loop(0, NCTX, advance, s0[...])

    def send_prefix(k, carry):
        peer = wrap(c + k, NCTX)
        ctx_copy(PF, k, pf_s.at[peer], pf_r.at[c]).start()
        return carry

    lax.fori_loop(1, NCTX, send_prefix, 0)
    pf_r[c] = pf_s[c]

    ctx_wait_recv(AO, ao_r)

    def req_copy(kind, k, src, dst):
        return copy_to(
            "req", wrap(g + k, NREQ), src, dst, req_send.at[kind, k], req_recv.at[kind, k]
        )

    def join_heads(i, carry):
        heads = [
            ao_r[2 * i + half].astype(F32).reshape(T, R, HD) for half in range(2)
        ]
        o_all[i] = jnp.concatenate(heads, axis=1).reshape(2 * T * R, HD).astype(BF16)
        return carry

    lax.fori_loop(0, R, join_heads, 0)

    def give_attention(k, carry):
        taker = wrap(g + k, NREQ)
        i = meta[taker]
        both = o_all[i]

        @pl.when(k > 0)
        def _():
            o_s[taker] = both
            req_copy(0, k, o_s.at[taker], att.at[g]).start()

        @pl.when(k == 0)
        def _():
            att[g] = both

        return carry

    lax.fori_loop(0, NREQ, give_attention, 0)

    def finish_tile(k, carry):
        j = wrap(c - k, NCTX)
        lanes = tile_lanes(j)

        @pl.when(k > 0)
        def _():
            ctx_copy(PF, k, pf_r.at[j], pf_r.at[j]).wait_recv()

        start = pf_r[j].astype(F32)
        limit = nlr[...]

        def step(t, state):
            rows = pl.ds(pl.multiple_of(t * R, R), R)
            parts = [yl[rows, lanes], None]
            new = []
            for s in range(S):
                h = av[j * (T * S) + t * S + s] * state[s]
                new.append(h)
                y = cb[t * S + s] * h
                parts[s % 2] = y if parts[s % 2] is None else parts[s % 2] + y
            y = jnp.where(c * T + t < limit, parts[0] + parts[1], 0.0)
            yr[j, pl.ds(t, R, stride=T), :] = y
            return tuple(new)

        lax.fori_loop(0, T, step, tuple(start[s * R : s * R + R] for s in range(S)))
        return carry

    lax.fori_loop(0, NCTX, finish_tile, 0)

    def join_tiles(i, carry):
        rows = yr[:, pl.ds(pl.multiple_of(i * T, T), T), :]
        y_all[i] = jnp.concatenate([rows[j] for j in range(TILES)], axis=1).astype(BF16)
        return carry

    lax.fori_loop(0, R, join_tiles, 0)

    def give_mixed(k, carry):
        taker = wrap(g + k, NREQ)
        i = meta[taker]
        rows = y_all[i]

        @pl.when(k > 0)
        def _():
            y_s[taker] = rows
            req_copy(1, k, y_s.at[taker], mix.at[g]).start()

        @pl.when(k == 0)
        def _():
            mix[g] = rows

        return carry

    lax.fori_loop(0, NREQ, give_mixed, 0)

    rim.wait_send()
    for kind, src in ((Q, qs), (KV, kvs), (ST, st_s), (AO, ao_s), (PF, pf_s)):
        ctx_wait_send(kind, src)

    def last(k, carry):
        taker, giver = wrap(g + k, NREQ), wrap(g - k, NREQ)
        req_copy(0, k, o_s.at[taker], att.at[giver]).wait()
        req_copy(1, k, y_s.at[taker], mix.at[giver]).wait()
        return carry

    lax.fori_loop(1, NREQ, last, 0)


def per_device(
    queries,
    kv_pool,
    new_kv,
    block_table,
    cached_len,
    new_len,
    mamba_x,
    conv_state,
    conv_weight,
    conv_bias,
    x_proj,
    dt_raw,
    a_log,
    skip_gain,
    ssm_state,
    target_group,
):
    c = lax.axis_index("ctx")
    qs = queries.reshape(R, T, 2, 8, HD).transpose(0, 2, 1, 3, 4).reshape(NCTX, T * 8, HD)
    cached = jnp.take(kv_pool[:, 0], block_table[0, 0], axis=1)
    cached = cached.reshape(2, R, SPAN, 2, HD).transpose(1, 3, 0, 2, 4)
    fresh = new_kv.transpose(1, 3, 0, 2, 4)
    kvs = jnp.concatenate([cached, fresh], axis=3).reshape(NCTX, 128, HD)
    x3 = mamba_x.transpose(1, 0, 2)
    xt = x3.reshape(T * R, C)
    rs = x3[T - 3 :].reshape(3, R, 2, C // 2).transpose(0, 2, 1, 3).reshape(3, 2 * R, C // 2)
    dtt = dt_raw.transpose(1, 0, 2).reshape(T * R, C)
    cs = conv_state.transpose(1, 0, 2).reshape(3 * R, C).astype(F32)
    cwb = jnp.concatenate(
        [conv_weight, conv_bias[None], skip_gain[None], jnp.zeros((2, C), F32)], axis=0
    )
    xp = jnp.pad(x_proj.T, ((0, 0), (0, 128 - 2 * S)))
    a2 = -jnp.exp(a_log) * LOG2E
    a2o = jnp.repeat(lax.dynamic_slice_in_dim(a2, c * 128, 128, 1), R, axis=0)
    s0 = lax.dynamic_slice_in_dim(ssm_state, c * 128, 128, 2)
    s0 = s0.transpose(1, 0, 2).reshape(S * R, 128).astype(F32)
    mine = c // 2
    clen, nlen = cached_len[0, mine], new_len[0, mine]
    block = jnp.arange(NCTX, dtype=jnp.int32)[:, None]
    never = jnp.int32(1 << 20)
    cpos = block * SPAN + jnp.arange(SPAN, dtype=jnp.int32)[None]
    npos = block * T + jnp.arange(T, dtype=jnp.int32)[None]
    thr = jnp.concatenate(
        [jnp.where(cpos < clen, -1, never), jnp.where(npos < nlen, npos, never)], axis=1
    ).reshape(1, NCTX * 64)
    nlr = jnp.broadcast_to(new_len[0][:, None], (R, 128))
    slots = jnp.arange(NREQ, dtype=jnp.int32)
    order = jnp.sum(
        jnp.where(target_group[0][None, :] == slots[:, None], slots[None, :], 0), axis=1
    )
    meta = jnp.concatenate([order, nlen[None]]).astype(jnp.int32)

    vmem = pl.BlockSpec(memory_space=pltpu.VMEM)
    smem = pl.BlockSpec(memory_space=pltpu.SMEM)
    dma = pltpu.SemaphoreType.DMA
    att, mix = pl.pallas_call(
        kernel,
        out_shape=(
            jax.ShapeDtypeStruct((NREQ, 2 * T * 8, HD), BF16),
            jax.ShapeDtypeStruct((NREQ, T, C), BF16),
        ),
        in_specs=[vmem] * 13 + [smem],
        out_specs=(vmem, vmem),
        scratch_shapes=[
            pltpu.VMEM((NCTX, 128, HD), BF16),
            pltpu.VMEM((NCTX, 128, HD), BF16),
            pltpu.VMEM((3, 2 * R, C // 2), BF16),
            pltpu.VMEM((3 * R, C), F32),
            pltpu.VMEM((T * R, C), F32),
            pltpu.VMEM((T * R, C), BF16),
            pltpu.VMEM((T * R, C), F32),
            pltpu.VMEM((T * R, 128), F32),
            pltpu.VMEM((NTP - 1, T * R, 128), F32),
            pltpu.VMEM((T * S, R, 128), F32),
            pltpu.VMEM((T * S, R, 128), F32),
            pltpu.VMEM((TILES * T * S, R, 128), F32),
            pltpu.VMEM((T * R, C), F32),
            pltpu.VMEM((TILES, T * R, 128), F32),
            pltpu.VMEM((NCTX, S * R + 2 * R, 128), BF16),
            pltpu.VMEM((NCTX, S * R + 2 * R, 128), BF16),
            pltpu.VMEM((NCTX, S * R, 128), BF16),
            pltpu.VMEM((NCTX, S * R, 128), BF16),
            pltpu.VMEM((NCTX, 128, HD), BF16),
            pltpu.VMEM((NCTX, 128, HD), BF16),
            pltpu.VMEM((NREQ, T, C), BF16),
            pltpu.VMEM((NREQ, 2 * T * 8, HD), BF16),
            pltpu.VMEM((R, T, C), BF16),
            pltpu.VMEM((R, 2 * T * 8, HD), BF16),
            dma((5, NCTX)),
            dma((5, NCTX)),
            dma,
            dma,
            dma((NTP,)),
            dma((NTP,)),
            dma((2, NREQ)),
            dma((2, NREQ)),
        ],
        compiler_params=pltpu.CompilerParams(
            collective_id=0, has_side_effects=True, vmem_limit_bytes=56 << 20
        ),
    )(qs, kvs, rs, xt, dtt, cwb, cs, xp, a2, a2o, s0, thr, nlr, meta)
    return att.reshape(NREQ, T, 16, HD), mix


def solution(mesh):
    in_specs = (
        P("req", "ctx", "tp", None),
        P(None, "req", "ctx", None, "tp", None),
        P(None, "req", "ctx", "tp", None),
        P("req", "ctx", None),
        P("req", None),
        P("req", None),
        P("req", "ctx", "tp"),
        P("req", None, "tp"),
        P(None, "tp"),
        P("tp"),
        P(None, "tp"),
        P("req", "ctx", "tp"),
        P(None, "tp"),
        P("tp"),
        P("req", None, "tp"),
        P("req", None),
    )
    out_specs = (P("req", "ctx", "tp", None), P("req", "ctx", "tp"))
    return jax.shard_map(
        per_device, mesh=mesh, in_specs=in_specs, out_specs=out_specs, check_vma=False
    )
```

```python
import math

import jax
import jax.numpy as jnp
from jax import lax
from jax.experimental import pallas as pl
from jax.experimental.pallas import tpu as pltpu
from jax.sharding import PartitionSpec as P

MESH = pl.DeviceIdType.MESH
F32 = jnp.float32
BF16 = jnp.bfloat16
LOG2E = math.log2(math.e)
NREQ, NCTX, NTP = 8, 16, 4
R, T, C, S = 8, 16, 2048, 16
HD = 128
PAGE, PAGES_REQ = 8, 6
SPAN = PAGE * PAGES_REQ
TILES = C // 128
QU, KV, ST, PF = range(4)


def wrap(a, n):
    return lax.rem(a + n, n)


def tile_lanes(j):
    return pl.ds(pl.multiple_of(j * 128, 128), 128)


def copy_to(axis, peer, src, dst, send_sem, recv_sem):
    return pltpu.make_async_remote_copy(
        src_ref=src,
        dst_ref=dst,
        send_sem=send_sem,
        recv_sem=recv_sem,
        device_id={axis: peer},
        device_id_type=MESH,
    )


def ctx_step(c, k, sign):
    dx, m = k // 4, lax.rem(k, 4)
    dz = lax.rem(2 * m, 4) + m // 2
    x, z = c // 4, lax.rem(c, 4)
    return wrap(x + sign * dx, 4) * 4 + wrap(z + sign * dz, 4)


def kernel(
    q_ref, pool, fresh, x_ref, dt_ref, taps_ref, bias, gains, a_log, old_x, xp, ssm,
    table, clens, nlens, target,
    att, mix,
    xf, df, q_s, q_r, kv_s, kv_r, rs, rr, rf, a2, xc, xcb, dts, pp, pr, pj,
    bb, cb, av, yl, yr, s0,
    st_s, st_r, pf_s, pf_r, ao_s, ao_r, y_s, y_all, order,
    ctx_send, ctx_recv, out_send, out_recv, rim_send, rim_recv,
    tp_send, tp_recv, req_send, req_recv,
):
    g, c, p = lax.axis_index("req"), lax.axis_index("ctx"), lax.axis_index("tp")
    slot, key_head = c // 2, lax.rem(c, 2)

    barrier = pltpu.get_barrier_semaphore()
    for axis, me, n in (("ctx", c, NCTX), ("tp", p, NTP), ("req", g, NREQ)):

        def greet(k, carry, axis=axis, me=me, n=n):
            pl.semaphore_signal(
                barrier, inc=1, device_id={axis: wrap(me + k, n)}, device_id_type=MESH
            )
            return carry

        lax.fori_loop(1, n, greet, 0)

    def greet_owner(k, carry):
        pl.semaphore_signal(
            barrier,
            inc=1,
            device_id={"req": k // 2, "ctx": 2 * g + lax.rem(k, 2)},
            device_id_type=MESH,
        )
        return carry

    lax.fori_loop(0, 2 * NREQ, greet_owner, 0)
    def convert(j, carry):
        lanes = tile_lanes(j)
        xf[j] = x_ref[:, :, lanes].astype(F32).reshape(R * T, 128)
        df[j] = dt_ref[:, :, lanes].astype(F32).reshape(R * T, 128)
        return carry

    lax.fori_loop(0, TILES, convert, 0)
    for k in range(3):
        tiles = [xf[j, pl.ds(T - 3 + k, R, stride=T), :] for j in range(TILES)]
        halves = [
            jnp.concatenate(tiles[: TILES // 2], axis=1),
            jnp.concatenate(tiles[TILES // 2 :], axis=1),
        ]
        rs[k] = jnp.concatenate(halves, axis=0).astype(BF16)

    for taker in range(NREQ):
        found = jnp.int32(0)
        for i in range(1, R):
            found = jnp.where(target[i] == taker, i, found)
        order[taker] = found

    def fill(o, carry):
        i = order[o]
        parts = [[[], []], [[], []]]
        for n in range(PAGES_REQ):
            page = table[i, n]
            for head in range(2):
                both = pool[page, head].astype(F32)
                for kind in range(2):
                    parts[head][kind].append(both[kind * PAGE : kind * PAGE + PAGE])
        new = fresh[i]
        for head in range(2):
            for kind in range(2):
                at = kind * 64
                rows = jnp.concatenate(parts[head][kind], axis=0).astype(BF16)
                kv_s[2 * o + head, at : at + SPAN] = rows
                kv_s[2 * o + head, at + SPAN : at + 64] = new[head, kind]
        return carry

    lax.fori_loop(0, R, fill, 0)

    pl.semaphore_wait(barrier, NCTX + NTP + NREQ - 3 + 2 * NREQ)

    def ctx_copy(kind, k, src, dst):
        return copy_to(
            "ctx", ctx_step(c, k, 1), src, dst, ctx_send.at[kind, k], ctx_recv.at[kind, k]
        )

    def ctx_wait_recv(kind, dst):
        def one(k, carry):
            place = dst.at[ctx_step(c, k, -1)]
            ctx_copy(kind, k, place, place).wait_recv()
            return carry

        lax.fori_loop(1, NCTX, one, 0)

    def ctx_wait_send(kind, src):
        def one(k, carry):
            place = src.at[ctx_step(c, k, 1)]
            ctx_copy(kind, k, place, place).wait_send()
            return carry

        lax.fori_loop(1, NCTX, one, 0)

    rim = copy_to("ctx", wrap(c + 1, NCTX), rs, rr, rim_send, rim_recv)
    rim.start()

    def send_kv(k, carry):
        ctx_copy(KV, k, kv_s.at[ctx_step(c, k, 1)], kv_r.at[c]).start()
        return carry

    lax.fori_loop(1, NCTX, send_kv, 0)
    kv_r[c] = kv_s[c]

    def fill_queries(o, carry):
        q = q_ref[order[o]].astype(F32)
        for head in range(2):
            rows = q[:, head * 8 : head * 8 + 8].reshape(T * 8, HD)
            q_s[2 * o + head] = rows.astype(BF16)
        return carry

    lax.fori_loop(0, R, fill_queries, 0)
    a2[...] = jnp.exp(a_log[...]) * (-LOG2E)

    def soften(j, carry):
        lanes = tile_lanes(j)
        for t in range(T):
            d = df[j, pl.ds(t, R, stride=T), :]
            soft = jnp.maximum(d, 0.0) + jnp.log1p(jnp.exp(-jnp.abs(d)))
            dts[t * R : t * R + R, lanes] = soft
        return carry

    lax.fori_loop(0, TILES, soften, 0)

    rim.wait_recv()
    for k in range(3):
        got = rr[k].astype(F32)
        rows = slice(k * R, k * R + R)
        for half in range(2):
            rf[rows, half * 1024 : half * 1024 + 1024] = got[half * R : half * R + R]

    @pl.when(c == 0)
    def _():
        for k in range(3):
            rf[k * R : k * R + R, :] = old_x[k].astype(F32)

    def convolve(j, carry):
        lanes = tile_lanes(j)
        rows = [rf[k * R : k * R + R, lanes] for k in range(3)]
        rows += [xf[j, pl.ds(t, R, stride=T), :] for t in range(T)]
        taps = [jnp.broadcast_to(taps_ref[k : k + 1, lanes], (R, 128)) for k in range(4)]
        shift = jnp.broadcast_to(bias[0:1, lanes], (R, 128))
        outs = []
        for t in range(T):
            total = taps[0] * rows[t]
            for k in range(1, 4):
                total = total + taps[k] * rows[t + k]
            total = total + shift
            outs.append(total / (1.0 + jnp.exp(-total)))
        rounded = jnp.concatenate(outs, axis=0).astype(BF16)
        xcb[:, lanes] = rounded
        xc[:, lanes] = rounded.astype(F32)
        return carry

    lax.fori_loop(0, TILES, convolve, 0)

    pp[...] = lax.dot_general(
        xp[...], xcb[...], (((1,), (1,)), ((), ())), preferred_element_type=F32
    )
    for k in range(1, NTP):
        copy_to("tp", wrap(p + k, NTP), pp, pr.at[k - 1], tp_send.at[k], tp_recv.at[k]).start()
    for k in range(1, NTP):
        copy_to("tp", wrap(p + k, NTP), pp, pr.at[k - 1], tp_send.at[k], tp_recv.at[k]).wait()
    pj[...] = jnp.transpose((pp[...] + pr[0]) + (pr[1] + pr[2]), (1, 0))

    def spread(t, carry):
        rows = pj[pl.ds(pl.multiple_of(t * R, R), R), :]
        for s in range(S):
            bb[t * S + s] = jnp.broadcast_to(rows[:, s : s + 1], (R, 128))
            cb[t * S + s] = jnp.broadcast_to(rows[:, S + s : S + s + 1], (R, 128))
        return carry

    lax.fori_loop(0, T, spread, 0)

    def scan_tile(k, carry):
        j = ctx_step(c, k, 1)
        lanes = tile_lanes(j)
        rate = [jnp.broadcast_to(a2[s : s + 1, lanes], (R, 128)) for s in range(S)]
        gain = jnp.broadcast_to(gains[0:1, lanes], (R, 128))

        def step(t, carry):
            elapsed, state = carry[0], carry[1:]
            rows = pl.ds(pl.multiple_of(t * R, R), R)
            d, x = dts[rows, lanes], xc[rows, lanes]
            u = d * x
            parts = [gain * x, None]
            new = []
            for s in range(S):
                decay = jnp.exp2(d * rate[s])
                av[j * (T * S) + t * S + s] = decay
                h = decay * state[s] + u * bb[t * S + s]
                new.append(h)
                y = cb[t * S + s] * h
                parts[s % 2] = y if parts[s % 2] is None else parts[s % 2] + y
            yl[rows, lanes] = parts[0] + parts[1]
            return (elapsed + d, *new)

        zero = jnp.zeros((R, 128), F32)
        last = lax.fori_loop(0, T, step, (zero,) * (S + 1))
        high = last[0].astype(BF16).astype(F32)
        packed = jnp.concatenate([*last[1:], high, last[0] - high], axis=0).astype(BF16)
        st_s[j] = packed

        @pl.when(k > 0)
        def _():
            ctx_copy(ST, k, st_s.at[j], st_r.at[c]).start()

        @pl.when(k == 0)
        def _():
            st_r[c] = packed

        return carry

    lax.fori_loop(0, NCTX, scan_tile, 0)

    def send_queries(k, carry):
        ctx_copy(QU, k, q_s.at[ctx_step(c, k, 1)], q_r.at[c]).start()
        return carry

    lax.fori_loop(1, NCTX, send_queries, 0)
    q_r[c] = q_s[c]

    ctx_wait_recv(ST, st_r)

    lanes_c = tile_lanes(c)
    s0[...] = ssm[:, :, lanes_c].astype(F32).reshape(R * S, 128)
    rates = jnp.concatenate(
        [jnp.broadcast_to(a2[s : s + 1, lanes_c], (R, 128)) for s in range(S)], axis=0
    )
    start = jnp.concatenate([s0[pl.ds(s, R, stride=S), :] for s in range(S)], axis=0)

    def advance(b, state):
        pf_s[b] = state.astype(BF16)
        item = st_r[b].astype(F32)
        elapsed = item[S * R : S * R + R] + item[S * R + R :]
        return jnp.exp2(rates * jnp.concatenate([elapsed] * S, axis=0)) * state + item[: S * R]

    lax.fori_loop(0, NCTX, advance, start)

    def send_prefix(k, carry):
        peer = ctx_step(c, k, 1)
        ctx_copy(PF, k, pf_s.at[peer], pf_r.at[c]).start()
        return carry

    lax.fori_loop(1, NCTX, send_prefix, 0)
    pf_r[c] = pf_s[c]

    ctx_wait_recv(KV, kv_r)
    ctx_wait_recv(QU, q_r)
    own = order[slot]
    own_cached, own_len = clens[own], nlens[own]
    factor = HD**-0.5 * LOG2E
    key = lax.broadcasted_iota(jnp.int32, (1, NCTX * 64), 1)
    block, spot = key // 64, lax.rem(key, 64)
    never = jnp.int32(1 << 20)
    cached_from = jnp.where(block * SPAN + spot < own_cached, -1, never)
    fresh_at = block * T + spot - SPAN
    fresh_from = jnp.where(fresh_at < own_len, fresh_at, never)
    seen_from = jnp.where(spot < SPAN, cached_from, fresh_from)

    def out_copy(peer, src):
        return pltpu.make_async_remote_copy(
            src_ref=src,
            dst_ref=ao_r.at[2 * g + key_head],
            send_sem=out_send.at[peer],
            recv_sem=out_recv.at[2 * g + key_head],
            device_id={"req": slot, "ctx": peer},
            device_id_type=MESH,
        )

    def is_me(peer):
        return jnp.logical_and(slot == g, peer == c)

    def attend(k, carry):
        b = wrap(slot + k, NCTX // 2)
        q = q_r[pl.ds(2 * b, 2)].reshape(2 * T * 8, HD)
        keys = kv_r[:, 0:64, :].reshape(NCTX * 64, HD)
        values = kv_r[:, 64:128, :].reshape(NCTX * 64, HD)
        scores = lax.dot_general(
            q, keys, (((1,), (1,)), ((), ())), preferred_element_type=F32
        )
        row = lax.broadcasted_iota(jnp.int32, (2 * T * 8, 1), 0)
        when = b * (2 * T) + row // 8
        scores = jnp.where(when >= seen_from, scores, -1e30)
        top = jnp.max(scores, axis=1, keepdims=True)
        weight = jnp.exp2((scores - top) * factor)
        total = jnp.sum(weight, axis=1, keepdims=True)
        out = jnp.dot(weight.astype(BF16), values, preferred_element_type=F32) / total
        out = jnp.where(when < own_len, out, 0.0).astype(BF16)
        for half in range(2):
            peer = 2 * b + half
            part = out[half * T * 8 : (half + 1) * T * 8]
            ao_s[peer] = part

            @pl.when(jnp.logical_not(is_me(peer)))
            def _():
                out_copy(peer, ao_s.at[peer]).start()

            @pl.when(is_me(peer))
            def _():
                ao_r[2 * g + key_head] = part

        return carry

    lax.fori_loop(0, NCTX // 2, attend, 0)

    request = lax.broadcasted_iota(jnp.int32, (R, 128), 0)
    limits = jnp.zeros((R, 128), jnp.int32)
    for i in range(R):
        limits = jnp.where(request == i, nlens[i], limits)

    def finish_tile(k, carry):
        j = ctx_step(c, k, -1)
        lanes = tile_lanes(j)

        @pl.when(k > 0)
        def _():
            ctx_copy(PF, k, pf_r.at[j], pf_r.at[j]).wait_recv()

        begin = pf_r[j].astype(F32)

        def step(t, state):
            rows = pl.ds(pl.multiple_of(t * R, R), R)
            parts = [yl[rows, lanes], None]
            new = []
            for s in range(S):
                h = av[j * (T * S) + t * S + s] * state[s]
                new.append(h)
                y = cb[t * S + s] * h
                parts[s % 2] = y if parts[s % 2] is None else parts[s % 2] + y
            y = jnp.where(c * T + t < limits, parts[0] + parts[1], 0.0)
            yr[j, pl.ds(t, R, stride=T), :] = y
            return tuple(new)

        lax.fori_loop(0, T, step, tuple(begin[s * R : s * R + R] for s in range(S)))
        return carry

    lax.fori_loop(0, NCTX, finish_tile, 0)

    def join_tiles(i, carry):
        rows = yr[:, pl.ds(pl.multiple_of(i * T, T), T), :]
        y_all[i] = jnp.concatenate([rows[j] for j in range(TILES)], axis=1).astype(BF16)
        return carry

    lax.fori_loop(0, R, join_tiles, 0)

    def req_copy(k, src, dst):
        return copy_to("req", wrap(g + k, NREQ), src, dst, req_send.at[k], req_recv.at[k])

    def give_mixed(k, carry):
        taker = wrap(g + k, NREQ)
        i = order[taker]
        rows = y_all[i]

        @pl.when(k > 0)
        def _():
            y_s[taker] = rows
            req_copy(k, y_s.at[taker], mix.at[g]).start()

        @pl.when(k == 0)
        def _():
            mix[g] = rows

        return carry

    lax.fori_loop(0, NREQ, give_mixed, 0)

    def land(source, carry):
        own_part = jnp.logical_and(
            source // 2 == g, 2 * g + lax.rem(source, 2) == c
        )

        @pl.when(jnp.logical_not(own_part))
        def _():
            place = ao_r.at[source]
            pltpu.make_async_remote_copy(
                src_ref=place,
                dst_ref=place,
                send_sem=out_send.at[source],
                recv_sem=out_recv.at[source],
                device_id={"req": slot, "ctx": source},
                device_id_type=MESH,
            ).wait_recv()

        return carry

    lax.fori_loop(0, 2 * NREQ, land, 0)

    def join_heads(i, carry):
        heads = [
            ao_r[2 * i + half].astype(F32).reshape(T, 8, HD) for half in range(2)
        ]
        att[i] = jnp.concatenate(heads, axis=1).astype(BF16)
        return carry

    lax.fori_loop(0, NREQ, join_heads, 0)

    rim.wait_send()
    for kind, src in ((QU, q_s), (KV, kv_s), (ST, st_s), (PF, pf_s)):
        ctx_wait_send(kind, src)

    def sent(peer, carry):
        @pl.when(jnp.logical_not(is_me(peer)))
        def _():
            out_copy(peer, ao_s.at[peer]).wait_send()

        return carry

    lax.fori_loop(0, NCTX, sent, 0)

    def last(k, carry):
        taker, giver = wrap(g + k, NREQ), wrap(g - k, NREQ)
        req_copy(k, y_s.at[taker], mix.at[giver]).wait()
        return carry

    lax.fori_loop(1, NREQ, last, 0)


def per_device(
    queries,
    kv_pool,
    new_kv,
    block_table,
    cached_len,
    new_len,
    mamba_x,
    conv_state,
    conv_weight,
    conv_bias,
    x_proj,
    dt_raw,
    a_log,
    skip_gain,
    ssm_state,
    target_group,
):
    pool = kv_pool[:, 0].transpose(1, 3, 0, 2, 4).reshape(-1, 2, 2 * PAGE, HD)
    fresh = new_kv.transpose(1, 3, 0, 2, 4)
    vmem = pl.BlockSpec(memory_space=pltpu.VMEM)
    smem = pl.BlockSpec(memory_space=pltpu.SMEM)
    dma = pltpu.SemaphoreType.DMA
    att, mix = pl.pallas_call(
        kernel,
        out_shape=(
            jax.ShapeDtypeStruct((NREQ, T, 16, HD), BF16),
            jax.ShapeDtypeStruct((NREQ, T, C), BF16),
        ),
        in_specs=[vmem] * 12 + [smem] * 4,
        out_specs=(vmem, vmem),
        scratch_shapes=[
            pltpu.VMEM((TILES, R * T, 128), F32),
            pltpu.VMEM((TILES, R * T, 128), F32),
            pltpu.VMEM((NCTX, 128, HD), BF16),
            pltpu.VMEM((NCTX, 128, HD), BF16),
            pltpu.VMEM((NCTX, 128, HD), BF16),
            pltpu.VMEM((NCTX, 128, HD), BF16),
            pltpu.VMEM((3, 2 * R, C // 2), BF16),
            pltpu.VMEM((3, 2 * R, C // 2), BF16),
            pltpu.VMEM((3 * R, C), F32),
            pltpu.VMEM((S, C), F32),
            pltpu.VMEM((T * R, C), F32),
            pltpu.VMEM((T * R, C), BF16),
            pltpu.VMEM((T * R, C), F32),
            pltpu.VMEM((2 * S, T * R), F32),
            pltpu.VMEM((NTP - 1, 2 * S, T * R), F32),
            pltpu.VMEM((T * R, 2 * S), F32),
            pltpu.VMEM((T * S, R, 128), F32),
            pltpu.VMEM((T * S, R, 128), F32),
            pltpu.VMEM((TILES * T * S, R, 128), F32),
            pltpu.VMEM((T * R, C), F32),
            pltpu.VMEM((TILES, T * R, 128), F32),
            pltpu.VMEM((R * S, 128), F32),
            pltpu.VMEM((NCTX, S * R + 2 * R, 128), BF16),
            pltpu.VMEM((NCTX, S * R + 2 * R, 128), BF16),
            pltpu.VMEM((NCTX, S * R, 128), BF16),
            pltpu.VMEM((NCTX, S * R, 128), BF16),
            pltpu.VMEM((NCTX, 128, HD), BF16),
            pltpu.VMEM((2 * NREQ, 128, HD), BF16),
            pltpu.VMEM((NREQ, T, C), BF16),
            pltpu.VMEM((R, T, C), BF16),
            pltpu.SMEM((NREQ,), jnp.int32),
            dma((4, NCTX)),
            dma((4, NCTX)),
            dma((NCTX,)),
            dma((2 * NREQ,)),
            dma,
            dma,
            dma((NTP,)),
            dma((NTP,)),
            dma((NREQ,)),
            dma((NREQ,)),
        ],
        compiler_params=pltpu.CompilerParams(
            collective_id=0, has_side_effects=True, vmem_limit_bytes=56 << 20
        ),
    )(
        queries, pool, fresh, mamba_x, dt_raw, conv_weight, conv_bias[None], skip_gain[None],
        a_log, conv_state.transpose(1, 0, 2), x_proj, ssm_state,
        block_table.reshape(R, PAGES_REQ), cached_len[0], new_len[0], target_group[0],
    )
    return att, mix


def solution(mesh):
    in_specs = (
        P("req", "ctx", "tp", None),
        P(None, "req", "ctx", None, "tp", None),
        P(None, "req", "ctx", "tp", None),
        P("req", "ctx", None),
        P("req", None),
        P("req", None),
        P("req", "ctx", "tp"),
        P("req", None, "tp"),
        P(None, "tp"),
        P("tp"),
        P(None, "tp"),
        P("req", "ctx", "tp"),
        P(None, "tp"),
        P("tp"),
        P("req", None, "tp"),
        P("req", None),
    )
    out_specs = (P("req", "ctx", "tp", None), P("req", "ctx", "tp"))
    return jax.shard_map(
        per_device, mesh=mesh, in_specs=in_specs, out_specs=out_specs, check_vma=False
    )
```

```python
import math

import jax
import jax.numpy as jnp
from jax import lax
from jax.experimental import pallas as pl
from jax.experimental.pallas import tpu as pltpu
from jax.sharding import PartitionSpec as P

MESH = pl.DeviceIdType.MESH
F32 = jnp.float32
BF16 = jnp.bfloat16
LOG2E = math.log2(math.e)
NREQ, NCTX, NTP = 8, 16, 4
R, T, C, S = 8, 16, 2048, 16
HD = 128
PAGE, PAGES_REQ = 8, 6
SPAN = PAGE * PAGES_REQ
TILES = C // 128
QU, KV, ST, PF = range(4)
EARLY_KV, EARLY_Q = 6, 5


def wrap(a, n):
    return lax.rem(a + n, n)


def tile_lanes(j):
    return pl.ds(pl.multiple_of(j * 128, 128), 128)


def copy_to(axis, peer, src, dst, send_sem, recv_sem):
    return pltpu.make_async_remote_copy(
        src_ref=src,
        dst_ref=dst,
        send_sem=send_sem,
        recv_sem=recv_sem,
        device_id={axis: peer},
        device_id_type=MESH,
    )


def ctx_step(c, k, sign):
    dx, m = k // 4, lax.rem(k, 4)
    dz = lax.rem(2 * m, 4) + m // 2
    x, z = c // 4, lax.rem(c, 4)
    return wrap(x + sign * dx, 4) * 4 + wrap(z + sign * dz, 4)


def ctx_back(c, source):
    dx = wrap(c // 4 - source // 4, 4)
    dz = wrap(lax.rem(c, 4) - lax.rem(source, 4), 4)
    return dx * 4 + lax.rem(2 * dz, 4) + dz // 2


def kernel(
    q_ref, pool, fresh, x_ref, dt_ref, taps_ref, bias, gains, a_log, old_x, xp, ssm,
    table, clens, nlens, target,
    att, mix,
    xf, df, q_s, q_r, kv_s, kv_r, rs, rr, rf, a2, xc, xcb, dts, pp, pr, pj,
    bb, cb, av, yl, yr, s0,
    st_s, st_r, pf_s, pf_r, ao_s, ao_r, y_s, y_all, order,
    ctx_send, ctx_recv, out_send, out_recv, rim_send, rim_recv,
    tp_send, tp_recv, req_send, req_recv,
):
    g, c, p = lax.axis_index("req"), lax.axis_index("ctx"), lax.axis_index("tp")
    slot, key_head = c // 2, lax.rem(c, 2)

    barrier = pltpu.get_barrier_semaphore()
    for axis, me, n in (("ctx", c, NCTX), ("tp", p, NTP), ("req", g, NREQ)):

        def greet(k, carry, axis=axis, me=me, n=n):
            pl.semaphore_signal(
                barrier, inc=1, device_id={axis: wrap(me + k, n)}, device_id_type=MESH
            )
            return carry

        lax.fori_loop(1, n, greet, 0)

    def greet_owner(k, carry):
        pl.semaphore_signal(
            barrier,
            inc=1,
            device_id={"req": k // 2, "ctx": 2 * g + lax.rem(k, 2)},
            device_id_type=MESH,
        )
        return carry

    lax.fori_loop(0, 2 * NREQ, greet_owner, 0)
    def convert(j, carry):
        lanes = tile_lanes(j)
        xf[j] = x_ref[:, :, lanes].astype(F32).reshape(R * T, 128)
        df[j] = dt_ref[:, :, lanes].astype(F32).reshape(R * T, 128)
        return carry

    lax.fori_loop(0, TILES, convert, 0)
    for k in range(3):
        tiles = [xf[j, pl.ds(T - 3 + k, R, stride=T), :] for j in range(TILES)]
        halves = [
            jnp.concatenate(tiles[: TILES // 2], axis=1),
            jnp.concatenate(tiles[TILES // 2 :], axis=1),
        ]
        rs[k] = jnp.concatenate(halves, axis=0).astype(BF16)

    for taker in range(NREQ):
        found = jnp.int32(0)
        for i in range(1, R):
            found = jnp.where(target[i] == taker, i, found)
        order[taker] = found

    def fill(o, carry):
        i = order[o]
        parts = [[[], []], [[], []]]
        for n in range(PAGES_REQ):
            page = table[0, 0, i * PAGES_REQ + n]
            for head in range(2):
                both = pool[page, head].astype(F32)
                for kind in range(2):
                    parts[head][kind].append(both[kind * PAGE : kind * PAGE + PAGE])
        new = fresh[i]
        for head in range(2):
            for kind in range(2):
                at = kind * 64
                rows = jnp.concatenate(parts[head][kind], axis=0).astype(BF16)
                kv_s[2 * o + head, at : at + SPAN] = rows
                kv_s[2 * o + head, at + SPAN : at + 64] = new[head, kind]
        return carry

    lax.fori_loop(0, R, fill, 0)

    pl.semaphore_wait(barrier, NCTX + NTP + NREQ - 3 + 2 * NREQ)

    def ctx_copy(kind, k, src, dst):
        return copy_to(
            "ctx", ctx_step(c, k, 1), src, dst, ctx_send.at[kind, k], ctx_recv.at[kind, k]
        )

    def ctx_wait_recv(kind, dst):
        def one(k, carry):
            place = dst.at[ctx_step(c, k, -1)]
            ctx_copy(kind, k, place, place).wait_recv()
            return carry

        lax.fori_loop(1, NCTX, one, 0)

    def ctx_wait_send(kind, src):
        def one(k, carry):
            place = src.at[ctx_step(c, k, 1)]
            ctx_copy(kind, k, place, place).wait_send()
            return carry

        lax.fori_loop(1, NCTX, one, 0)

    rim = copy_to("ctx", wrap(c + 1, NCTX), rs, rr, rim_send, rim_recv)
    rim.start()

    def send_kv(k, carry):
        ctx_copy(KV, k, kv_s.at[ctx_step(c, k, 1)], kv_r.at[c]).start()
        return carry

    lax.fori_loop(1, EARLY_KV, send_kv, 0)
    kv_r[c] = kv_s[c]

    def fill_queries(o, carry):
        q = q_ref[order[o]].astype(F32)
        for head in range(2):
            rows = q[:, head * 8 : head * 8 + 8].reshape(T * 8, HD)
            q_s[2 * o + head] = rows.astype(BF16)
        return carry

    lax.fori_loop(0, R, fill_queries, 0)
    a2[...] = jnp.exp(a_log[...]) * (-LOG2E)

    def soften(j, carry):
        lanes = tile_lanes(j)
        for t in range(T):
            d = df[j, pl.ds(t, R, stride=T), :]
            soft = jnp.maximum(d, 0.0) + jnp.log1p(jnp.exp(-jnp.abs(d)))
            dts[t * R : t * R + R, lanes] = soft
        return carry

    lax.fori_loop(0, TILES, soften, 0)

    rim.wait_recv()
    for k in range(3):
        got = rr[k].astype(F32)
        rows = slice(k * R, k * R + R)
        for half in range(2):
            rf[rows, half * 1024 : half * 1024 + 1024] = got[half * R : half * R + R]

    @pl.when(c == 0)
    def _():
        for k in range(3):
            rf[k * R : k * R + R, :] = old_x[k].astype(F32)

    def convolve(j, carry):
        lanes = tile_lanes(j)
        rows = [rf[k * R : k * R + R, lanes] for k in range(3)]
        rows += [xf[j, pl.ds(t, R, stride=T), :] for t in range(T)]
        taps = [jnp.broadcast_to(taps_ref[k : k + 1, lanes], (R, 128)) for k in range(4)]
        shift = jnp.broadcast_to(bias[0:1, lanes], (R, 128))
        outs = []
        for t in range(T):
            total = taps[0] * rows[t]
            for k in range(1, 4):
                total = total + taps[k] * rows[t + k]
            total = total + shift
            outs.append(total / (1.0 + jnp.exp(-total)))
        rounded = jnp.concatenate(outs, axis=0).astype(BF16)
        xcb[:, lanes] = rounded
        xc[:, lanes] = rounded.astype(F32)
        return carry

    lax.fori_loop(0, TILES, convolve, 0)

    pp[...] = lax.dot_general(
        xp[...], xcb[...], (((1,), (1,)), ((), ())), preferred_element_type=F32
    )
    for k in range(1, NTP):
        copy_to("tp", wrap(p + k, NTP), pp, pr.at[k - 1], tp_send.at[k], tp_recv.at[k]).start()
    lax.fori_loop(EARLY_KV, NCTX, send_kv, 0)
    for k in range(1, NTP):
        copy_to("tp", wrap(p + k, NTP), pp, pr.at[k - 1], tp_send.at[k], tp_recv.at[k]).wait()
    pj[...] = jnp.transpose((pp[...] + pr[0]) + (pr[1] + pr[2]), (1, 0))

    def spread(t, carry):
        rows = pj[pl.ds(pl.multiple_of(t * R, R), R), :]
        for s in range(S):
            bb[t * S + s] = jnp.broadcast_to(rows[:, s : s + 1], (R, 128))
            cb[t * S + s] = jnp.broadcast_to(rows[:, S + s : S + s + 1], (R, 128))
        return carry

    lax.fori_loop(0, T, spread, 0)

    def scan_tile(k, carry):
        j = ctx_step(c, k, 1)
        lanes = tile_lanes(j)
        rate = [jnp.broadcast_to(a2[s : s + 1, lanes], (R, 128)) for s in range(S)]
        gain = jnp.broadcast_to(gains[0:1, lanes], (R, 128))

        def step(t, carry):
            elapsed, state = carry[0], carry[1:]
            rows = pl.ds(pl.multiple_of(t * R, R), R)
            d, x = dts[rows, lanes], xc[rows, lanes]
            u = d * x
            parts = [gain * x, None]
            new = []
            for s in range(S):
                decay = jnp.exp2(d * rate[s])
                av[j * (T * S) + t * S + s] = decay
                h = decay * state[s] + u * bb[t * S + s]
                new.append(h)
                y = cb[t * S + s] * h
                parts[s % 2] = y if parts[s % 2] is None else parts[s % 2] + y
            yl[rows, lanes] = parts[0] + parts[1]
            return (elapsed + d, *new)

        zero = jnp.zeros((R, 128), F32)
        last = lax.fori_loop(0, T, step, (zero,) * (S + 1))
        high = last[0].astype(BF16).astype(F32)
        packed = jnp.concatenate([*last[1:], high, last[0] - high], axis=0).astype(BF16)
        st_s[j] = packed

        @pl.when(k > 0)
        def _():
            ctx_copy(ST, k, st_s.at[j], st_r.at[c]).start()

        @pl.when(k == 0)
        def _():
            st_r[c] = packed

        return carry

    lax.fori_loop(0, NCTX, scan_tile, 0)

    def send_queries(k, carry):
        ctx_copy(QU, k, q_s.at[ctx_step(c, k, 1)], q_r.at[c]).start()
        return carry

    lax.fori_loop(1, EARLY_Q, send_queries, 0)
    q_r[c] = q_s[c]

    ctx_wait_recv(ST, st_r)

    lanes_c = tile_lanes(c)
    s0[...] = ssm[:, :, lanes_c].astype(F32).reshape(R * S, 128)
    rates = jnp.concatenate(
        [jnp.broadcast_to(a2[s : s + 1, lanes_c], (R, 128)) for s in range(S)], axis=0
    )
    start = jnp.concatenate([s0[pl.ds(s, R, stride=S), :] for s in range(S)], axis=0)

    def advance(b, state):
        pf_s[b] = state.astype(BF16)
        item = st_r[b].astype(F32)
        elapsed = item[S * R : S * R + R] + item[S * R + R :]
        return jnp.exp2(rates * jnp.concatenate([elapsed] * S, axis=0)) * state + item[: S * R]

    lax.fori_loop(0, NCTX, advance, start)

    def send_prefix(k, carry):
        peer = ctx_step(c, k, 1)
        ctx_copy(PF, k, pf_s.at[peer], pf_r.at[c]).start()
        return carry

    lax.fori_loop(1, NCTX, send_prefix, 0)
    pf_r[c] = pf_s[c]
    lax.fori_loop(EARLY_Q, NCTX, send_queries, 0)

    request = lax.broadcasted_iota(jnp.int32, (R, 128), 0)
    limits = jnp.zeros((R, 128), jnp.int32)
    for i in range(R):
        limits = jnp.where(request == i, nlens[i], limits)

    def finish_tile(k, carry):
        j = ctx_step(c, k, -1)
        lanes = tile_lanes(j)

        @pl.when(k > 0)
        def _():
            ctx_copy(PF, k, pf_r.at[j], pf_r.at[j]).wait_recv()

        begin = pf_r[j].astype(F32)

        def step(t, state):
            rows = pl.ds(pl.multiple_of(t * R, R), R)
            parts = [yl[rows, lanes], None]
            new = []
            for s in range(S):
                h = av[j * (T * S) + t * S + s] * state[s]
                new.append(h)
                y = cb[t * S + s] * h
                parts[s % 2] = y if parts[s % 2] is None else parts[s % 2] + y
            y = jnp.where(c * T + t < limits, parts[0] + parts[1], 0.0)
            yr[j, pl.ds(t, R, stride=T), :] = y
            return tuple(new)

        lax.fori_loop(0, T, step, tuple(begin[s * R : s * R + R] for s in range(S)))
        return carry

    lax.fori_loop(0, NCTX, finish_tile, 0)

    def join_tiles(i, carry):
        rows = yr[:, pl.ds(pl.multiple_of(i * T, T), T), :]
        y_all[i] = jnp.concatenate([rows[j] for j in range(TILES)], axis=1).astype(BF16)
        return carry

    lax.fori_loop(0, R, join_tiles, 0)

    def req_copy(k, src, dst):
        return copy_to("req", wrap(g + k, NREQ), src, dst, req_send.at[k], req_recv.at[k])

    def give_mixed(k, carry):
        taker = wrap(g + k, NREQ)
        i = order[taker]
        rows = y_all[i]

        @pl.when(k > 0)
        def _():
            y_s[taker] = rows
            req_copy(k, y_s.at[taker], mix.at[g]).start()

        @pl.when(k == 0)
        def _():
            mix[g] = rows

        return carry

    lax.fori_loop(0, NREQ, give_mixed, 0)

    ctx_wait_recv(KV, kv_r)
    own = order[slot]
    own_cached, own_len = clens[own], nlens[own]
    factor = HD**-0.5 * LOG2E
    key = lax.broadcasted_iota(jnp.int32, (1, NCTX * 64), 1)
    block, spot = key // 64, lax.rem(key, 64)
    never = jnp.int32(1 << 20)
    cached_from = jnp.where(block * SPAN + spot < own_cached, -1, never)
    fresh_at = block * T + spot - SPAN
    fresh_from = jnp.where(fresh_at < own_len, fresh_at, never)
    seen_from = jnp.where(spot < SPAN, cached_from, fresh_from)

    def out_copy(peer, src):
        return pltpu.make_async_remote_copy(
            src_ref=src,
            dst_ref=ao_r.at[2 * g + key_head],
            send_sem=out_send.at[peer],
            recv_sem=out_recv.at[2 * g + key_head],
            device_id={"req": slot, "ctx": peer},
            device_id_type=MESH,
        )

    def is_me(peer):
        return jnp.logical_and(slot == g, peer == c)

    def attend(k, carry):
        b = wrap(c // 4 - k // 2, 4) * 2 + lax.rem(k, 2)
        for half in range(2):
            source = 2 * b + half
            step = ctx_back(c, source)

            @pl.when(step > 0)
            def _():
                ctx_copy(QU, step, q_r.at[source], q_r.at[source]).wait_recv()

        q = q_r[pl.ds(2 * b, 2)].reshape(2 * T * 8, HD)
        keys = kv_r[:, 0:64, :].reshape(NCTX * 64, HD)
        values = kv_r[:, 64:128, :].reshape(NCTX * 64, HD)
        scores = lax.dot_general(
            q, keys, (((1,), (1,)), ((), ())), preferred_element_type=F32
        )
        row = lax.broadcasted_iota(jnp.int32, (2 * T * 8, 1), 0)
        when = b * (2 * T) + row // 8
        scores = jnp.where(when >= seen_from, scores, -1e30)
        top = jnp.max(scores, axis=1, keepdims=True)
        weight = jnp.exp2((scores - top) * factor)
        total = jnp.sum(weight, axis=1, keepdims=True)
        out = jnp.dot(weight.astype(BF16), values, preferred_element_type=F32) / total
        out = jnp.where(when < own_len, out, 0.0).astype(BF16)
        for half in range(2):
            peer = 2 * b + half
            part = out[half * T * 8 : (half + 1) * T * 8]
            ao_s[peer] = part

            @pl.when(jnp.logical_not(is_me(peer)))
            def _():
                out_copy(peer, ao_s.at[peer]).start()

            @pl.when(is_me(peer))
            def _():
                ao_r[2 * g + key_head] = part

        return carry

    lax.fori_loop(0, NCTX // 2, attend, 0)

    def land(source, carry):
        own_part = jnp.logical_and(
            source // 2 == g, 2 * g + lax.rem(source, 2) == c
        )

        @pl.when(jnp.logical_not(own_part))
        def _():
            place = ao_r.at[source]
            pltpu.make_async_remote_copy(
                src_ref=place,
                dst_ref=place,
                send_sem=out_send.at[source],
                recv_sem=out_recv.at[source],
                device_id={"req": slot, "ctx": source},
                device_id_type=MESH,
            ).wait_recv()

        return carry

    lax.fori_loop(0, 2 * NREQ, land, 0)

    def join_heads(i, carry):
        heads = [
            ao_r[2 * i + half].astype(F32).reshape(T, 8, HD) for half in range(2)
        ]
        att[i] = jnp.concatenate(heads, axis=1).astype(BF16)
        return carry

    lax.fori_loop(0, NREQ, join_heads, 0)

    rim.wait_send()
    for kind, src in ((QU, q_s), (KV, kv_s), (ST, st_s), (PF, pf_s)):
        ctx_wait_send(kind, src)

    def sent(peer, carry):
        @pl.when(jnp.logical_not(is_me(peer)))
        def _():
            out_copy(peer, ao_s.at[peer]).wait_send()

        return carry

    lax.fori_loop(0, NCTX, sent, 0)

    def last(k, carry):
        taker, giver = wrap(g + k, NREQ), wrap(g - k, NREQ)
        req_copy(k, y_s.at[taker], mix.at[giver]).wait()
        return carry

    lax.fori_loop(1, NREQ, last, 0)


def per_device(
    queries,
    kv_pool,
    new_kv,
    block_table,
    cached_len,
    new_len,
    mamba_x,
    conv_state,
    conv_weight,
    conv_bias,
    x_proj,
    dt_raw,
    a_log,
    skip_gain,
    ssm_state,
    target_group,
):
    pool = kv_pool[:, 0].transpose(1, 3, 0, 2, 4).reshape(-1, 2, 2 * PAGE, HD)
    fresh = new_kv.transpose(1, 3, 0, 2, 4)
    vmem = pl.BlockSpec(memory_space=pltpu.VMEM)
    smem = pl.BlockSpec(memory_space=pltpu.SMEM)
    dma = pltpu.SemaphoreType.DMA
    att, mix = pl.pallas_call(
        kernel,
        out_shape=(
            jax.ShapeDtypeStruct((NREQ, T, 16, HD), BF16),
            jax.ShapeDtypeStruct((NREQ, T, C), BF16),
        ),
        in_specs=[vmem] * 12 + [smem] * 4,
        out_specs=(vmem, vmem),
        scratch_shapes=[
            pltpu.VMEM((TILES, R * T, 128), F32),
            pltpu.VMEM((TILES, R * T, 128), F32),
            pltpu.VMEM((NCTX, 128, HD), BF16),
            pltpu.VMEM((NCTX, 128, HD), BF16),
            pltpu.VMEM((NCTX, 128, HD), BF16),
            pltpu.VMEM((NCTX, 128, HD), BF16),
            pltpu.VMEM((3, 2 * R, C // 2), BF16),
            pltpu.VMEM((3, 2 * R, C // 2), BF16),
            pltpu.VMEM((3 * R, C), F32),
            pltpu.VMEM((S, C), F32),
            pltpu.VMEM((T * R, C), F32),
            pltpu.VMEM((T * R, C), BF16),
            pltpu.VMEM((T * R, C), F32),
            pltpu.VMEM((2 * S, T * R), F32),
            pltpu.VMEM((NTP - 1, 2 * S, T * R), F32),
            pltpu.VMEM((T * R, 2 * S), F32),
            pltpu.VMEM((T * S, R, 128), F32),
            pltpu.VMEM((T * S, R, 128), F32),
            pltpu.VMEM((TILES * T * S, R, 128), F32),
            pltpu.VMEM((T * R, C), F32),
            pltpu.VMEM((TILES, T * R, 128), F32),
            pltpu.VMEM((R * S, 128), F32),
            pltpu.VMEM((NCTX, S * R + 2 * R, 128), BF16),
            pltpu.VMEM((NCTX, S * R + 2 * R, 128), BF16),
            pltpu.VMEM((NCTX, S * R, 128), BF16),
            pltpu.VMEM((NCTX, S * R, 128), BF16),
            pltpu.VMEM((NCTX, 128, HD), BF16),
            pltpu.VMEM((2 * NREQ, 128, HD), BF16),
            pltpu.VMEM((NREQ, T, C), BF16),
            pltpu.VMEM((R, T, C), BF16),
            pltpu.SMEM((NREQ,), jnp.int32),
            dma((4, NCTX)),
            dma((4, NCTX)),
            dma((NCTX,)),
            dma((2 * NREQ,)),
            dma,
            dma,
            dma((NTP,)),
            dma((NTP,)),
            dma((NREQ,)),
            dma((NREQ,)),
        ],
        compiler_params=pltpu.CompilerParams(
            collective_id=0, has_side_effects=True, vmem_limit_bytes=56 << 20
        ),
    )(
        queries, pool, fresh, mamba_x, dt_raw, conv_weight, conv_bias[None], skip_gain[None],
        a_log, conv_state.transpose(1, 0, 2), x_proj, ssm_state,
        block_table, cached_len[0], new_len[0], target_group[0],
    )
    return att, mix


def solution(mesh):
    in_specs = (
        P("req", "ctx", "tp", None),
        P(None, "req", "ctx", None, "tp", None),
        P(None, "req", "ctx", "tp", None),
        P("req", "ctx", None),
        P("req", None),
        P("req", None),
        P("req", "ctx", "tp"),
        P("req", None, "tp"),
        P(None, "tp"),
        P("tp"),
        P(None, "tp"),
        P("req", "ctx", "tp"),
        P(None, "tp"),
        P("tp"),
        P("req", None, "tp"),
        P("req", None),
    )
    out_specs = (P("req", "ctx", "tp", None), P("req", "ctx", "tp"))
    return jax.shard_map(
        per_device, mesh=mesh, in_specs=in_specs, out_specs=out_specs, check_vma=False
    )
```

```python
import math

import jax
import jax.numpy as jnp
from jax import lax
from jax.experimental import pallas as pl
from jax.experimental.pallas import tpu as pltpu
from jax.sharding import PartitionSpec as P

MESH = pl.DeviceIdType.MESH
F32 = jnp.float32
BF16 = jnp.bfloat16
LOG2E = math.log2(math.e)
NREQ, NCTX, NTP = 8, 16, 4
R, T, C, S = 8, 16, 2048, 16
HD = 128
PAGE, PAGES_REQ = 8, 6
SPAN = PAGE * PAGES_REQ
TILES = C // 128
RUNS, RUN = 4, 2 * T
PAD = RUN + 3
X, D, KV, QU = range(4)


def wrap(a, n):
    return lax.rem(a + n, n)


class Owners:
    def __init__(self, c, shift):
        self.shift = shift
        self.x = c // 4
        self.ring = wrap(lax.rem(c, 4) - shift, 4)
        self.b = self.ring // 2
        self.slot = self.x * 2 + self.ring + self.b * (3 - 2 * self.ring)
        self.rank = self.x * 2 + lax.rem(self.ring, 2)
        self.partner = self.x * 4 + lax.rem(3 - self.ring + shift, 4)

    def owner(self, slot, b=None):
        b = self.b if b is None else b
        a = lax.rem(slot, 2)
        return (slot // 2) * 4 + lax.rem(a + b * (3 - 2 * a) + self.shift, 4)

    def block(self, rank, b=None):
        b = self.b if b is None else b
        return (rank // 2) * 4 + lax.rem(2 * b + lax.rem(rank, 2) + self.shift, 4)


def remote(device, src, dst, send_sem, recv_sem):
    return pltpu.make_async_remote_copy(
        src_ref=src,
        dst_ref=dst,
        send_sem=send_sem,
        recv_sem=recv_sem,
        device_id=device,
        device_id_type=MESH,
    )


def kernel(
    q_ref, pool, fresh, x_ref, dt_ref, taps_ref, bias, gains, a_log, old_x, xp, ssm,
    table, clens, nlens, target,
    att, mix,
    x_s, x_r, d_s, d_r, q_s, q_r, kv_s, kv_r, edge, edge_s, edge_r,
    taps, a2, xf, xc, dts, pp, pr, pj, sp, av, yl, s0, st_s, st_r, y_s, o_s, order,
    in_send, in_recv, edge_send, edge_recv, pass_send, pass_recv, st_send, st_recv,
    tp_send, tp_recv, out_send, out_recv,
):
    g, c, p = lax.axis_index("req"), lax.axis_index("ctx"), lax.axis_index("tp")
    z = lax.rem(c, 4)
    mine, heads = Owners(c, 0), Owners(c, 1)

    barrier = pltpu.get_barrier_semaphore()

    def greet(device):
        pl.semaphore_signal(barrier, inc=1, device_id=device, device_id_type=MESH)

    for who in (mine, heads):

        def greet_set(k, carry, who=who):
            greet({"ctx": who.owner(lax.rem(who.slot + k, R))})
            return carry

        def greet_givers(k, carry, who=who):
            greet({"req": k, "ctx": who.owner(wrap(g - k, NREQ))})
            return carry

        lax.fori_loop(1, R, greet_set, 0)
        greet({"ctx": who.partner})
        lax.fori_loop(0, NREQ, greet_givers, 0)
    for k in range(1, NTP):
        greet({"tp": wrap(p + k, NTP)})
    for k in range(RUNS):
        greet({"ctx": k * 4 + 3 - 2 * mine.b})

    for slot in range(NREQ):
        taker = lax.rem(g + slot, NREQ)
        found = jnp.int32(0)
        for i in range(1, R):
            found = jnp.where(target[i] == taker, i, found)
        order[slot] = found

    def fill_scan(o, carry):
        i = order[o]
        rows = x_ref[i]
        x_s[o] = rows
        d_s[o] = dt_ref[i]
        ends = rows.astype(F32)
        for j in range(TILES):
            for k in range(3):
                edge[k * TILES + j : k * TILES + j + 1, :] = ends[
                    T - 3 + k : T - 2 + k, j * 128 : j * 128 + 128
                ]
        edge_s[o] = edge[...].astype(BF16)
        return carry

    lax.fori_loop(0, R, fill_scan, 0)

    def fill_attention(o, carry):
        i = order[o]
        q_s[o] = q_ref[i].reshape(2 * T * 8, HD)
        parts = [[[], []], [[], []]]
        for n in range(PAGES_REQ):
            page = table[0, 0, i * PAGES_REQ + n]
            for head in range(2):
                both = pool[page, head].astype(F32)
                for kind in range(2):
                    parts[head][kind].append(both[kind * PAGE : kind * PAGE + PAGE])
        new = fresh[i]
        for head in range(2):
            for kind in range(2):
                at = head * 128 + kind * 64
                rows = jnp.concatenate(parts[head][kind], axis=0).astype(BF16)
                kv_s[o, at : at + SPAN] = rows
                kv_s[o, at + SPAN : at + 64] = new[head, kind]
        return carry

    lax.fori_loop(0, R, fill_attention, 0)

    pl.semaphore_wait(barrier, 2 * (R - 1 + 1 + NREQ) + NTP - 1 + R * lax.rem(z, 2))

    def in_copy(kind, who, slot, src, dst):
        return remote(
            {"ctx": who.owner(slot)},
            src.at[slot],
            dst.at[who.rank],
            in_send.at[kind, slot],
            in_recv.at[kind, who.rank],
        )

    def in_wait(kind, who, rank, dst):
        @pl.when(rank != who.rank)
        def _():
            place = dst.at[rank]
            remote(
                {"ctx": who.partner}, place, place, in_send.at[kind, rank], in_recv.at[kind, rank]
            ).wait_recv()

    inputs = ((X, mine, x_s, x_r), (KV, heads, kv_s, kv_r), (D, mine, d_s, d_r), (QU, heads, q_s, q_r))

    def edge_copy(slot):
        return remote(
            {"ctx": mine.owner(slot, 1 - mine.b)},
            edge_s.at[slot],
            edge_r.at[mine.x],
            edge_send.at[slot],
            edge_recv.at[mine.x],
        )

    @pl.when(lax.rem(z, 2) == 1)
    def _():
        def send_edge(o, carry):
            edge_copy(o).start()
            return carry

        lax.fori_loop(0, R, send_edge, 0)

    for pair in (inputs[:2], inputs[2:]):

        def send_pair(k, carry, pair=pair):
            for kind, who, src, dst in pair:
                in_copy(kind, who, lax.rem(who.slot + k, R), src, dst).start()
            return carry

        lax.fori_loop(1, R, send_pair, 0)
    for kind, who, src, dst in inputs:
        dst[who.rank] = src[who.slot]

    for j in range(TILES):
        lanes = slice(j * 128, j * 128 + 128)
        for k in range(4):
            taps[k * TILES + j : k * TILES + j + 1, :] = taps_ref[k : k + 1, lanes]
        taps[4 * TILES + j : 4 * TILES + j + 1, :] = bias[0:1, lanes]
        taps[5 * TILES + j : 5 * TILES + j + 1, :] = gains[0:1, lanes]
        a2[pl.ds(j, S, stride=TILES), :] = jnp.exp(a_log[:, lanes]) * (-LOG2E)
    own = order[mine.slot]
    old_state = ssm[own].astype(F32)
    for j in range(TILES):
        s0[pl.ds(j, S, stride=TILES), :] = old_state[:, j * 128 : j * 128 + 128]

    request = lax.broadcasted_iota(jnp.int32, (R, C), 0)
    for k in range(3):
        row = jnp.sum(jnp.where(request == own, old_x[k].astype(F32), 0.0), axis=0, keepdims=True)
        for j in range(TILES):
            edge[k * TILES + j : k * TILES + j + 1, :] = row[:, j * 128 : j * 128 + 128]

    def land_edge(i, carry):
        place = edge_r.at[i]
        remote({"ctx": mine.partner}, place, place, edge_send.at[i], edge_recv.at[i]).wait_recv()
        return carry

    lax.fori_loop(0, RUNS, land_edge, 0)
    leads = mine.b == 0
    before = edge[...]
    for i in range(RUNS):
        got = edge_r[i].astype(F32)
        xf[i * PAD * TILES : (i * PAD + 3) * TILES, :] = jnp.where(leads, before, got)
        before = got

    def land_x(n, carry):
        in_wait(X, mine, n, x_r)
        rows = x_r[n].astype(F32)
        at = ((n // 2) * PAD + 3 + lax.rem(n, 2) * T) * TILES
        for j in range(TILES):
            xf[pl.ds(at + j, T, stride=TILES), :] = rows[:, j * 128 : j * 128 + 128]
        return carry

    lax.fori_loop(0, R, land_x, 0)

    def convolve(m, carry):
        at = (m * 8 + (m // 4) * 3) * TILES
        total = jnp.zeros((8, TILES, 128), F32)
        for k in range(4):
            rows = xf[pl.ds(pl.multiple_of(at + k * TILES, TILES), 8 * TILES), :]
            weight = taps[k * TILES : k * TILES + TILES, :]
            total = total + weight[None] * rows.reshape(8, TILES, 128)
        total = total + taps[4 * TILES : 5 * TILES, :][None]
        out = (total / (1.0 + jnp.exp(-total))).astype(BF16).astype(F32)
        xc[pl.ds(pl.multiple_of(m * 8 * TILES, TILES), 8 * TILES), :] = out.reshape(8 * TILES, 128)
        return carry

    lax.fori_loop(0, R * T // 8, convolve, 0)

    total = jnp.zeros((2 * S, R * T), F32)
    for j in range(TILES):
        rows = xc[pl.ds(j, R * T, stride=TILES), :].astype(BF16)
        total = total + lax.dot_general(
            xp[:, j * 128 : j * 128 + 128],
            rows,
            (((1,), (1,)), ((), ())),
            preferred_element_type=F32,
        )
    pp[...] = total

    def tp_copy(k):
        return remote(
            {"tp": wrap(p + k, NTP)}, pp, pr.at[k - 1], tp_send.at[k], tp_recv.at[k]
        )

    for k in range(1, NTP):
        tp_copy(k).start()

    def pass_copy(n):
        return remote(
            {"ctx": heads.partner},
            kv_r.at[n],
            kv_r.at[R + n],
            pass_send.at[n],
            pass_recv.at[n],
        )

    def pass_on(n, carry):
        in_wait(KV, heads, n, kv_r)
        pass_copy(n).start()
        return carry

    lax.fori_loop(0, R, pass_on, 0)

    def land_d(n, carry):
        in_wait(D, mine, n, d_r)
        rows = d_r[n].astype(F32)
        soft = jnp.maximum(rows, 0.0) + jnp.log1p(jnp.exp(-jnp.abs(rows)))
        for j in range(TILES):
            dts[pl.ds(n * T * TILES + j, T, stride=TILES), :] = soft[:, j * 128 : j * 128 + 128]
        return carry

    lax.fori_loop(0, R, land_d, 0)

    for k in range(1, NTP):
        tp_copy(k).wait()
    pj[...] = jnp.transpose((pp[...] + pr[0]) + (pr[1] + pr[2]), (1, 0))
    for s in range(2 * S):
        sp[s * R * T : (s + 1) * R * T, :] = jnp.broadcast_to(pj[:, s : s + 1], (R * T, 128))

    def position(at):
        return pl.ds(pl.multiple_of(at * TILES, TILES), TILES)

    def spread(s, at):
        return jnp.broadcast_to(sp[pl.ds(s * (R * T) + at, 1), :], (TILES, 128))

    def st_copy(i):
        return remote(
            {"ctx": mine.partner}, st_s.at[i], st_r.at[i], st_send.at[i], st_recv.at[i]
        )

    def scan_run(i, carry):
        def step(t, carry):
            elapsed, state = carry[0], carry[1:]
            at = i * RUN + t
            d, x = dts[position(at), :], xc[position(at), :]
            u = d * x
            parts = [taps[5 * TILES : 6 * TILES, :] * x, None]
            new = []
            for s in range(S):
                decay = jnp.exp2(d * a2[s * TILES : s * TILES + TILES, :])
                av[at * S + s] = decay
                h = decay * state[s] + u * spread(s, at)
                new.append(h)
                y = spread(S + s, at) * h
                parts[s % 2] = y if parts[s % 2] is None else parts[s % 2] + y
            yl[position(at), :] = parts[0] + parts[1]
            return (elapsed + d, *new)

        zero = jnp.zeros((TILES, 128), F32)
        last = lax.fori_loop(0, RUN, step, (zero,) * (S + 1))
        high = last[0].astype(BF16).astype(F32)
        st_s[i] = jnp.concatenate([*last[1:], high, last[0] - high], axis=0).astype(BF16)
        st_copy(i).start()
        return carry

    lax.fori_loop(0, RUNS, scan_run, 0)

    def out_copy(kind, who, rank, src, dst):
        return remote(
            {"req": lax.rem(g + who.slot, NREQ), "ctx": who.block(rank)},
            src.at[rank],
            dst.at[g],
            out_send.at[kind, rank],
            out_recv.at[kind, g],
        )

    def stays(who, rank):
        return jnp.logical_and(who.slot == 0, rank == who.rank)

    def give(kind, who, rank, src, dst):
        @pl.when(jnp.logical_not(stays(who, rank)))
        def _():
            out_copy(kind, who, rank, src, dst).start()

        @pl.when(stays(who, rank))
        def _():
            dst[g] = src[rank]

    own_len = nlens[own]

    def finish_run(i, carry):
        st_copy(i).wait_recv()
        own_item, other = st_s[i].astype(F32), st_r[i].astype(F32)

        def advance(item, state):
            elapsed = item[S * TILES : (S + 1) * TILES] + item[(S + 1) * TILES :]
            decay = jnp.exp2(a2[...] * jnp.concatenate([elapsed] * S, axis=0))
            return decay * state + item[: S * TILES]

        ahead = s0[...]
        middle = advance(jnp.where(leads, own_item, other), ahead)
        s0[...] = advance(jnp.where(leads, other, own_item), middle)
        begin = jnp.where(leads, ahead, middle)

        def half(h, state):
            rank = i * 2 + h
            first = mine.block(rank) * T

            def step(t, state):
                at = rank * T + t
                parts = [yl[position(at), :], None]
                new = []
                for s in range(S):
                    h = av[at * S + s] * state[s]
                    new.append(h)
                    y = spread(S + s, at) * h
                    parts[s % 2] = y if parts[s % 2] is None else parts[s % 2] + y
                live = jnp.full((TILES, 128), first + t, jnp.int32) < own_len
                yl[position(at), :] = jnp.where(live, parts[0] + parts[1], 0.0)
                return tuple(new)

            state = lax.fori_loop(0, T, step, state)
            rows = [
                yl[pl.ds(rank * T * TILES + j, T, stride=TILES), :] for j in range(TILES)
            ]
            y_s[rank] = jnp.concatenate(rows, axis=1).astype(BF16)
            give(0, mine, rank, y_s, mix)
            return state

        lax.fori_loop(
            0, 2, half, tuple(begin[s * TILES : (s + 1) * TILES] for s in range(S))
        )
        return carry

    lax.fori_loop(0, RUNS, finish_run, 0)

    def land_kv(n, carry):
        pass_copy(n).wait_recv()
        return carry

    lax.fori_loop(0, R, land_kv, 0)
    asked = order[heads.slot]
    cached_len, new_len = clens[asked], nlens[asked]
    factor = HD**-0.5 * LOG2E
    key = lax.broadcasted_iota(jnp.int32, (1, NCTX * 64), 1)
    place, spot = key // 64, lax.rem(key, 64)
    rank = lax.rem(place, R)
    side = jnp.where(place < R, heads.b, 1 - heads.b)
    block = heads.block(rank, side)
    never = jnp.int32(1 << 20)
    cached_from = jnp.where(block * SPAN + spot < cached_len, -1, never)
    fresh_at = block * T + spot - SPAN
    fresh_from = jnp.where(fresh_at < new_len, fresh_at, never)
    seen_from = jnp.where(spot < SPAN, cached_from, fresh_from)

    def attend(k, carry):
        pair = wrap(heads.x - k, 4)
        for half in range(2):
            in_wait(QU, heads, 2 * pair + half, q_r)
        q = q_r[pl.ds(2 * pair, 2)].astype(F32).reshape(2 * T, 16, HD)
        row = lax.broadcasted_iota(jnp.int32, (2 * T * 8, 1), 0) // 8
        first, second = heads.block(2 * pair), heads.block(2 * pair + 1)
        when = jnp.where(row < T, first * T + row, second * T + row - T)
        outs = []
        for head in range(2):
            rows = q[:, head * 8 : head * 8 + 8].reshape(2 * T * 8, HD).astype(BF16)
            at = head * 128
            keys = kv_r[:, at : at + 64, :].reshape(NCTX * 64, HD)
            values = kv_r[:, at + 64 : at + 128, :].reshape(NCTX * 64, HD)
            scores = lax.dot_general(
                rows, keys, (((1,), (1,)), ((), ())), preferred_element_type=F32
            )
            scores = jnp.where(when >= seen_from, scores, -1e30)
            top = jnp.max(scores, axis=1, keepdims=True)
            weight = jnp.exp2((scores - top) * factor)
            total = jnp.sum(weight, axis=1, keepdims=True)
            out = jnp.dot(weight.astype(BF16), values, preferred_element_type=F32) / total
            out = jnp.where(when < new_len, out, 0.0)
            outs.append(out.reshape(2 * T, 8, HD))
        both = jnp.concatenate(outs, axis=1).astype(BF16)
        for half in range(2):
            o_s[2 * pair + half] = both[half * T : half * T + T]
            give(1, heads, 2 * pair + half, o_s, att)
        return carry

    lax.fori_loop(0, 4, attend, 0)

    for kind, who, dst in ((0, mine, mix), (1, heads, att)):

        def land_out(giver, carry, kind=kind, who=who, dst=dst):
            own_part = jnp.logical_and(giver == g, who.slot == 0)

            @pl.when(jnp.logical_not(own_part))
            def _():
                place = dst.at[giver]
                remote(
                    {"ctx": who.partner},
                    place,
                    place,
                    out_send.at[kind, giver],
                    out_recv.at[kind, giver],
                ).wait_recv()

            return carry

        lax.fori_loop(0, NREQ, land_out, 0)

    @pl.when(lax.rem(z, 2) == 1)
    def _():
        def sent_edge(o, carry):
            edge_copy(o).wait_send()
            return carry

        lax.fori_loop(0, R, sent_edge, 0)

    for kind, who, src, dst in inputs:

        def sent_in(k, carry, kind=kind, who=who, src=src, dst=dst):
            in_copy(kind, who, lax.rem(who.slot + k, R), src, dst).wait_send()
            return carry

        lax.fori_loop(1, R, sent_in, 0)

    def sent_rest(n, carry):
        pass_copy(n).wait_send()
        for kind, who, src, dst in ((0, mine, y_s, mix), (1, heads, o_s, att)):

            @pl.when(jnp.logical_not(stays(who, n)))
            def _():
                out_copy(kind, who, n, src, dst).wait_send()

        return carry

    lax.fori_loop(0, R, sent_rest, 0)

    def sent_state(i, carry):
        st_copy(i).wait_send()
        return carry

    lax.fori_loop(0, RUNS, sent_state, 0)


def per_device(
    queries,
    kv_pool,
    new_kv,
    block_table,
    cached_len,
    new_len,
    mamba_x,
    conv_state,
    conv_weight,
    conv_bias,
    x_proj,
    dt_raw,
    a_log,
    skip_gain,
    ssm_state,
    target_group,
):
    pool = kv_pool[:, 0].transpose(1, 3, 0, 2, 4).reshape(-1, 2, 2 * PAGE, HD)
    fresh = new_kv.transpose(1, 3, 0, 2, 4)
    vmem = pl.BlockSpec(memory_space=pltpu.VMEM)
    smem = pl.BlockSpec(memory_space=pltpu.SMEM)
    dma = pltpu.SemaphoreType.DMA
    att, mix = pl.pallas_call(
        kernel,
        out_shape=(
            jax.ShapeDtypeStruct((NREQ, T, 16, HD), BF16),
            jax.ShapeDtypeStruct((NREQ, T, C), BF16),
        ),
        in_specs=[vmem] * 12 + [smem] * 4,
        out_specs=(vmem, vmem),
        scratch_shapes=[
            pltpu.VMEM((R, T, C), BF16),
            pltpu.VMEM((R, T, C), BF16),
            pltpu.VMEM((R, T, C), BF16),
            pltpu.VMEM((R, T, C), BF16),
            pltpu.VMEM((R, 256, HD), BF16),
            pltpu.VMEM((R, 256, HD), BF16),
            pltpu.VMEM((R, 256, HD), BF16),
            pltpu.VMEM((2 * R, 256, HD), BF16),
            pltpu.VMEM((3 * TILES, 128), F32),
            pltpu.VMEM((R, 3 * TILES, 128), BF16),
            pltpu.VMEM((RUNS, 3 * TILES, 128), BF16),
            pltpu.VMEM((6 * TILES, 128), F32),
            pltpu.VMEM((S * TILES, 128), F32),
            pltpu.VMEM((RUNS * PAD * TILES, 128), F32),
            pltpu.VMEM((R * T * TILES, 128), F32),
            pltpu.VMEM((R * T * TILES, 128), F32),
            pltpu.VMEM((2 * S, R * T), F32),
            pltpu.VMEM((NTP - 1, 2 * S, R * T), F32),
            pltpu.VMEM((R * T, 2 * S), F32),
            pltpu.VMEM((2 * S * R * T, 128), F32),
            pltpu.VMEM((R * T * S, TILES, 128), F32),
            pltpu.VMEM((R * T * TILES, 128), F32),
            pltpu.VMEM((S * TILES, 128), F32),
            pltpu.VMEM((RUNS, (S + 2) * TILES, 128), BF16),
            pltpu.VMEM((RUNS, (S + 2) * TILES, 128), BF16),
            pltpu.VMEM((R, T, C), BF16),
            pltpu.VMEM((R, T, 16, HD), BF16),
            pltpu.SMEM((NREQ,), jnp.int32),
            dma((4, R)),
            dma((4, R)),
            dma((R,)),
            dma((RUNS,)),
            dma((R,)),
            dma((R,)),
            dma((RUNS,)),
            dma((RUNS,)),
            dma((NTP,)),
            dma((NTP,)),
            dma((2, R)),
            dma((2, NREQ)),
        ],
        compiler_params=pltpu.CompilerParams(
            collective_id=0, has_side_effects=True, vmem_limit_bytes=56 << 20
        ),
    )(
        queries, pool, fresh, mamba_x, dt_raw, conv_weight, conv_bias[None], skip_gain[None],
        a_log, conv_state.transpose(1, 0, 2), x_proj, ssm_state,
        block_table, cached_len[0], new_len[0], target_group[0],
    )
    return att, mix


def solution(mesh):
    in_specs = (
        P("req", "ctx", "tp", None),
        P(None, "req", "ctx", None, "tp", None),
        P(None, "req", "ctx", "tp", None),
        P("req", "ctx", None),
        P("req", None),
        P("req", None),
        P("req", "ctx", "tp"),
        P("req", None, "tp"),
        P(None, "tp"),
        P("tp"),
        P(None, "tp"),
        P("req", "ctx", "tp"),
        P(None, "tp"),
        P("tp"),
        P("req", None, "tp"),
        P("req", None),
    )
    out_specs = (P("req", "ctx", "tp", None), P("req", "ctx", "tp"))
    return jax.shard_map(
        per_device, mesh=mesh, in_specs=in_specs, out_specs=out_specs, check_vma=False
    )
```

```python
import functools
import math

import jax
import jax.numpy as jnp
from jax import lax
from jax.experimental import pallas as pl
from jax.experimental.pallas import tpu as pltpu
from jax.sharding import PartitionSpec as P

MESH = pl.DeviceIdType.MESH
F32 = jnp.float32
BF16 = jnp.bfloat16
LOG2E = math.log2(math.e)
NREQ, NCTX, NTP = 8, 16, 4
R, T, C, S = 8, 16, 2048, 16
HD = 128
PAGE, PAGES_REQ = 8, 6
SPAN = PAGE * PAGES_REQ
TILES = C // 128
RUNS, RUN = 4, 2 * T
PAD = RUN + 3
X, D, KV, QU = range(4)


def wrap(a, n):
    return lax.rem(a + n, n)


class Owners:
    def __init__(self, c, shift):
        self.shift = shift
        self.x = c // 4
        self.ring = wrap(lax.rem(c, 4) - shift, 4)
        self.b = self.ring // 2
        self.slot = self.x * 2 + self.ring + self.b * (3 - 2 * self.ring)
        self.rank = self.x * 2 + lax.rem(self.ring, 2)
        self.partner = self.x * 4 + lax.rem(3 - self.ring + shift, 4)

    def owner(self, slot, b=None):
        b = self.b if b is None else b
        a = lax.rem(slot, 2)
        return (slot // 2) * 4 + lax.rem(a + b * (3 - 2 * a) + self.shift, 4)

    def block(self, rank, b=None):
        b = self.b if b is None else b
        return (rank // 2) * 4 + lax.rem(2 * b + lax.rem(rank, 2) + self.shift, 4)


def remote(device, src, dst, send_sem, recv_sem):
    return pltpu.make_async_remote_copy(
        src_ref=src,
        dst_ref=dst,
        send_sem=send_sem,
        recv_sem=recv_sem,
        device_id=device,
        device_id_type=MESH,
    )


def kernel(
    q_ref, pool, fresh, x_ref, dt_ref, taps_ref, bias, gains, a_log, old_x, xp, ssm,
    table, clens, nlens, target,
    att, mix,
    x_s, x_r, d_s, d_r, q_s, q_r, kv_s, kv_r, edge, edge_s, edge_r,
    taps, a2, xf, xc, dts, pp, pr, pj, sp, av, yl, s0, st_s, st_r, y_s, o_s, order,
    in_send, in_recv, edge_send, edge_recv, pass_send, pass_recv, st_send, st_recv,
    tp_send, tp_recv, out_send, out_recv,
):
    g, c, p = lax.axis_index("req"), lax.axis_index("ctx"), lax.axis_index("tp")
    z = lax.rem(c, 4)
    mine, heads = Owners(c, 0), Owners(c, 1)

    barrier = pltpu.get_barrier_semaphore()

    def greet(device):
        pl.semaphore_signal(barrier, inc=1, device_id=device, device_id_type=MESH)

    for who in (mine, heads):

        def greet_set(k, carry, who=who):
            greet({"ctx": who.owner(lax.rem(who.slot + k, R))})
            return carry

        def greet_givers(k, carry, who=who):
            greet({"req": k, "ctx": who.owner(wrap(g - k, NREQ))})
            return carry

        lax.fori_loop(1, R, greet_set, 0)
        greet({"ctx": who.partner})
        lax.fori_loop(0, NREQ, greet_givers, 0)
    for k in range(1, NTP):
        greet({"tp": wrap(p + k, NTP)})
    for k in range(RUNS):
        greet({"ctx": k * 4 + 3 - 2 * mine.b})

    for slot in range(NREQ):
        taker = lax.rem(g + slot, NREQ)
        found = jnp.int32(0)
        for i in range(1, R):
            found = jnp.where(target[i] == taker, i, found)
        order[slot] = found

    def fill_scan(o, carry):
        i = order[o]
        rows = x_ref[i]
        x_s[o] = rows
        d_s[o] = dt_ref[i]
        ends = rows.astype(F32)
        for j in range(TILES):
            for k in range(3):
                edge[k * TILES + j : k * TILES + j + 1, :] = ends[
                    T - 3 + k : T - 2 + k, j * 128 : j * 128 + 128
                ]
        edge_s[o] = edge[...].astype(BF16)
        return carry

    lax.fori_loop(0, R, fill_scan, 0)

    pl.semaphore_wait(barrier, 2 * (R - 1 + 1 + NREQ) + NTP - 1 + R * lax.rem(z, 2))

    def in_copy(kind, who, slot, src, dst):
        return remote(
            {"ctx": who.owner(slot)},
            src.at[slot],
            dst.at[who.rank],
            in_send.at[kind, slot],
            in_recv.at[kind, who.rank],
        )

    def in_wait(kind, who, rank, dst):
        @pl.when(rank != who.rank)
        def _():
            place = dst.at[rank]
            remote(
                {"ctx": who.partner}, place, place, in_send.at[kind, rank], in_recv.at[kind, rank]
            ).wait_recv()

    inputs = ((X, mine, x_s, x_r), (KV, heads, kv_s, kv_r), (D, mine, d_s, d_r), (QU, heads, q_s, q_r))

    def edge_copy(slot):
        return remote(
            {"ctx": mine.owner(slot, 1 - mine.b)},
            edge_s.at[slot],
            edge_r.at[mine.x],
            edge_send.at[slot],
            edge_recv.at[mine.x],
        )

    @pl.when(lax.rem(z, 2) == 1)
    def _():
        def send_edge(o, carry):
            edge_copy(o).start()
            return carry

        lax.fori_loop(0, R, send_edge, 0)

    def send_in(k, carry, which):
        for kind, who, src, dst in which:
            in_copy(kind, who, lax.rem(who.slot + k, R), src, dst).start()
        return carry

    lax.fori_loop(1, R, functools.partial(send_in, which=inputs[:1]), 0)

    def fill_attention(o, carry):
        i = order[o]
        q_s[o] = q_ref[i].reshape(2 * T * 8, HD)
        parts = [[[], []], [[], []]]
        for n in range(PAGES_REQ):
            page = table[0, 0, i * PAGES_REQ + n]
            for head in range(2):
                both = pool[page, head].astype(F32)
                for kind in range(2):
                    parts[head][kind].append(both[kind * PAGE : kind * PAGE + PAGE])
        new = fresh[i]
        for head in range(2):
            for kind in range(2):
                at = head * 128 + kind * 64
                rows = jnp.concatenate(parts[head][kind], axis=0).astype(BF16)
                kv_s[o, at : at + SPAN] = rows
                kv_s[o, at + SPAN : at + 64] = new[head, kind]
        return carry

    lax.fori_loop(0, R, fill_attention, 0)

    lax.fori_loop(1, R, functools.partial(send_in, which=inputs[1:2]), 0)
    for kind, who, src, dst in inputs:
        dst[who.rank] = src[who.slot]

    for j in range(TILES):
        lanes = slice(j * 128, j * 128 + 128)
        for k in range(4):
            taps[k * TILES + j : k * TILES + j + 1, :] = taps_ref[k : k + 1, lanes]
        taps[4 * TILES + j : 4 * TILES + j + 1, :] = bias[0:1, lanes]
        taps[5 * TILES + j : 5 * TILES + j + 1, :] = gains[0:1, lanes]
        a2[pl.ds(j, S, stride=TILES), :] = jnp.exp(a_log[:, lanes]) * (-LOG2E)
    own = order[mine.slot]
    old_state = ssm[own].astype(F32)
    for j in range(TILES):
        s0[pl.ds(j, S, stride=TILES), :] = old_state[:, j * 128 : j * 128 + 128]

    request = lax.broadcasted_iota(jnp.int32, (R, C), 0)
    for k in range(3):
        row = jnp.sum(jnp.where(request == own, old_x[k].astype(F32), 0.0), axis=0, keepdims=True)
        for j in range(TILES):
            edge[k * TILES + j : k * TILES + j + 1, :] = row[:, j * 128 : j * 128 + 128]

    def land_edge(i, carry):
        place = edge_r.at[i]
        remote({"ctx": mine.partner}, place, place, edge_send.at[i], edge_recv.at[i]).wait_recv()
        return carry

    lax.fori_loop(0, RUNS, land_edge, 0)
    leads = mine.b == 0
    before = edge[...]
    for i in range(RUNS):
        got = edge_r[i].astype(F32)
        xf[i * PAD * TILES : (i * PAD + 3) * TILES, :] = jnp.where(leads, before, got)
        before = got

    def land_x(n, carry):
        in_wait(X, mine, n, x_r)
        rows = x_r[n].astype(F32)
        at = ((n // 2) * PAD + 3 + lax.rem(n, 2) * T) * TILES
        for j in range(TILES):
            xf[pl.ds(at + j, T, stride=TILES), :] = rows[:, j * 128 : j * 128 + 128]

        @pl.when(n > 0)
        def _():
            send_in(n, 0, inputs[2:])

        return carry

    lax.fori_loop(0, R, land_x, 0)

    def convolve(m, carry):
        at = (m * 8 + (m // 4) * 3) * TILES
        total = jnp.zeros((8, TILES, 128), F32)
        for k in range(4):
            rows = xf[pl.ds(pl.multiple_of(at + k * TILES, TILES), 8 * TILES), :]
            weight = taps[k * TILES : k * TILES + TILES, :]
            total = total + weight[None] * rows.reshape(8, TILES, 128)
        total = total + taps[4 * TILES : 5 * TILES, :][None]
        out = (total / (1.0 + jnp.exp(-total))).astype(BF16).astype(F32)
        xc[pl.ds(pl.multiple_of(m * 8 * TILES, TILES), 8 * TILES), :] = out.reshape(8 * TILES, 128)
        return carry

    lax.fori_loop(0, R * T // 8, convolve, 0)

    total = jnp.zeros((2 * S, R * T), F32)
    for j in range(TILES):
        rows = xc[pl.ds(j, R * T, stride=TILES), :].astype(BF16)
        total = total + lax.dot_general(
            xp[:, j * 128 : j * 128 + 128],
            rows,
            (((1,), (1,)), ((), ())),
            preferred_element_type=F32,
        )
    pp[...] = total

    def tp_copy(k):
        return remote(
            {"tp": wrap(p + k, NTP)}, pp, pr.at[k - 1], tp_send.at[k], tp_recv.at[k]
        )

    for k in range(1, NTP):
        tp_copy(k).start()

    def pass_copy(n):
        return remote(
            {"ctx": heads.partner},
            kv_r.at[n],
            kv_r.at[R + n],
            pass_send.at[n],
            pass_recv.at[n],
        )

    def pass_on(n, carry):
        in_wait(KV, heads, n, kv_r)
        pass_copy(n).start()
        return carry

    lax.fori_loop(0, R, pass_on, 0)

    def land_d(n, carry):
        in_wait(D, mine, n, d_r)
        rows = d_r[n].astype(F32)
        soft = jnp.maximum(rows, 0.0) + jnp.log1p(jnp.exp(-jnp.abs(rows)))
        for j in range(TILES):
            dts[pl.ds(n * T * TILES + j, T, stride=TILES), :] = soft[:, j * 128 : j * 128 + 128]
        return carry

    lax.fori_loop(0, R, land_d, 0)

    for k in range(1, NTP):
        tp_copy(k).wait()
    pj[...] = jnp.transpose((pp[...] + pr[0]) + (pr[1] + pr[2]), (1, 0))
    for s in range(2 * S):
        sp[s * R * T : (s + 1) * R * T, :] = jnp.broadcast_to(pj[:, s : s + 1], (R * T, 128))

    def position(at):
        return pl.ds(pl.multiple_of(at * TILES, TILES), TILES)

    def spread(s, at):
        return jnp.broadcast_to(sp[pl.ds(s * (R * T) + at, 1), :], (TILES, 128))

    def st_copy(i):
        return remote(
            {"ctx": mine.partner}, st_s.at[i], st_r.at[i], st_send.at[i], st_recv.at[i]
        )

    def scan_run(i, carry):
        def step(t, carry):
            elapsed, state = carry[0], carry[1:]
            at = i * RUN + t
            d, x = dts[position(at), :], xc[position(at), :]
            u = d * x
            parts = [taps[5 * TILES : 6 * TILES, :] * x, None]
            new = []
            for s in range(S):
                decay = jnp.exp2(d * a2[s * TILES : s * TILES + TILES, :])
                av[at * S + s] = decay
                h = decay * state[s] + u * spread(s, at)
                new.append(h)
                y = spread(S + s, at) * h
                parts[s % 2] = y if parts[s % 2] is None else parts[s % 2] + y
            yl[position(at), :] = parts[0] + parts[1]
            return (elapsed + d, *new)

        zero = jnp.zeros((TILES, 128), F32)
        last = lax.fori_loop(0, RUN, step, (zero,) * (S + 1))
        high = last[0].astype(BF16).astype(F32)
        st_s[i] = jnp.concatenate([*last[1:], high, last[0] - high], axis=0).astype(BF16)
        st_copy(i).start()
        return carry

    lax.fori_loop(0, RUNS, scan_run, 0)

    def out_copy(kind, who, rank, src, dst):
        return remote(
            {"req": lax.rem(g + who.slot, NREQ), "ctx": who.block(rank)},
            src.at[rank],
            dst.at[g],
            out_send.at[kind, rank],
            out_recv.at[kind, g],
        )

    def stays(who, rank):
        return jnp.logical_and(who.slot == 0, rank == who.rank)

    def give(kind, who, rank, src, dst):
        @pl.when(jnp.logical_not(stays(who, rank)))
        def _():
            out_copy(kind, who, rank, src, dst).start()

        @pl.when(stays(who, rank))
        def _():
            dst[g] = src[rank]

    own_len = nlens[own]

    def finish_run(i, carry):
        st_copy(i).wait_recv()
        own_item, other = st_s[i].astype(F32), st_r[i].astype(F32)

        def advance(item, state):
            elapsed = item[S * TILES : (S + 1) * TILES] + item[(S + 1) * TILES :]
            decay = jnp.exp2(a2[...] * jnp.concatenate([elapsed] * S, axis=0))
            return decay * state + item[: S * TILES]

        ahead = s0[...]
        middle = advance(jnp.where(leads, own_item, other), ahead)
        s0[...] = advance(jnp.where(leads, other, own_item), middle)
        begin = jnp.where(leads, ahead, middle)

        def half(h, state):
            rank = i * 2 + h
            first = mine.block(rank) * T

            def step(t, state):
                at = rank * T + t
                parts = [yl[position(at), :], None]
                new = []
                for s in range(S):
                    h = av[at * S + s] * state[s]
                    new.append(h)
                    y = spread(S + s, at) * h
                    parts[s % 2] = y if parts[s % 2] is None else parts[s % 2] + y
                live = jnp.full((TILES, 128), first + t, jnp.int32) < own_len
                yl[position(at), :] = jnp.where(live, parts[0] + parts[1], 0.0)
                return tuple(new)

            state = lax.fori_loop(0, T, step, state)
            rows = [
                yl[pl.ds(rank * T * TILES + j, T, stride=TILES), :] for j in range(TILES)
            ]
            y_s[rank] = jnp.concatenate(rows, axis=1).astype(BF16)
            give(0, mine, rank, y_s, mix)
            return state

        lax.fori_loop(
            0, 2, half, tuple(begin[s * TILES : (s + 1) * TILES] for s in range(S))
        )
        return carry

    lax.fori_loop(0, RUNS, finish_run, 0)

    def land_kv(n, carry):
        pass_copy(n).wait_recv()
        return carry

    lax.fori_loop(0, R, land_kv, 0)
    asked = order[heads.slot]
    cached_len, new_len = clens[asked], nlens[asked]
    factor = HD**-0.5 * LOG2E
    key = lax.broadcasted_iota(jnp.int32, (1, NCTX * 64), 1)
    place, spot = key // 64, lax.rem(key, 64)
    rank = lax.rem(place, R)
    side = jnp.where(place < R, heads.b, 1 - heads.b)
    block = heads.block(rank, side)
    never = jnp.int32(1 << 20)
    cached_from = jnp.where(block * SPAN + spot < cached_len, -1, never)
    fresh_at = block * T + spot - SPAN
    fresh_from = jnp.where(fresh_at < new_len, fresh_at, never)
    seen_from = jnp.where(spot < SPAN, cached_from, fresh_from)

    def attend(k, carry):
        pair = wrap(heads.x - k, 4)
        for half in range(2):
            in_wait(QU, heads, 2 * pair + half, q_r)
        q = q_r[pl.ds(2 * pair, 2)].astype(F32).reshape(2 * T, 16, HD)
        row = lax.broadcasted_iota(jnp.int32, (2 * T * 8, 1), 0) // 8
        first, second = heads.block(2 * pair), heads.block(2 * pair + 1)
        when = jnp.where(row < T, first * T + row, second * T + row - T)
        outs = []
        for head in range(2):
            rows = q[:, head * 8 : head * 8 + 8].reshape(2 * T * 8, HD).astype(BF16)
            at = head * 128
            keys = kv_r[:, at : at + 64, :].reshape(NCTX * 64, HD)
            values = kv_r[:, at + 64 : at + 128, :].reshape(NCTX * 64, HD)
            scores = lax.dot_general(
                rows, keys, (((1,), (1,)), ((), ())), preferred_element_type=F32
            )
            scores = jnp.where(when >= seen_from, scores, -1e30)
            top = jnp.max(scores, axis=1, keepdims=True)
            weight = jnp.exp2((scores - top) * factor)
            total = jnp.sum(weight, axis=1, keepdims=True)
            out = jnp.dot(weight.astype(BF16), values, preferred_element_type=F32) / total
            out = jnp.where(when < new_len, out, 0.0)
            outs.append(out.reshape(2 * T, 8, HD))
        both = jnp.concatenate(outs, axis=1).astype(BF16)
        for half in range(2):
            o_s[2 * pair + half] = both[half * T : half * T + T]
            give(1, heads, 2 * pair + half, o_s, att)
        return carry

    lax.fori_loop(0, 4, attend, 0)

    for kind, who, dst in ((0, mine, mix), (1, heads, att)):

        def land_out(giver, carry, kind=kind, who=who, dst=dst):
            own_part = jnp.logical_and(giver == g, who.slot == 0)

            @pl.when(jnp.logical_not(own_part))
            def _():
                place = dst.at[giver]
                remote(
                    {"ctx": who.partner},
                    place,
                    place,
                    out_send.at[kind, giver],
                    out_recv.at[kind, giver],
                ).wait_recv()

            return carry

        lax.fori_loop(0, NREQ, land_out, 0)

    @pl.when(lax.rem(z, 2) == 1)
    def _():
        def sent_edge(o, carry):
            edge_copy(o).wait_send()
            return carry

        lax.fori_loop(0, R, sent_edge, 0)

    for kind, who, src, dst in inputs:

        def sent_in(k, carry, kind=kind, who=who, src=src, dst=dst):
            in_copy(kind, who, lax.rem(who.slot + k, R), src, dst).wait_send()
            return carry

        lax.fori_loop(1, R, sent_in, 0)

    def sent_rest(n, carry):
        pass_copy(n).wait_send()
        for kind, who, src, dst in ((0, mine, y_s, mix), (1, heads, o_s, att)):

            @pl.when(jnp.logical_not(stays(who, n)))
            def _():
                out_copy(kind, who, n, src, dst).wait_send()

        return carry

    lax.fori_loop(0, R, sent_rest, 0)

    def sent_state(i, carry):
        st_copy(i).wait_send()
        return carry

    lax.fori_loop(0, RUNS, sent_state, 0)


def per_device(
    queries,
    kv_pool,
    new_kv,
    block_table,
    cached_len,
    new_len,
    mamba_x,
    conv_state,
    conv_weight,
    conv_bias,
    x_proj,
    dt_raw,
    a_log,
    skip_gain,
    ssm_state,
    target_group,
):
    pool = kv_pool[:, 0].transpose(1, 3, 0, 2, 4).reshape(-1, 2, 2 * PAGE, HD)
    fresh = new_kv.transpose(1, 3, 0, 2, 4)
    vmem = pl.BlockSpec(memory_space=pltpu.VMEM)
    smem = pl.BlockSpec(memory_space=pltpu.SMEM)
    dma = pltpu.SemaphoreType.DMA
    att, mix = pl.pallas_call(
        kernel,
        out_shape=(
            jax.ShapeDtypeStruct((NREQ, T, 16, HD), BF16),
            jax.ShapeDtypeStruct((NREQ, T, C), BF16),
        ),
        in_specs=[vmem] * 12 + [smem] * 4,
        out_specs=(vmem, vmem),
        scratch_shapes=[
            pltpu.VMEM((R, T, C), BF16),
            pltpu.VMEM((R, T, C), BF16),
            pltpu.VMEM((R, T, C), BF16),
            pltpu.VMEM((R, T, C), BF16),
            pltpu.VMEM((R, 256, HD), BF16),
            pltpu.VMEM((R, 256, HD), BF16),
            pltpu.VMEM((R, 256, HD), BF16),
            pltpu.VMEM((2 * R, 256, HD), BF16),
            pltpu.VMEM((3 * TILES, 128), F32),
            pltpu.VMEM((R, 3 * TILES, 128), BF16),
            pltpu.VMEM((RUNS, 3 * TILES, 128), BF16),
            pltpu.VMEM((6 * TILES, 128), F32),
            pltpu.VMEM((S * TILES, 128), F32),
            pltpu.VMEM((RUNS * PAD * TILES, 128), F32),
            pltpu.VMEM((R * T * TILES, 128), F32),
            pltpu.VMEM((R * T * TILES, 128), F32),
            pltpu.VMEM((2 * S, R * T), F32),
            pltpu.VMEM((NTP - 1, 2 * S, R * T), F32),
            pltpu.VMEM((R * T, 2 * S), F32),
            pltpu.VMEM((2 * S * R * T, 128), F32),
            pltpu.VMEM((R * T * S, TILES, 128), F32),
            pltpu.VMEM((R * T * TILES, 128), F32),
            pltpu.VMEM((S * TILES, 128), F32),
            pltpu.VMEM((RUNS, (S + 2) * TILES, 128), BF16),
            pltpu.VMEM((RUNS, (S + 2) * TILES, 128), BF16),
            pltpu.VMEM((R, T, C), BF16),
            pltpu.VMEM((R, T, 16, HD), BF16),
            pltpu.SMEM((NREQ,), jnp.int32),
            dma((4, R)),
            dma((4, R)),
            dma((R,)),
            dma((RUNS,)),
            dma((R,)),
            dma((R,)),
            dma((RUNS,)),
            dma((RUNS,)),
            dma((NTP,)),
            dma((NTP,)),
            dma((2, R)),
            dma((2, NREQ)),
        ],
        compiler_params=pltpu.CompilerParams(
            collective_id=0, has_side_effects=True, vmem_limit_bytes=56 << 20
        ),
    )(
        queries, pool, fresh, mamba_x, dt_raw, conv_weight, conv_bias[None], skip_gain[None],
        a_log, conv_state.transpose(1, 0, 2), x_proj, ssm_state,
        block_table, cached_len[0], new_len[0], target_group[0],
    )
    return att, mix


def solution(mesh):
    in_specs = (
        P("req", "ctx", "tp", None),
        P(None, "req", "ctx", None, "tp", None),
        P(None, "req", "ctx", "tp", None),
        P("req", "ctx", None),
        P("req", None),
        P("req", None),
        P("req", "ctx", "tp"),
        P("req", None, "tp"),
        P(None, "tp"),
        P("tp"),
        P(None, "tp"),
        P("req", "ctx", "tp"),
        P(None, "tp"),
        P("tp"),
        P("req", None, "tp"),
        P("req", None),
    )
    out_specs = (P("req", "ctx", "tp", None), P("req", "ctx", "tp"))
    return jax.shard_map(
        per_device, mesh=mesh, in_specs=in_specs, out_specs=out_specs, check_vma=False
    )
```

```python
import functools
import math

import jax
import jax.numpy as jnp
from jax import lax
from jax.experimental import pallas as pl
from jax.experimental.pallas import tpu as pltpu
from jax.sharding import PartitionSpec as P

MESH = pl.DeviceIdType.MESH
F32 = jnp.float32
BF16 = jnp.bfloat16
LOG2E = math.log2(math.e)
NREQ, NCTX, NTP = 8, 16, 4
R, T, C, S = 8, 16, 2048, 16
HD = 128
PAGE, PAGES_REQ = 8, 6
SPAN = PAGE * PAGES_REQ
TILES = C // 128
RUNS, RUN = 4, 2 * T
PAD = T + 3
X, D, KV, QU = range(4)


def wrap(a, n):
    return lax.rem(a + n, n)


class Owners:
    def __init__(self, c, shift):
        self.shift = shift
        self.x = c // 4
        self.ring = wrap(lax.rem(c, 4) - shift, 4)
        self.b = self.ring // 2
        self.slot = self.x * 2 + self.ring + self.b * (3 - 2 * self.ring)
        second = lax.rem(self.ring, 2)
        self.rank = wrap(self.x - shift * self.b * second, 4) * 2 + second
        self.partner = self.x * 4 + lax.rem(3 - self.ring + shift, 4)

    def owner(self, slot, b=None):
        b = self.b if b is None else b
        a = lax.rem(slot, 2)
        return (slot // 2) * 4 + lax.rem(a + b * (3 - 2 * a) + self.shift, 4)

    def block(self, rank, b=None):
        b = self.b if b is None else b
        second = lax.rem(rank, 2)
        x = lax.rem(rank // 2 + self.shift * b * second, 4)
        return x * 4 + lax.rem(2 * b + second + self.shift, 4)


def remote(device, src, dst, send_sem, recv_sem):
    return pltpu.make_async_remote_copy(
        src_ref=src,
        dst_ref=dst,
        send_sem=send_sem,
        recv_sem=recv_sem,
        device_id=device,
        device_id_type=MESH,
    )


def kernel(
    q_ref, pool, fresh, x_ref, dt_ref, taps_ref, bias, gains, a_log, old_x, xp, ssm,
    table, clens, nlens, target,
    att, mix,
    x_s, x_r, d_s, d_r, q_s, q_r, kv_s, kv_r, edge, edge_s, edge_r,
    taps, a2, xf, xc, dts, pp, pr, pj, sp, av, yl, s0, s1, st_s, st_r, y_s, o_s, order,
    in_send, in_recv, edge_send, edge_recv, pass_send, pass_recv, st_send, st_recv,
    tp_send, tp_recv, out_send, out_recv,
):
    g, c, p = lax.axis_index("req"), lax.axis_index("ctx"), lax.axis_index("tp")
    shift = lax.rem(g, 2)
    mine, heads = Owners(c, shift), Owners(c, 1 - shift)
    ends_run = lax.rem(mine.ring, 2)
    leads = mine.b == shift
    split = shift * mine.b

    barrier = pltpu.get_barrier_semaphore()

    def greet(device):
        pl.semaphore_signal(barrier, inc=1, device_id=device, device_id_type=MESH)

    for kind, who in enumerate((mine, heads)):

        def greet_set(k, carry, who=who):
            greet({"ctx": who.owner(lax.rem(who.slot + k, R))})
            return carry

        def greet_givers(k, carry, kind=kind):
            giver = Owners(c, kind + (1 - 2 * kind) * lax.rem(k, 2))
            greet({"req": k, "ctx": giver.owner(wrap(g - k, NREQ))})
            return carry

        lax.fori_loop(1, R, greet_set, 0)
        greet({"ctx": who.partner})
        lax.fori_loop(0, NREQ, greet_givers, 0)
    for k in range(1, NTP):
        greet({"tp": wrap(p + k, NTP)})
    for k in range(RUNS):
        greet({"ctx": mine.block(2 * k + 1, 1 - mine.b)})

    for slot in range(NREQ):
        taker = lax.rem(g + slot, NREQ)
        found = jnp.int32(0)
        for i in range(1, R):
            found = jnp.where(target[i] == taker, i, found)
        order[slot] = found

    def fill_scan(o, carry):
        i = order[o]
        rows = x_ref[i]
        x_s[o] = rows
        d_s[o] = dt_ref[i]
        ends = rows.astype(F32)
        for j in range(TILES):
            for k in range(3):
                edge[k * TILES + j : k * TILES + j + 1, :] = ends[
                    T - 3 + k : T - 2 + k, j * 128 : j * 128 + 128
                ]
        edge_s[o] = edge[...].astype(BF16)
        return carry

    lax.fori_loop(0, R, fill_scan, 0)

    pl.semaphore_wait(barrier, 2 * (R - 1 + 1 + NREQ) + NTP - 1 + R * ends_run)

    def in_copy(kind, who, slot, src, dst):
        return remote(
            {"ctx": who.owner(slot)},
            src.at[slot],
            dst.at[who.rank],
            in_send.at[kind, slot],
            in_recv.at[kind, who.rank],
        )

    def in_wait(kind, who, rank, dst):
        @pl.when(rank != who.rank)
        def _():
            place = dst.at[rank]
            remote(
                {"ctx": who.partner}, place, place, in_send.at[kind, rank], in_recv.at[kind, rank]
            ).wait_recv()

    inputs = ((X, mine, x_s, x_r), (KV, heads, kv_s, kv_r), (D, mine, d_s, d_r), (QU, heads, q_s, q_r))

    def edge_copy(slot):
        return remote(
            {"ctx": mine.owner(slot, 1 - mine.b)},
            edge_s.at[slot],
            edge_r.at[mine.rank // 2],
            edge_send.at[slot],
            edge_recv.at[mine.rank // 2],
        )

    @pl.when(ends_run == 1)
    def _():
        def send_edge(o, carry):
            edge_copy(o).start()
            return carry

        lax.fori_loop(0, R, send_edge, 0)

    def send_in(k, carry, which):
        for kind, who, src, dst in which:
            in_copy(kind, who, lax.rem(who.slot + k, R), src, dst).start()
        return carry

    lax.fori_loop(1, R, functools.partial(send_in, which=inputs[:1]), 0)

    def fill_attention(o, carry):
        i = order[o]
        q_s[o] = q_ref[i].reshape(2 * T * 8, HD)
        parts = [[[], []], [[], []]]
        for n in range(PAGES_REQ):
            page = table[0, 0, i * PAGES_REQ + n]
            for head in range(2):
                both = pool[page, head].astype(F32)
                for kind in range(2):
                    parts[head][kind].append(both[kind * PAGE : kind * PAGE + PAGE])
        new = fresh[i]
        for head in range(2):
            for kind in range(2):
                at = head * 128 + kind * 64
                rows = jnp.concatenate(parts[head][kind], axis=0).astype(BF16)
                kv_s[o, at : at + SPAN] = rows
                kv_s[o, at + SPAN : at + 64] = new[head, kind]
        return carry

    lax.fori_loop(0, R, fill_attention, 0)

    lax.fori_loop(1, R, functools.partial(send_in, which=inputs[1:]), 0)
    for kind, who, src, dst in inputs:
        dst[who.rank] = src[who.slot]

    for j in range(TILES):
        lanes = slice(j * 128, j * 128 + 128)
        for k in range(4):
            taps[k * TILES + j : k * TILES + j + 1, :] = taps_ref[k : k + 1, lanes]
        taps[4 * TILES + j : 4 * TILES + j + 1, :] = bias[0:1, lanes]
        taps[5 * TILES + j : 5 * TILES + j + 1, :] = gains[0:1, lanes]
        a2[pl.ds(j, S, stride=TILES), :] = jnp.exp(a_log[:, lanes]) * (-LOG2E)
    own = order[mine.slot]
    old_state = ssm[own].astype(F32)
    for j in range(TILES):
        s0[pl.ds(j, S, stride=TILES), :] = old_state[:, j * 128 : j * 128 + 128]

    request = lax.broadcasted_iota(jnp.int32, (R, C), 0)
    for k in range(3):
        row = jnp.sum(jnp.where(request == own, old_x[k].astype(F32), 0.0), axis=0, keepdims=True)
        for j in range(TILES):
            edge[k * TILES + j : k * TILES + j + 1, :] = row[:, j * 128 : j * 128 + 128]

    def land_edge(i, carry):
        place = edge_r.at[i]
        remote({"ctx": mine.partner}, place, place, edge_send.at[i], edge_recv.at[i]).wait_recv()
        return carry

    lax.fori_loop(0, RUNS, land_edge, 0)
    stored = edge[...]
    for i in range(RUNS):
        late, early = edge_r[i].astype(F32), edge_r[(i + RUNS - 1) % RUNS].astype(F32)
        if i == 0:
            early = jnp.where(shift == 0, stored, early)
        at = 2 * i * PAD * TILES
        xf[at : at + 3 * TILES, :] = jnp.where(mine.b == 0, early, late)

    def land_x(n, carry):
        in_wait(X, mine, n, x_r)
        rows = x_r[n].astype(F32)
        at = (n * PAD + 3) * TILES
        for j in range(TILES):
            xf[pl.ds(at + j, T, stride=TILES), :] = rows[:, j * 128 : j * 128 + 128]
        return carry

    lax.fori_loop(0, R, land_x, 0)
    for i in range(RUNS):
        at = (2 * i + 1) * PAD * TILES
        rows = xf[at - 3 * TILES : at, :]
        if i == RUNS - 1:
            rows = jnp.where(split == 1, stored, rows)
        xf[at : at + 3 * TILES, :] = rows

    def convolve(m, carry):
        at = (m * 8 + (m // 2) * 3) * TILES
        total = jnp.zeros((8, TILES, 128), F32)
        for k in range(4):
            rows = xf[pl.ds(pl.multiple_of(at + k * TILES, TILES), 8 * TILES), :]
            weight = taps[k * TILES : k * TILES + TILES, :]
            total = total + weight[None] * rows.reshape(8, TILES, 128)
        total = total + taps[4 * TILES : 5 * TILES, :][None]
        out = (total / (1.0 + jnp.exp(-total))).astype(BF16).astype(F32)
        xc[pl.ds(pl.multiple_of(m * 8 * TILES, TILES), 8 * TILES), :] = out.reshape(8 * TILES, 128)
        return carry

    lax.fori_loop(0, R * T // 8, convolve, 0)

    total = jnp.zeros((2 * S, R * T), F32)
    for j in range(TILES):
        rows = xc[pl.ds(j, R * T, stride=TILES), :].astype(BF16)
        total = total + lax.dot_general(
            xp[:, j * 128 : j * 128 + 128],
            rows,
            (((1,), (1,)), ((), ())),
            preferred_element_type=F32,
        )
    pp[...] = total

    def tp_copy(k):
        return remote(
            {"tp": wrap(p + k, NTP)}, pp, pr.at[k - 1], tp_send.at[k], tp_recv.at[k]
        )

    for k in range(1, NTP):
        tp_copy(k).start()

    def pass_copy(n):
        return remote(
            {"ctx": heads.partner},
            kv_r.at[n],
            kv_r.at[R + n],
            pass_send.at[n],
            pass_recv.at[n],
        )

    def pass_on(n, carry):
        in_wait(KV, heads, n, kv_r)
        pass_copy(n).start()
        return carry

    lax.fori_loop(0, R, pass_on, 0)

    def land_d(n, carry):
        in_wait(D, mine, n, d_r)
        rows = d_r[n].astype(F32)
        soft = jnp.maximum(rows, 0.0) + jnp.log1p(jnp.exp(-jnp.abs(rows)))
        for j in range(TILES):
            dts[pl.ds(n * T * TILES + j, T, stride=TILES), :] = soft[:, j * 128 : j * 128 + 128]
        return carry

    lax.fori_loop(0, R, land_d, 0)

    for k in range(1, NTP):
        tp_copy(k).wait()
    pj[...] = jnp.transpose((pp[...] + pr[0]) + (pr[1] + pr[2]), (1, 0))
    for s in range(2 * S):
        sp[s * R * T : (s + 1) * R * T, :] = jnp.broadcast_to(pj[:, s : s + 1], (R * T, 128))

    def position(at):
        return pl.ds(pl.multiple_of(at * TILES, TILES), TILES)

    def spread(s, at):
        return jnp.broadcast_to(sp[pl.ds(s * (R * T) + at, 1), :], (TILES, 128))

    def st_copy(i):
        return remote(
            {"ctx": mine.partner}, st_s.at[i], st_r.at[i], st_send.at[i], st_recv.at[i]
        )

    def scan_run(i, carry):
        def step(t, carry):
            elapsed, state = carry[0], carry[1:]
            at = i * RUN + t
            d, x = dts[position(at), :], xc[position(at), :]
            u = d * x
            parts = [taps[5 * TILES : 6 * TILES, :] * x, None]
            new = []
            for s in range(S):
                decay = jnp.exp2(d * a2[s * TILES : s * TILES + TILES, :])
                av[at * S + s] = decay
                h = decay * state[s] + u * spread(s, at)
                new.append(h)
                y = spread(S + s, at) * h
                parts[s % 2] = y if parts[s % 2] is None else parts[s % 2] + y
            yl[position(at), :] = parts[0] + parts[1]
            return (elapsed + d, *new)

        zero = jnp.zeros((TILES, 128), F32)

        def half(h, carry):
            apart = jnp.logical_and(split == 1, i * 2 + h == 2 * RUNS - 1)
            carry = tuple(jnp.where(apart, 0.0, v) for v in carry)
            return lax.fori_loop(h * T, h * T + T, step, carry)

        last = lax.fori_loop(0, 2, half, (zero,) * (S + 1))
        high = last[0].astype(BF16).astype(F32)
        st_s[i] = jnp.concatenate([*last[1:], high, last[0] - high], axis=0).astype(BF16)
        st_copy(i).start()
        return carry

    lax.fori_loop(0, RUNS, scan_run, 0)

    def out_copy(kind, who, rank, src, dst):
        return remote(
            {"req": lax.rem(g + who.slot, NREQ), "ctx": who.block(rank)},
            src.at[rank],
            dst.at[g],
            out_send.at[kind, rank],
            out_recv.at[kind, g],
        )

    def stays(who, rank):
        return jnp.logical_and(who.slot == 0, rank == who.rank)

    def give(kind, who, rank, src, dst):
        @pl.when(jnp.logical_not(stays(who, rank)))
        def _():
            out_copy(kind, who, rank, src, dst).start()

        @pl.when(stays(who, rank))
        def _():
            dst[g] = src[rank]

    own_len = nlens[own]

    def land_state(i, carry):
        st_copy(i).wait_recv()
        return carry

    lax.fori_loop(0, RUNS, land_state, 0)
    s1[...] = s0[...]

    def finish_run(i, carry):
        own_item = st_s[lax.rem(i + 3 * split, RUNS)].astype(F32)
        other = st_r[lax.rem(i + 3 * shift * (1 - mine.b), RUNS)].astype(F32)

        def advance(item, state):
            elapsed = item[S * TILES : (S + 1) * TILES] + item[(S + 1) * TILES :]
            decay = jnp.exp2(a2[...] * jnp.concatenate([elapsed] * S, axis=0))
            return decay * state + item[: S * TILES]

        ahead = s0[...]
        middle = advance(jnp.where(leads, own_item, other), ahead)
        after = advance(jnp.where(leads, other, own_item), middle)
        s0[...] = after
        begin = jnp.where(split == 1, after, jnp.where(leads, ahead, middle))

        def half(h, state):
            rank = i * 2 + h
            first = mine.block(rank) * T
            apart = jnp.logical_and(split == 1, rank == 2 * RUNS - 1)
            state = tuple(
                jnp.where(apart, s1[s * TILES : (s + 1) * TILES, :], state[s]) for s in range(S)
            )

            def step(t, state):
                at = rank * T + t
                parts = [yl[position(at), :], None]
                new = []
                for s in range(S):
                    h = av[at * S + s] * state[s]
                    new.append(h)
                    y = spread(S + s, at) * h
                    parts[s % 2] = y if parts[s % 2] is None else parts[s % 2] + y
                live = jnp.full((TILES, 128), first + t, jnp.int32) < own_len
                yl[position(at), :] = jnp.where(live, parts[0] + parts[1], 0.0)
                return tuple(new)

            state = lax.fori_loop(0, T, step, state)
            rows = [
                yl[pl.ds(rank * T * TILES + j, T, stride=TILES), :] for j in range(TILES)
            ]
            y_s[rank] = jnp.concatenate(rows, axis=1).astype(BF16)
            give(0, mine, rank, y_s, mix)
            return state

        lax.fori_loop(
            0, 2, half, tuple(begin[s * TILES : (s + 1) * TILES] for s in range(S))
        )
        return carry

    lax.fori_loop(0, RUNS, finish_run, 0)

    def land_kv(n, carry):
        pass_copy(n).wait_recv()
        return carry

    lax.fori_loop(0, R, land_kv, 0)
    asked = order[heads.slot]
    cached_len, new_len = clens[asked], nlens[asked]
    factor = HD**-0.5 * LOG2E
    key = lax.broadcasted_iota(jnp.int32, (1, NCTX * 64), 1)
    place, spot = key // 64, lax.rem(key, 64)
    rank = lax.rem(place, R)
    side = jnp.where(place < R, heads.b, 1 - heads.b)
    block = heads.block(rank, side)
    never = jnp.int32(1 << 20)
    cached_from = jnp.where(block * SPAN + spot < cached_len, -1, never)
    fresh_at = block * T + spot - SPAN
    fresh_from = jnp.where(fresh_at < new_len, fresh_at, never)
    seen_from = jnp.where(spot < SPAN, cached_from, fresh_from)

    def attend(k, carry):
        pair = wrap(heads.x - k, 4)
        for half in range(2):
            in_wait(QU, heads, 2 * pair + half, q_r)
        q = q_r[pl.ds(2 * pair, 2)].astype(F32).reshape(2 * T, 16, HD)
        row = lax.broadcasted_iota(jnp.int32, (2 * T * 8, 1), 0) // 8
        first, second = heads.block(2 * pair), heads.block(2 * pair + 1)
        when = jnp.where(row < T, first * T + row, second * T + row - T)
        outs = []
        for head in range(2):
            rows = q[:, head * 8 : head * 8 + 8].reshape(2 * T * 8, HD).astype(BF16)
            at = head * 128
            keys = kv_r[:, at : at + 64, :].reshape(NCTX * 64, HD)
            values = kv_r[:, at + 64 : at + 128, :].reshape(NCTX * 64, HD)
            scores = lax.dot_general(
                rows, keys, (((1,), (1,)), ((), ())), preferred_element_type=F32
            )
            scores = jnp.where(when >= seen_from, scores, -1e30)
            top = jnp.max(scores, axis=1, keepdims=True)
            weight = jnp.exp2((scores - top) * factor)
            total = jnp.sum(weight, axis=1, keepdims=True)
            out = jnp.dot(weight.astype(BF16), values, preferred_element_type=F32) / total
            out = jnp.where(when < new_len, out, 0.0)
            outs.append(out.reshape(2 * T, 8, HD))
        both = jnp.concatenate(outs, axis=1).astype(BF16)
        for half in range(2):
            o_s[2 * pair + half] = both[half * T : half * T + T]
            give(1, heads, 2 * pair + half, o_s, att)
        return carry

    lax.fori_loop(0, 4, attend, 0)

    for kind, who, dst in ((0, mine, mix), (1, heads, att)):

        def land_out(giver, carry, kind=kind, who=who, dst=dst):
            own_part = jnp.logical_and(giver == g, who.slot == 0)

            @pl.when(jnp.logical_not(own_part))
            def _():
                place = dst.at[giver]
                remote(
                    {"ctx": who.partner},
                    place,
                    place,
                    out_send.at[kind, giver],
                    out_recv.at[kind, giver],
                ).wait_recv()

            return carry

        lax.fori_loop(0, NREQ, land_out, 0)

    @pl.when(ends_run == 1)
    def _():
        def sent_edge(o, carry):
            edge_copy(o).wait_send()
            return carry

        lax.fori_loop(0, R, sent_edge, 0)

    for kind, who, src, dst in inputs:

        def sent_in(k, carry, kind=kind, who=who, src=src, dst=dst):
            in_copy(kind, who, lax.rem(who.slot + k, R), src, dst).wait_send()
            return carry

        lax.fori_loop(1, R, sent_in, 0)

    def sent_rest(n, carry):
        pass_copy(n).wait_send()
        for kind, who, src, dst in ((0, mine, y_s, mix), (1, heads, o_s, att)):

            @pl.when(jnp.logical_not(stays(who, n)))
            def _():
                out_copy(kind, who, n, src, dst).wait_send()

        return carry

    lax.fori_loop(0, R, sent_rest, 0)

    def sent_state(i, carry):
        st_copy(i).wait_send()
        return carry

    lax.fori_loop(0, RUNS, sent_state, 0)


def per_device(
    queries,
    kv_pool,
    new_kv,
    block_table,
    cached_len,
    new_len,
    mamba_x,
    conv_state,
    conv_weight,
    conv_bias,
    x_proj,
    dt_raw,
    a_log,
    skip_gain,
    ssm_state,
    target_group,
):
    pool = kv_pool[:, 0].transpose(1, 3, 0, 2, 4).reshape(-1, 2, 2 * PAGE, HD)
    fresh = new_kv.transpose(1, 3, 0, 2, 4)
    vmem = pl.BlockSpec(memory_space=pltpu.VMEM)
    smem = pl.BlockSpec(memory_space=pltpu.SMEM)
    dma = pltpu.SemaphoreType.DMA
    att, mix = pl.pallas_call(
        kernel,
        out_shape=(
            jax.ShapeDtypeStruct((NREQ, T, 16, HD), BF16),
            jax.ShapeDtypeStruct((NREQ, T, C), BF16),
        ),
        in_specs=[vmem] * 12 + [smem] * 4,
        out_specs=(vmem, vmem),
        scratch_shapes=[
            pltpu.VMEM((R, T, C), BF16),
            pltpu.VMEM((R, T, C), BF16),
            pltpu.VMEM((R, T, C), BF16),
            pltpu.VMEM((R, T, C), BF16),
            pltpu.VMEM((R, 256, HD), BF16),
            pltpu.VMEM((R, 256, HD), BF16),
            pltpu.VMEM((R, 256, HD), BF16),
            pltpu.VMEM((2 * R, 256, HD), BF16),
            pltpu.VMEM((3 * TILES, 128), F32),
            pltpu.VMEM((R, 3 * TILES, 128), BF16),
            pltpu.VMEM((RUNS, 3 * TILES, 128), BF16),
            pltpu.VMEM((6 * TILES, 128), F32),
            pltpu.VMEM((S * TILES, 128), F32),
            pltpu.VMEM((R * PAD * TILES, 128), F32),
            pltpu.VMEM((R * T * TILES, 128), F32),
            pltpu.VMEM((R * T * TILES, 128), F32),
            pltpu.VMEM((2 * S, R * T), F32),
            pltpu.VMEM((NTP - 1, 2 * S, R * T), F32),
            pltpu.VMEM((R * T, 2 * S), F32),
            pltpu.VMEM((2 * S * R * T, 128), F32),
            pltpu.VMEM((R * T * S, TILES, 128), F32),
            pltpu.VMEM((R * T * TILES, 128), F32),
            pltpu.VMEM((S * TILES, 128), F32),
            pltpu.VMEM((S * TILES, 128), F32),
            pltpu.VMEM((RUNS, (S + 2) * TILES, 128), BF16),
            pltpu.VMEM((RUNS, (S + 2) * TILES, 128), BF16),
            pltpu.VMEM((R, T, C), BF16),
            pltpu.VMEM((R, T, 16, HD), BF16),
            pltpu.SMEM((NREQ,), jnp.int32),
            dma((4, R)),
            dma((4, R)),
            dma((R,)),
            dma((RUNS,)),
            dma((R,)),
            dma((R,)),
            dma((RUNS,)),
            dma((RUNS,)),
            dma((NTP,)),
            dma((NTP,)),
            dma((2, R)),
            dma((2, NREQ)),
        ],
        compiler_params=pltpu.CompilerParams(
            collective_id=0, has_side_effects=True, vmem_limit_bytes=56 << 20
        ),
    )(
        queries, pool, fresh, mamba_x, dt_raw, conv_weight, conv_bias[None], skip_gain[None],
        a_log, conv_state.transpose(1, 0, 2), x_proj, ssm_state,
        block_table, cached_len[0], new_len[0], target_group[0],
    )
    return att, mix


def solution(mesh):
    in_specs = (
        P("req", "ctx", "tp", None),
        P(None, "req", "ctx", None, "tp", None),
        P(None, "req", "ctx", "tp", None),
        P("req", "ctx", None),
        P("req", None),
        P("req", None),
        P("req", "ctx", "tp"),
        P("req", None, "tp"),
        P(None, "tp"),
        P("tp"),
        P(None, "tp"),
        P("req", "ctx", "tp"),
        P(None, "tp"),
        P("tp"),
        P("req", None, "tp"),
        P("req", None),
    )
    out_specs = (P("req", "ctx", "tp", None), P("req", "ctx", "tp"))
    return jax.shard_map(
        per_device, mesh=mesh, in_specs=in_specs, out_specs=out_specs, check_vma=False
    )
```

```python
import functools
import math

import jax
import jax.numpy as jnp
from jax import lax
from jax.experimental import pallas as pl
from jax.experimental.pallas import tpu as pltpu
from jax.sharding import PartitionSpec as P

MESH = pl.DeviceIdType.MESH
F32 = jnp.float32
BF16 = jnp.bfloat16
LOG2E = math.log2(math.e)
NREQ, NCTX, NTP = 8, 16, 4
R, T, C, S = 8, 16, 2048, 16
HD = 128
PAGE, PAGES_REQ = 8, 6
SPAN = PAGE * PAGES_REQ
TILES = C // 128
RUNS, RUN = 4, 2 * T
PAD = T + 3
X, D, KV, QU = range(4)


def wrap(a, n):
    return lax.rem(a + n, n)


class Owners:
    def __init__(self, c, shift):
        self.shift = shift
        self.x = c // 4
        self.ring = wrap(lax.rem(c, 4) - shift, 4)
        self.b = self.ring // 2
        self.slot = self.x * 2 + self.ring + self.b * (3 - 2 * self.ring)
        second = lax.rem(self.ring, 2)
        self.rank = wrap(self.x - shift * self.b * second, 4) * 2 + second
        self.partner = self.x * 4 + lax.rem(3 - self.ring + shift, 4)

    def owner(self, slot, b=None):
        b = self.b if b is None else b
        a = lax.rem(slot, 2)
        return (slot // 2) * 4 + lax.rem(a + b * (3 - 2 * a) + self.shift, 4)

    def block(self, rank, b=None):
        b = self.b if b is None else b
        second = lax.rem(rank, 2)
        x = lax.rem(rank // 2 + self.shift * b * second, 4)
        return x * 4 + lax.rem(2 * b + second + self.shift, 4)


def remote(device, src, dst, send_sem, recv_sem):
    return pltpu.make_async_remote_copy(
        src_ref=src,
        dst_ref=dst,
        send_sem=send_sem,
        recv_sem=recv_sem,
        device_id=device,
        device_id_type=MESH,
    )


def kernel(
    q_ref, pool, fresh, x_ref, dt_ref, taps_ref, bias, gains, a_log, old_x, xp, ssm,
    table, clens, nlens, target,
    att, mix,
    x_s, x_r, d_s, d_r, q_s, q_r, kv_s, kv_r, edge, edge_s, edge_r,
    taps, a2, xf, xc, dts, pp, pr, pj, sp, av, yl, s0, s1, st_s, st_r, y_s, o_s, order,
    in_send, in_recv, edge_send, edge_recv, pass_send, pass_recv, st_send, st_recv,
    tp_send, tp_recv, out_send, out_recv,
):
    g, c, p = lax.axis_index("req"), lax.axis_index("ctx"), lax.axis_index("tp")
    shift = lax.rem(g, 2)
    mine, heads = Owners(c, shift), Owners(c, 1 - shift)
    ends_run = lax.rem(mine.ring, 2)
    leads = mine.b == shift
    split = shift * mine.b

    barrier = pltpu.get_barrier_semaphore()

    def greet(device):
        pl.semaphore_signal(barrier, inc=1, device_id=device, device_id_type=MESH)

    for kind, who in enumerate((mine, heads)):

        def greet_set(k, carry, who=who):
            greet({"ctx": who.owner(lax.rem(who.slot + k, R))})
            return carry

        def greet_givers(k, carry, kind=kind):
            giver = Owners(c, kind + (1 - 2 * kind) * lax.rem(k, 2))
            greet({"req": k, "ctx": giver.owner(wrap(g - k, NREQ))})
            return carry

        lax.fori_loop(1, R, greet_set, 0)
        greet({"ctx": who.partner})
        lax.fori_loop(0, NREQ, greet_givers, 0)
    for k in range(1, NTP):
        greet({"tp": wrap(p + k, NTP)})
    for k in range(RUNS):
        greet({"ctx": mine.block(2 * k + 1, 1 - mine.b)})

    for slot in range(NREQ):
        taker = lax.rem(g + slot, NREQ)
        found = jnp.int32(0)
        for i in range(1, R):
            found = jnp.where(target[i] == taker, i, found)
        order[slot] = found

    def fill_scan(o, carry):
        i = order[o]
        rows = x_ref[i]
        x_s[o] = rows
        d_s[o] = dt_ref[i]
        ends = rows.astype(F32)
        for j in range(TILES):
            for k in range(3):
                edge[k * TILES + j : k * TILES + j + 1, :] = ends[
                    T - 3 + k : T - 2 + k, j * 128 : j * 128 + 128
                ]
        edge_s[o] = edge[...].astype(BF16)
        return carry

    lax.fori_loop(0, R, fill_scan, 0)

    pl.semaphore_wait(barrier, 2 * (R - 1 + 1 + NREQ) + NTP - 1 + R * ends_run)

    def in_copy(kind, who, slot, src, dst):
        return remote(
            {"ctx": who.owner(slot)},
            src.at[slot],
            dst.at[who.rank],
            in_send.at[kind, slot],
            in_recv.at[kind, who.rank],
        )

    def in_wait(kind, who, rank, dst):
        @pl.when(rank != who.rank)
        def _():
            place = dst.at[rank]
            remote(
                {"ctx": who.partner}, place, place, in_send.at[kind, rank], in_recv.at[kind, rank]
            ).wait_recv()

    inputs = ((X, mine, x_s, x_r), (KV, heads, kv_s, kv_r), (D, mine, d_s, d_r), (QU, heads, q_s, q_r))

    def edge_copy(slot):
        return remote(
            {"ctx": mine.owner(slot, 1 - mine.b)},
            edge_s.at[slot],
            edge_r.at[mine.rank // 2],
            edge_send.at[slot],
            edge_recv.at[mine.rank // 2],
        )

    @pl.when(ends_run == 1)
    def _():
        def send_edge(o, carry):
            edge_copy(o).start()
            return carry

        lax.fori_loop(0, R, send_edge, 0)

    def send_in(k, carry, which):
        for kind, who, src, dst in which:
            in_copy(kind, who, lax.rem(who.slot + k, R), src, dst).start()
        return carry

    lax.fori_loop(1, R, functools.partial(send_in, which=inputs[:1]), 0)

    def fill_attention(o, carry):
        i = order[o]
        q_s[o] = q_ref[i].reshape(2 * T * 8, HD)
        parts = [[[], []], [[], []]]
        for n in range(PAGES_REQ):
            page = table[0, 0, i * PAGES_REQ + n]
            for head in range(2):
                both = pool[page, head].astype(F32)
                for kind in range(2):
                    parts[head][kind].append(both[kind * PAGE : kind * PAGE + PAGE])
        new = fresh[i]
        for head in range(2):
            for kind in range(2):
                at = head * 128 + kind * 64
                rows = jnp.concatenate(parts[head][kind], axis=0).astype(BF16)
                kv_s[o, at : at + SPAN] = rows
                kv_s[o, at + SPAN : at + 64] = new[head, kind]
        return carry

    lax.fori_loop(0, R, fill_attention, 0)

    lax.fori_loop(1, R, functools.partial(send_in, which=inputs[1:2]), 0)
    for kind, who, src, dst in inputs:
        dst[who.rank] = src[who.slot]

    def pass_copy(n):
        return remote(
            {"ctx": heads.partner},
            kv_r.at[n],
            kv_r.at[R + n],
            pass_send.at[n],
            pass_recv.at[n],
        )

    def pass_on(n, carry):
        in_wait(KV, heads, n, kv_r)
        pass_copy(n).start()

        @pl.when(n > 0)
        def _():
            send_in(n, 0, inputs[2:])

        return carry

    lax.fori_loop(0, R, pass_on, 0)

    for j in range(TILES):
        lanes = slice(j * 128, j * 128 + 128)
        for k in range(4):
            taps[k * TILES + j : k * TILES + j + 1, :] = taps_ref[k : k + 1, lanes]
        taps[4 * TILES + j : 4 * TILES + j + 1, :] = bias[0:1, lanes]
        taps[5 * TILES + j : 5 * TILES + j + 1, :] = gains[0:1, lanes]
        a2[pl.ds(j, S, stride=TILES), :] = jnp.exp(a_log[:, lanes]) * (-LOG2E)
    own = order[mine.slot]
    old_state = ssm[own].astype(F32)
    for j in range(TILES):
        s0[pl.ds(j, S, stride=TILES), :] = old_state[:, j * 128 : j * 128 + 128]

    request = lax.broadcasted_iota(jnp.int32, (R, C), 0)
    for k in range(3):
        row = jnp.sum(jnp.where(request == own, old_x[k].astype(F32), 0.0), axis=0, keepdims=True)
        for j in range(TILES):
            edge[k * TILES + j : k * TILES + j + 1, :] = row[:, j * 128 : j * 128 + 128]

    def land_edge(i, carry):
        place = edge_r.at[i]
        remote({"ctx": mine.partner}, place, place, edge_send.at[i], edge_recv.at[i]).wait_recv()
        return carry

    lax.fori_loop(0, RUNS, land_edge, 0)
    stored = edge[...]
    for i in range(RUNS):
        late, early = edge_r[i].astype(F32), edge_r[(i + RUNS - 1) % RUNS].astype(F32)
        if i == 0:
            early = jnp.where(shift == 0, stored, early)
        at = 2 * i * PAD * TILES
        xf[at : at + 3 * TILES, :] = jnp.where(mine.b == 0, early, late)

    def land_x(n, carry):
        in_wait(X, mine, n, x_r)
        rows = x_r[n].astype(F32)
        at = (n * PAD + 3) * TILES
        for j in range(TILES):
            xf[pl.ds(at + j, T, stride=TILES), :] = rows[:, j * 128 : j * 128 + 128]
        return carry

    lax.fori_loop(0, R, land_x, 0)
    for i in range(RUNS):
        at = (2 * i + 1) * PAD * TILES
        rows = xf[at - 3 * TILES : at, :]
        if i == RUNS - 1:
            rows = jnp.where(split == 1, stored, rows)
        xf[at : at + 3 * TILES, :] = rows

    def convolve(m, carry):
        at = (m * 8 + (m // 2) * 3) * TILES
        total = jnp.zeros((8, TILES, 128), F32)
        for k in range(4):
            rows = xf[pl.ds(pl.multiple_of(at + k * TILES, TILES), 8 * TILES), :]
            weight = taps[k * TILES : k * TILES + TILES, :]
            total = total + weight[None] * rows.reshape(8, TILES, 128)
        total = total + taps[4 * TILES : 5 * TILES, :][None]
        out = (total / (1.0 + jnp.exp(-total))).astype(BF16).astype(F32)
        xc[pl.ds(pl.multiple_of(m * 8 * TILES, TILES), 8 * TILES), :] = out.reshape(8 * TILES, 128)
        return carry

    lax.fori_loop(0, R * T // 8, convolve, 0)

    total = jnp.zeros((2 * S, R * T), F32)
    for j in range(TILES):
        rows = xc[pl.ds(j, R * T, stride=TILES), :].astype(BF16)
        total = total + lax.dot_general(
            xp[:, j * 128 : j * 128 + 128],
            rows,
            (((1,), (1,)), ((), ())),
            preferred_element_type=F32,
        )
    pp[...] = total

    def tp_copy(k):
        return remote(
            {"tp": wrap(p + k, NTP)}, pp, pr.at[k - 1], tp_send.at[k], tp_recv.at[k]
        )

    for k in range(1, NTP):
        tp_copy(k).start()

    def land_d(n, carry):
        in_wait(D, mine, n, d_r)
        rows = d_r[n].astype(F32)
        soft = jnp.maximum(rows, 0.0) + jnp.log1p(jnp.exp(-jnp.abs(rows)))
        for j in range(TILES):
            dts[pl.ds(n * T * TILES + j, T, stride=TILES), :] = soft[:, j * 128 : j * 128 + 128]
        return carry

    lax.fori_loop(0, R, land_d, 0)

    for k in range(1, NTP):
        tp_copy(k).wait()
    pj[...] = jnp.transpose((pp[...] + pr[0]) + (pr[1] + pr[2]), (1, 0))
    for s in range(2 * S):
        sp[s * R * T : (s + 1) * R * T, :] = jnp.broadcast_to(pj[:, s : s + 1], (R * T, 128))

    def position(at):
        return pl.ds(pl.multiple_of(at * TILES, TILES), TILES)

    def spread(s, at):
        return jnp.broadcast_to(sp[pl.ds(s * (R * T) + at, 1), :], (TILES, 128))

    def st_copy(i):
        return remote(
            {"ctx": mine.partner}, st_s.at[i], st_r.at[i], st_send.at[i], st_recv.at[i]
        )

    def scan_run(i, carry):
        def step(t, carry):
            elapsed, state = carry[0], carry[1:]
            at = i * RUN + t
            d, x = dts[position(at), :], xc[position(at), :]
            u = d * x
            parts = [taps[5 * TILES : 6 * TILES, :] * x, None]
            new = []
            for s in range(S):
                decay = jnp.exp2(d * a2[s * TILES : s * TILES + TILES, :])
                av[at * S + s] = decay
                h = decay * state[s] + u * spread(s, at)
                new.append(h)
                y = spread(S + s, at) * h
                parts[s % 2] = y if parts[s % 2] is None else parts[s % 2] + y
            yl[position(at), :] = parts[0] + parts[1]
            return (elapsed + d, *new)

        zero = jnp.zeros((TILES, 128), F32)

        def half(h, carry):
            apart = jnp.logical_and(split == 1, i * 2 + h == 2 * RUNS - 1)
            carry = tuple(jnp.where(apart, 0.0, v) for v in carry)
            return lax.fori_loop(h * T, h * T + T, step, carry)

        last = lax.fori_loop(0, 2, half, (zero,) * (S + 1))
        high = last[0].astype(BF16).astype(F32)
        st_s[i] = jnp.concatenate([*last[1:], high, last[0] - high], axis=0).astype(BF16)
        st_copy(i).start()
        return carry

    lax.fori_loop(0, RUNS, scan_run, 0)

    def out_copy(kind, who, rank, src, dst):
        return remote(
            {"req": lax.rem(g + who.slot, NREQ), "ctx": who.block(rank)},
            src.at[rank],
            dst.at[g],
            out_send.at[kind, rank],
            out_recv.at[kind, g],
        )

    def stays(who, rank):
        return jnp.logical_and(who.slot == 0, rank == who.rank)

    def give(kind, who, rank, src, dst):
        @pl.when(jnp.logical_not(stays(who, rank)))
        def _():
            out_copy(kind, who, rank, src, dst).start()

        @pl.when(stays(who, rank))
        def _():
            dst[g] = src[rank]

    def land_kv(n, carry):
        pass_copy(n).wait_recv()
        return carry

    lax.fori_loop(0, R, land_kv, 0)
    asked = order[heads.slot]
    cached_len, new_len = clens[asked], nlens[asked]
    factor = HD**-0.5 * LOG2E
    key = lax.broadcasted_iota(jnp.int32, (1, NCTX * 64), 1)
    place, spot = key // 64, lax.rem(key, 64)
    rank = lax.rem(place, R)
    side = jnp.where(place < R, heads.b, 1 - heads.b)
    block = heads.block(rank, side)
    never = jnp.int32(1 << 20)
    cached_from = jnp.where(block * SPAN + spot < cached_len, -1, never)
    fresh_at = block * T + spot - SPAN
    fresh_from = jnp.where(fresh_at < new_len, fresh_at, never)
    seen_from = jnp.where(spot < SPAN, cached_from, fresh_from)

    def attend(k, carry):
        pair = wrap(heads.x - k, 4)
        for half in range(2):
            in_wait(QU, heads, 2 * pair + half, q_r)
        q = q_r[pl.ds(2 * pair, 2)].astype(F32).reshape(2 * T, 16, HD)
        row = lax.broadcasted_iota(jnp.int32, (2 * T * 8, 1), 0) // 8
        first, second = heads.block(2 * pair), heads.block(2 * pair + 1)
        when = jnp.where(row < T, first * T + row, second * T + row - T)
        outs = []
        for head in range(2):
            rows = q[:, head * 8 : head * 8 + 8].reshape(2 * T * 8, HD).astype(BF16)
            at = head * 128
            keys = kv_r[:, at : at + 64, :].reshape(NCTX * 64, HD)
            values = kv_r[:, at + 64 : at + 128, :].reshape(NCTX * 64, HD)
            scores = lax.dot_general(
                rows, keys, (((1,), (1,)), ((), ())), preferred_element_type=F32
            )
            scores = jnp.where(when >= seen_from, scores, -1e30)
            top = jnp.max(scores, axis=1, keepdims=True)
            weight = jnp.exp2((scores - top) * factor)
            total = jnp.sum(weight, axis=1, keepdims=True)
            out = jnp.dot(weight.astype(BF16), values, preferred_element_type=F32) / total
            out = jnp.where(when < new_len, out, 0.0)
            outs.append(out.reshape(2 * T, 8, HD))
        both = jnp.concatenate(outs, axis=1).astype(BF16)
        for half in range(2):
            o_s[2 * pair + half] = both[half * T : half * T + T]
            give(1, heads, 2 * pair + half, o_s, att)
        return carry

    lax.fori_loop(0, 4, attend, 0)

    own_len = nlens[own]

    def land_state(i, carry):
        st_copy(i).wait_recv()
        return carry

    lax.fori_loop(0, RUNS, land_state, 0)
    s1[...] = s0[...]

    def finish_run(i, carry):
        own_item = st_s[lax.rem(i + 3 * split, RUNS)].astype(F32)
        other = st_r[lax.rem(i + 3 * shift * (1 - mine.b), RUNS)].astype(F32)

        def advance(item, state):
            elapsed = item[S * TILES : (S + 1) * TILES] + item[(S + 1) * TILES :]
            decay = jnp.exp2(a2[...] * jnp.concatenate([elapsed] * S, axis=0))
            return decay * state + item[: S * TILES]

        ahead = s0[...]
        middle = advance(jnp.where(leads, own_item, other), ahead)
        after = advance(jnp.where(leads, other, own_item), middle)
        s0[...] = after
        begin = jnp.where(split == 1, after, jnp.where(leads, ahead, middle))

        def half(h, state):
            rank = i * 2 + h
            first = mine.block(rank) * T
            apart = jnp.logical_and(split == 1, rank == 2 * RUNS - 1)
            state = tuple(
                jnp.where(apart, s1[s * TILES : (s + 1) * TILES, :], state[s]) for s in range(S)
            )

            def step(t, state):
                at = rank * T + t
                parts = [yl[position(at), :], None]
                new = []
                for s in range(S):
                    h = av[at * S + s] * state[s]
                    new.append(h)
                    y = spread(S + s, at) * h
                    parts[s % 2] = y if parts[s % 2] is None else parts[s % 2] + y
                live = jnp.full((TILES, 128), first + t, jnp.int32) < own_len
                yl[position(at), :] = jnp.where(live, parts[0] + parts[1], 0.0)
                return tuple(new)

            state = lax.fori_loop(0, T, step, state)
            rows = [
                yl[pl.ds(rank * T * TILES + j, T, stride=TILES), :] for j in range(TILES)
            ]
            y_s[rank] = jnp.concatenate(rows, axis=1).astype(BF16)
            give(0, mine, rank, y_s, mix)
            return state

        lax.fori_loop(
            0, 2, half, tuple(begin[s * TILES : (s + 1) * TILES] for s in range(S))
        )
        return carry

    lax.fori_loop(0, RUNS, finish_run, 0)

    for kind, who, dst in ((0, mine, mix), (1, heads, att)):

        def land_out(giver, carry, kind=kind, who=who, dst=dst):
            own_part = jnp.logical_and(giver == g, who.slot == 0)

            @pl.when(jnp.logical_not(own_part))
            def _():
                place = dst.at[giver]
                remote(
                    {"ctx": who.partner},
                    place,
                    place,
                    out_send.at[kind, giver],
                    out_recv.at[kind, giver],
                ).wait_recv()

            return carry

        lax.fori_loop(0, NREQ, land_out, 0)

    @pl.when(ends_run == 1)
    def _():
        def sent_edge(o, carry):
            edge_copy(o).wait_send()
            return carry

        lax.fori_loop(0, R, sent_edge, 0)

    for kind, who, src, dst in inputs:

        def sent_in(k, carry, kind=kind, who=who, src=src, dst=dst):
            in_copy(kind, who, lax.rem(who.slot + k, R), src, dst).wait_send()
            return carry

        lax.fori_loop(1, R, sent_in, 0)

    def sent_rest(n, carry):
        pass_copy(n).wait_send()
        for kind, who, src, dst in ((0, mine, y_s, mix), (1, heads, o_s, att)):

            @pl.when(jnp.logical_not(stays(who, n)))
            def _():
                out_copy(kind, who, n, src, dst).wait_send()

        return carry

    lax.fori_loop(0, R, sent_rest, 0)

    def sent_state(i, carry):
        st_copy(i).wait_send()
        return carry

    lax.fori_loop(0, RUNS, sent_state, 0)


def per_device(
    queries,
    kv_pool,
    new_kv,
    block_table,
    cached_len,
    new_len,
    mamba_x,
    conv_state,
    conv_weight,
    conv_bias,
    x_proj,
    dt_raw,
    a_log,
    skip_gain,
    ssm_state,
    target_group,
):
    pool = kv_pool[:, 0].transpose(1, 3, 0, 2, 4).reshape(-1, 2, 2 * PAGE, HD)
    fresh = new_kv.transpose(1, 3, 0, 2, 4)
    vmem = pl.BlockSpec(memory_space=pltpu.VMEM)
    smem = pl.BlockSpec(memory_space=pltpu.SMEM)
    dma = pltpu.SemaphoreType.DMA
    att, mix = pl.pallas_call(
        kernel,
        out_shape=(
            jax.ShapeDtypeStruct((NREQ, T, 16, HD), BF16),
            jax.ShapeDtypeStruct((NREQ, T, C), BF16),
        ),
        in_specs=[vmem] * 12 + [smem] * 4,
        out_specs=(vmem, vmem),
        scratch_shapes=[
            pltpu.VMEM((R, T, C), BF16),
            pltpu.VMEM((R, T, C), BF16),
            pltpu.VMEM((R, T, C), BF16),
            pltpu.VMEM((R, T, C), BF16),
            pltpu.VMEM((R, 256, HD), BF16),
            pltpu.VMEM((R, 256, HD), BF16),
            pltpu.VMEM((R, 256, HD), BF16),
            pltpu.VMEM((2 * R, 256, HD), BF16),
            pltpu.VMEM((3 * TILES, 128), F32),
            pltpu.VMEM((R, 3 * TILES, 128), BF16),
            pltpu.VMEM((RUNS, 3 * TILES, 128), BF16),
            pltpu.VMEM((6 * TILES, 128), F32),
            pltpu.VMEM((S * TILES, 128), F32),
            pltpu.VMEM((R * PAD * TILES, 128), F32),
            pltpu.VMEM((R * T * TILES, 128), F32),
            pltpu.VMEM((R * T * TILES, 128), F32),
            pltpu.VMEM((2 * S, R * T), F32),
            pltpu.VMEM((NTP - 1, 2 * S, R * T), F32),
            pltpu.VMEM((R * T, 2 * S), F32),
            pltpu.VMEM((2 * S * R * T, 128), F32),
            pltpu.VMEM((R * T * S, TILES, 128), F32),
            pltpu.VMEM((R * T * TILES, 128), F32),
            pltpu.VMEM((S * TILES, 128), F32),
            pltpu.VMEM((S * TILES, 128), F32),
            pltpu.VMEM((RUNS, (S + 2) * TILES, 128), BF16),
            pltpu.VMEM((RUNS, (S + 2) * TILES, 128), BF16),
            pltpu.VMEM((R, T, C), BF16),
            pltpu.VMEM((R, T, 16, HD), BF16),
            pltpu.SMEM((NREQ,), jnp.int32),
            dma((4, R)),
            dma((4, R)),
            dma((R,)),
            dma((RUNS,)),
            dma((R,)),
            dma((R,)),
            dma((RUNS,)),
            dma((RUNS,)),
            dma((NTP,)),
            dma((NTP,)),
            dma((2, R)),
            dma((2, NREQ)),
        ],
        compiler_params=pltpu.CompilerParams(
            collective_id=0, has_side_effects=True, vmem_limit_bytes=56 << 20
        ),
    )(
        queries, pool, fresh, mamba_x, dt_raw, conv_weight, conv_bias[None], skip_gain[None],
        a_log, conv_state.transpose(1, 0, 2), x_proj, ssm_state,
        block_table, cached_len[0], new_len[0], target_group[0],
    )
    return att, mix


def solution(mesh):
    in_specs = (
        P("req", "ctx", "tp", None),
        P(None, "req", "ctx", None, "tp", None),
        P(None, "req", "ctx", "tp", None),
        P("req", "ctx", None),
        P("req", None),
        P("req", None),
        P("req", "ctx", "tp"),
        P("req", None, "tp"),
        P(None, "tp"),
        P("tp"),
        P(None, "tp"),
        P("req", "ctx", "tp"),
        P(None, "tp"),
        P("tp"),
        P("req", None, "tp"),
        P("req", None),
    )
    out_specs = (P("req", "ctx", "tp", None), P("req", "ctx", "tp"))
    return jax.shard_map(
        per_device, mesh=mesh, in_specs=in_specs, out_specs=out_specs, check_vma=False
    )
```

```python
import functools
import math

import jax
import jax.numpy as jnp
from jax import lax
from jax.experimental import pallas as pl
from jax.experimental.pallas import tpu as pltpu
from jax.sharding import PartitionSpec as P

MESH = pl.DeviceIdType.MESH
F32 = jnp.float32
BF16 = jnp.bfloat16
LOG2E = math.log2(math.e)
NREQ, NCTX, NTP = 8, 16, 4
R, T, C, S = 8, 16, 2048, 16
HD = 128
PAGE, PAGES_REQ = 8, 6
SPAN = PAGE * PAGES_REQ
TILES = C // 128
RUNS, RUN = 4, 2 * T
PAD = T + 3
X, D, KV, QU = range(4)


def wrap(a, add, n=None):
    return lax.rem(a + add, add if n is None else n)


class Owners:
    def __init__(self, c, shift):
        self.shift = shift
        self.turn = shift * (NREQ // 2)
        self.x = c // 4
        self.ring = wrap(lax.rem(c, 4) - shift, 4)
        self.b = self.ring // 2
        self.slot = self.x * 2 + self.ring + self.b * (3 - 2 * self.ring)
        second = lax.rem(self.ring, 2)
        self.rank = wrap(self.x - shift * self.b * second, 4) * 2 + second
        self.partner = self.x * 4 + lax.rem(3 - self.ring + shift, 4)

    def owner(self, slot, b=None):
        b = self.b if b is None else b
        a = lax.rem(slot, 2)
        return (slot // 2) * 4 + lax.rem(a + b * (3 - 2 * a) + self.shift, 4)

    def block(self, rank, b=None):
        b = self.b if b is None else b
        second = lax.rem(rank, 2)
        x = lax.rem(rank // 2 + self.shift * b * second, 4)
        return x * 4 + lax.rem(2 * b + second + self.shift, 4)


def remote(device, src, dst, send_sem, recv_sem):
    return pltpu.make_async_remote_copy(
        src_ref=src,
        dst_ref=dst,
        send_sem=send_sem,
        recv_sem=recv_sem,
        device_id=device,
        device_id_type=MESH,
    )


def kernel(
    q_ref, pool, fresh, x_ref, dt_ref, taps_ref, bias, gains, a_log, old_x, xp, ssm,
    table, clens, nlens, target,
    att, mix,
    x_s, x_r, d_s, d_r, q_s, q_r, kv_s, kv_r, edge, edge_s, edge_r,
    taps, a2, xf, xc, dts, pp, pr, pj, sp, av, yl, s0, s1, st_s, st_r, y_s, o_s, order,
    in_send, in_recv, edge_send, edge_recv, pass_send, pass_recv, st_send, st_recv,
    tp_send, tp_recv, out_send, out_recv,
):
    g, c, p = lax.axis_index("req"), lax.axis_index("ctx"), lax.axis_index("tp")
    shift = lax.rem(g, 2)
    mine, heads = Owners(c, shift), Owners(c, 1 - shift)
    ends_run = lax.rem(mine.ring, 2)
    leads = mine.b == shift
    split = shift * mine.b

    barrier = pltpu.get_barrier_semaphore()

    def greet(device):
        pl.semaphore_signal(barrier, inc=1, device_id=device, device_id_type=MESH)

    for kind, who in enumerate((mine, heads)):

        def greet_set(k, carry, who=who):
            greet({"ctx": who.owner(lax.rem(who.slot + k, R))})
            return carry

        def greet_givers(k, carry, kind=kind):
            giver = Owners(c, kind + (1 - 2 * kind) * lax.rem(k, 2))
            greet({"req": k, "ctx": giver.owner(wrap(g - k - giver.turn, 2 * NREQ, NREQ))})
            return carry

        lax.fori_loop(1, R, greet_set, 0)
        greet({"ctx": who.partner})
        lax.fori_loop(0, NREQ, greet_givers, 0)
    for k in range(1, NTP):
        greet({"tp": wrap(p + k, NTP)})
    for k in range(RUNS):
        greet({"ctx": mine.block(2 * k + 1, 1 - mine.b)})

    for slot in range(NREQ):
        taker = lax.rem(g + slot, NREQ)
        found = jnp.int32(0)
        for i in range(1, R):
            found = jnp.where(target[i] == taker, i, found)
        order[slot] = found

    def fill_scan(o, carry):
        i = order[lax.rem(o + mine.turn, NREQ)]
        rows = x_ref[i]
        x_s[o] = rows
        d_s[o] = dt_ref[i]
        ends = rows.astype(F32)
        for j in range(TILES):
            for k in range(3):
                edge[k * TILES + j : k * TILES + j + 1, :] = ends[
                    T - 3 + k : T - 2 + k, j * 128 : j * 128 + 128
                ]
        edge_s[o] = edge[...].astype(BF16)
        return carry

    lax.fori_loop(0, R, fill_scan, 0)

    pl.semaphore_wait(barrier, 2 * (R - 1 + 1 + NREQ) + NTP - 1 + R * ends_run)

    def in_copy(kind, who, slot, src, dst):
        return remote(
            {"ctx": who.owner(slot)},
            src.at[slot],
            dst.at[who.rank],
            in_send.at[kind, slot],
            in_recv.at[kind, who.rank],
        )

    def in_wait(kind, who, rank, dst):
        @pl.when(rank != who.rank)
        def _():
            place = dst.at[rank]
            remote(
                {"ctx": who.partner}, place, place, in_send.at[kind, rank], in_recv.at[kind, rank]
            ).wait_recv()

    inputs = ((X, mine, x_s, x_r), (KV, heads, kv_s, kv_r), (D, mine, d_s, d_r), (QU, heads, q_s, q_r))

    def edge_copy(slot):
        return remote(
            {"ctx": mine.owner(slot, 1 - mine.b)},
            edge_s.at[slot],
            edge_r.at[mine.rank // 2],
            edge_send.at[slot],
            edge_recv.at[mine.rank // 2],
        )

    @pl.when(ends_run == 1)
    def _():
        def send_edge(o, carry):
            edge_copy(o).start()
            return carry

        lax.fori_loop(0, R, send_edge, 0)

    def send_in(k, carry, which):
        for kind, who, src, dst in which:
            in_copy(kind, who, lax.rem(who.slot + k, R), src, dst).start()
        return carry

    lax.fori_loop(1, R, functools.partial(send_in, which=inputs[:1]), 0)

    def fill_attention(o, carry):
        i = order[lax.rem(o + heads.turn, NREQ)]
        q_s[o] = q_ref[i].reshape(2 * T * 8, HD)
        parts = [[[], []], [[], []]]
        for n in range(PAGES_REQ):
            page = table[0, 0, i * PAGES_REQ + n]
            for head in range(2):
                both = pool[page, head].astype(F32)
                for kind in range(2):
                    parts[head][kind].append(both[kind * PAGE : kind * PAGE + PAGE])
        new = fresh[i]
        for head in range(2):
            for kind in range(2):
                at = head * 128 + kind * 64
                rows = jnp.concatenate(parts[head][kind], axis=0).astype(BF16)
                kv_s[o, at : at + SPAN] = rows
                kv_s[o, at + SPAN : at + 64] = new[head, kind]
        return carry

    lax.fori_loop(0, R, fill_attention, 0)

    lax.fori_loop(1, R, functools.partial(send_in, which=inputs[1:2]), 0)
    for kind, who, src, dst in inputs:
        dst[who.rank] = src[who.slot]

    def pass_copy(n):
        return remote(
            {"ctx": heads.partner},
            kv_r.at[n],
            kv_r.at[R + n],
            pass_send.at[n],
            pass_recv.at[n],
        )

    def pass_on(n, carry):
        in_wait(KV, heads, n, kv_r)
        pass_copy(n).start()

        @pl.when(n > 0)
        def _():
            send_in(n, 0, inputs[2:])

        return carry

    lax.fori_loop(0, R, pass_on, 0)

    for j in range(TILES):
        lanes = slice(j * 128, j * 128 + 128)
        for k in range(4):
            taps[k * TILES + j : k * TILES + j + 1, :] = taps_ref[k : k + 1, lanes]
        taps[4 * TILES + j : 4 * TILES + j + 1, :] = bias[0:1, lanes]
        taps[5 * TILES + j : 5 * TILES + j + 1, :] = gains[0:1, lanes]
        a2[pl.ds(j, S, stride=TILES), :] = jnp.exp(a_log[:, lanes]) * (-LOG2E)
    own = order[lax.rem(mine.slot + mine.turn, NREQ)]
    old_state = ssm[own].astype(F32)
    for j in range(TILES):
        s0[pl.ds(j, S, stride=TILES), :] = old_state[:, j * 128 : j * 128 + 128]

    request = lax.broadcasted_iota(jnp.int32, (R, C), 0)
    for k in range(3):
        row = jnp.sum(jnp.where(request == own, old_x[k].astype(F32), 0.0), axis=0, keepdims=True)
        for j in range(TILES):
            edge[k * TILES + j : k * TILES + j + 1, :] = row[:, j * 128 : j * 128 + 128]

    def land_edge(i, carry):
        place = edge_r.at[i]
        remote({"ctx": mine.partner}, place, place, edge_send.at[i], edge_recv.at[i]).wait_recv()
        return carry

    lax.fori_loop(0, RUNS, land_edge, 0)
    stored = edge[...]
    for i in range(RUNS):
        late, early = edge_r[i].astype(F32), edge_r[(i + RUNS - 1) % RUNS].astype(F32)
        if i == 0:
            early = jnp.where(shift == 0, stored, early)
        at = 2 * i * PAD * TILES
        xf[at : at + 3 * TILES, :] = jnp.where(mine.b == 0, early, late)

    def land_x(n, carry):
        in_wait(X, mine, n, x_r)
        rows = x_r[n].astype(F32)
        at = (n * PAD + 3) * TILES
        for j in range(TILES):
            xf[pl.ds(at + j, T, stride=TILES), :] = rows[:, j * 128 : j * 128 + 128]
        return carry

    lax.fori_loop(0, R, land_x, 0)
    for i in range(RUNS):
        at = (2 * i + 1) * PAD * TILES
        rows = xf[at - 3 * TILES : at, :]
        if i == RUNS - 1:
            rows = jnp.where(split == 1, stored, rows)
        xf[at : at + 3 * TILES, :] = rows

    def convolve(m, carry):
        at = (m * 8 + (m // 2) * 3) * TILES
        total = jnp.zeros((8, TILES, 128), F32)
        for k in range(4):
            rows = xf[pl.ds(pl.multiple_of(at + k * TILES, TILES), 8 * TILES), :]
            weight = taps[k * TILES : k * TILES + TILES, :]
            total = total + weight[None] * rows.reshape(8, TILES, 128)
        total = total + taps[4 * TILES : 5 * TILES, :][None]
        out = (total / (1.0 + jnp.exp(-total))).astype(BF16).astype(F32)
        xc[pl.ds(pl.multiple_of(m * 8 * TILES, TILES), 8 * TILES), :] = out.reshape(8 * TILES, 128)
        return carry

    lax.fori_loop(0, R * T // 8, convolve, 0)

    total = jnp.zeros((2 * S, R * T), F32)
    for j in range(TILES):
        rows = xc[pl.ds(j, R * T, stride=TILES), :].astype(BF16)
        total = total + lax.dot_general(
            xp[:, j * 128 : j * 128 + 128],
            rows,
            (((1,), (1,)), ((), ())),
            preferred_element_type=F32,
        )
    pp[...] = total

    def tp_copy(k):
        return remote(
            {"tp": wrap(p + k, NTP)}, pp, pr.at[k - 1], tp_send.at[k], tp_recv.at[k]
        )

    for k in range(1, NTP):
        tp_copy(k).start()

    def land_d(n, carry):
        in_wait(D, mine, n, d_r)
        rows = d_r[n].astype(F32)
        soft = jnp.maximum(rows, 0.0) + jnp.log1p(jnp.exp(-jnp.abs(rows)))
        for j in range(TILES):
            dts[pl.ds(n * T * TILES + j, T, stride=TILES), :] = soft[:, j * 128 : j * 128 + 128]
        return carry

    lax.fori_loop(0, R, land_d, 0)

    for k in range(1, NTP):
        tp_copy(k).wait()
    pj[...] = jnp.transpose((pp[...] + pr[0]) + (pr[1] + pr[2]), (1, 0))
    for s in range(2 * S):
        sp[s * R * T : (s + 1) * R * T, :] = jnp.broadcast_to(pj[:, s : s + 1], (R * T, 128))

    def position(at):
        return pl.ds(pl.multiple_of(at * TILES, TILES), TILES)

    def spread(s, at):
        return jnp.broadcast_to(sp[pl.ds(s * (R * T) + at, 1), :], (TILES, 128))

    def st_copy(i):
        return remote(
            {"ctx": mine.partner}, st_s.at[i], st_r.at[i], st_send.at[i], st_recv.at[i]
        )

    def scan_run(i, carry):
        def step(t, carry):
            elapsed, state = carry[0], carry[1:]
            at = i * RUN + t
            d, x = dts[position(at), :], xc[position(at), :]
            u = d * x
            parts = [taps[5 * TILES : 6 * TILES, :] * x, None]
            new = []
            for s in range(S):
                decay = jnp.exp2(d * a2[s * TILES : s * TILES + TILES, :])
                av[at * S + s] = decay
                h = decay * state[s] + u * spread(s, at)
                new.append(h)
                y = spread(S + s, at) * h
                parts[s % 2] = y if parts[s % 2] is None else parts[s % 2] + y
            yl[position(at), :] = parts[0] + parts[1]
            return (elapsed + d, *new)

        zero = jnp.zeros((TILES, 128), F32)

        def half(h, carry):
            apart = jnp.logical_and(split == 1, i * 2 + h == 2 * RUNS - 1)
            carry = tuple(jnp.where(apart, 0.0, v) for v in carry)
            return lax.fori_loop(h * T, h * T + T, step, carry)

        last = lax.fori_loop(0, 2, half, (zero,) * (S + 1))
        high = last[0].astype(BF16).astype(F32)
        st_s[i] = jnp.concatenate([*last[1:], high, last[0] - high], axis=0).astype(BF16)
        st_copy(i).start()
        return carry

    lax.fori_loop(0, RUNS, scan_run, 0)

    def out_copy(kind, who, rank, src, dst):
        return remote(
            {"req": lax.rem(g + who.slot + who.turn, NREQ), "ctx": who.block(rank)},
            src.at[rank],
            dst.at[g],
            out_send.at[kind, rank],
            out_recv.at[kind, g],
        )

    def stays(who, rank):
        return jnp.logical_and(lax.rem(who.slot + who.turn, NREQ) == 0, rank == who.rank)

    def give(kind, who, rank, src, dst):
        @pl.when(jnp.logical_not(stays(who, rank)))
        def _():
            out_copy(kind, who, rank, src, dst).start()

        @pl.when(stays(who, rank))
        def _():
            dst[g] = src[rank]

    def land_kv(n, carry):
        pass_copy(n).wait_recv()
        return carry

    lax.fori_loop(0, R, land_kv, 0)
    asked = order[lax.rem(heads.slot + heads.turn, NREQ)]
    cached_len, new_len = clens[asked], nlens[asked]
    factor = HD**-0.5 * LOG2E
    key = lax.broadcasted_iota(jnp.int32, (1, NCTX * 64), 1)
    place, spot = key // 64, lax.rem(key, 64)
    rank = lax.rem(place, R)
    side = jnp.where(place < R, heads.b, 1 - heads.b)
    block = heads.block(rank, side)
    never = jnp.int32(1 << 20)
    cached_from = jnp.where(block * SPAN + spot < cached_len, -1, never)
    fresh_at = block * T + spot - SPAN
    fresh_from = jnp.where(fresh_at < new_len, fresh_at, never)
    seen_from = jnp.where(spot < SPAN, cached_from, fresh_from)

    def attend(k, carry):
        pair = wrap(heads.x - k, 4)
        for half in range(2):
            in_wait(QU, heads, 2 * pair + half, q_r)
        q = q_r[pl.ds(2 * pair, 2)].astype(F32).reshape(2 * T, 16, HD)
        row = lax.broadcasted_iota(jnp.int32, (2 * T * 8, 1), 0) // 8
        first, second = heads.block(2 * pair), heads.block(2 * pair + 1)
        when = jnp.where(row < T, first * T + row, second * T + row - T)
        outs = []
        for head in range(2):
            rows = q[:, head * 8 : head * 8 + 8].reshape(2 * T * 8, HD).astype(BF16)
            at = head * 128
            keys = kv_r[:, at : at + 64, :].reshape(NCTX * 64, HD)
            values = kv_r[:, at + 64 : at + 128, :].reshape(NCTX * 64, HD)
            scores = lax.dot_general(
                rows, keys, (((1,), (1,)), ((), ())), preferred_element_type=F32
            )
            scores = jnp.where(when >= seen_from, scores, -1e30)
            top = jnp.max(scores, axis=1, keepdims=True)
            weight = jnp.exp2((scores - top) * factor)
            total = jnp.sum(weight, axis=1, keepdims=True)
            out = jnp.dot(weight.astype(BF16), values, preferred_element_type=F32) / total
            out = jnp.where(when < new_len, out, 0.0)
            outs.append(out.reshape(2 * T, 8, HD))
        both = jnp.concatenate(outs, axis=1).astype(BF16)
        for half in range(2):
            o_s[2 * pair + half] = both[half * T : half * T + T]
            give(1, heads, 2 * pair + half, o_s, att)
        return carry

    lax.fori_loop(0, 4, attend, 0)

    own_len = nlens[own]

    def land_state(i, carry):
        st_copy(i).wait_recv()
        return carry

    lax.fori_loop(0, RUNS, land_state, 0)
    s1[...] = s0[...]

    def finish_run(i, carry):
        own_item = st_s[lax.rem(i + 3 * split, RUNS)].astype(F32)
        other = st_r[lax.rem(i + 3 * shift * (1 - mine.b), RUNS)].astype(F32)

        def advance(item, state):
            elapsed = item[S * TILES : (S + 1) * TILES] + item[(S + 1) * TILES :]
            decay = jnp.exp2(a2[...] * jnp.concatenate([elapsed] * S, axis=0))
            return decay * state + item[: S * TILES]

        ahead = s0[...]
        middle = advance(jnp.where(leads, own_item, other), ahead)
        after = advance(jnp.where(leads, other, own_item), middle)
        s0[...] = after
        begin = jnp.where(split == 1, after, jnp.where(leads, ahead, middle))

        def half(h, state):
            rank = i * 2 + h
            first = mine.block(rank) * T
            apart = jnp.logical_and(split == 1, rank == 2 * RUNS - 1)
            state = tuple(
                jnp.where(apart, s1[s * TILES : (s + 1) * TILES, :], state[s]) for s in range(S)
            )

            def step(t, state):
                at = rank * T + t
                parts = [yl[position(at), :], None]
                new = []
                for s in range(S):
                    h = av[at * S + s] * state[s]
                    new.append(h)
                    y = spread(S + s, at) * h
                    parts[s % 2] = y if parts[s % 2] is None else parts[s % 2] + y
                live = jnp.full((TILES, 128), first + t, jnp.int32) < own_len
                yl[position(at), :] = jnp.where(live, parts[0] + parts[1], 0.0)
                return tuple(new)

            state = lax.fori_loop(0, T, step, state)
            rows = [
                yl[pl.ds(rank * T * TILES + j, T, stride=TILES), :] for j in range(TILES)
            ]
            y_s[rank] = jnp.concatenate(rows, axis=1).astype(BF16)
            give(0, mine, rank, y_s, mix)
            return state

        lax.fori_loop(
            0, 2, half, tuple(begin[s * TILES : (s + 1) * TILES] for s in range(S))
        )
        return carry

    lax.fori_loop(0, RUNS, finish_run, 0)

    for kind, who, dst in ((0, mine, mix), (1, heads, att)):

        def land_out(giver, carry, kind=kind, who=who, dst=dst):
            own_part = jnp.logical_and(giver == g, lax.rem(who.slot + who.turn, NREQ) == 0)

            @pl.when(jnp.logical_not(own_part))
            def _():
                place = dst.at[giver]
                remote(
                    {"ctx": who.partner},
                    place,
                    place,
                    out_send.at[kind, giver],
                    out_recv.at[kind, giver],
                ).wait_recv()

            return carry

        lax.fori_loop(0, NREQ, land_out, 0)

    @pl.when(ends_run == 1)
    def _():
        def sent_edge(o, carry):
            edge_copy(o).wait_send()
            return carry

        lax.fori_loop(0, R, sent_edge, 0)

    for kind, who, src, dst in inputs:

        def sent_in(k, carry, kind=kind, who=who, src=src, dst=dst):
            in_copy(kind, who, lax.rem(who.slot + k, R), src, dst).wait_send()
            return carry

        lax.fori_loop(1, R, sent_in, 0)

    def sent_rest(n, carry):
        pass_copy(n).wait_send()
        for kind, who, src, dst in ((0, mine, y_s, mix), (1, heads, o_s, att)):

            @pl.when(jnp.logical_not(stays(who, n)))
            def _():
                out_copy(kind, who, n, src, dst).wait_send()

        return carry

    lax.fori_loop(0, R, sent_rest, 0)

    def sent_state(i, carry):
        st_copy(i).wait_send()
        return carry

    lax.fori_loop(0, RUNS, sent_state, 0)


def per_device(
    queries,
    kv_pool,
    new_kv,
    block_table,
    cached_len,
    new_len,
    mamba_x,
    conv_state,
    conv_weight,
    conv_bias,
    x_proj,
    dt_raw,
    a_log,
    skip_gain,
    ssm_state,
    target_group,
):
    pool = kv_pool[:, 0].transpose(1, 3, 0, 2, 4).reshape(-1, 2, 2 * PAGE, HD)
    fresh = new_kv.transpose(1, 3, 0, 2, 4)
    vmem = pl.BlockSpec(memory_space=pltpu.VMEM)
    smem = pl.BlockSpec(memory_space=pltpu.SMEM)
    dma = pltpu.SemaphoreType.DMA
    att, mix = pl.pallas_call(
        kernel,
        out_shape=(
            jax.ShapeDtypeStruct((NREQ, T, 16, HD), BF16),
            jax.ShapeDtypeStruct((NREQ, T, C), BF16),
        ),
        in_specs=[vmem] * 12 + [smem] * 4,
        out_specs=(vmem, vmem),
        scratch_shapes=[
            pltpu.VMEM((R, T, C), BF16),
            pltpu.VMEM((R, T, C), BF16),
            pltpu.VMEM((R, T, C), BF16),
            pltpu.VMEM((R, T, C), BF16),
            pltpu.VMEM((R, 256, HD), BF16),
            pltpu.VMEM((R, 256, HD), BF16),
            pltpu.VMEM((R, 256, HD), BF16),
            pltpu.VMEM((2 * R, 256, HD), BF16),
            pltpu.VMEM((3 * TILES, 128), F32),
            pltpu.VMEM((R, 3 * TILES, 128), BF16),
            pltpu.VMEM((RUNS, 3 * TILES, 128), BF16),
            pltpu.VMEM((6 * TILES, 128), F32),
            pltpu.VMEM((S * TILES, 128), F32),
            pltpu.VMEM((R * PAD * TILES, 128), F32),
            pltpu.VMEM((R * T * TILES, 128), F32),
            pltpu.VMEM((R * T * TILES, 128), F32),
            pltpu.VMEM((2 * S, R * T), F32),
            pltpu.VMEM((NTP - 1, 2 * S, R * T), F32),
            pltpu.VMEM((R * T, 2 * S), F32),
            pltpu.VMEM((2 * S * R * T, 128), F32),
            pltpu.VMEM((R * T * S, TILES, 128), F32),
            pltpu.VMEM((R * T * TILES, 128), F32),
            pltpu.VMEM((S * TILES, 128), F32),
            pltpu.VMEM((S * TILES, 128), F32),
            pltpu.VMEM((RUNS, (S + 2) * TILES, 128), BF16),
            pltpu.VMEM((RUNS, (S + 2) * TILES, 128), BF16),
            pltpu.VMEM((R, T, C), BF16),
            pltpu.VMEM((R, T, 16, HD), BF16),
            pltpu.SMEM((NREQ,), jnp.int32),
            dma((4, R)),
            dma((4, R)),
            dma((R,)),
            dma((RUNS,)),
            dma((R,)),
            dma((R,)),
            dma((RUNS,)),
            dma((RUNS,)),
            dma((NTP,)),
            dma((NTP,)),
            dma((2, R)),
            dma((2, NREQ)),
        ],
        compiler_params=pltpu.CompilerParams(
            collective_id=0, has_side_effects=True, vmem_limit_bytes=56 << 20
        ),
    )(
        queries, pool, fresh, mamba_x, dt_raw, conv_weight, conv_bias[None], skip_gain[None],
        a_log, conv_state.transpose(1, 0, 2), x_proj, ssm_state,
        block_table, cached_len[0], new_len[0], target_group[0],
    )
    return att, mix


def solution(mesh):
    in_specs = (
        P("req", "ctx", "tp", None),
        P(None, "req", "ctx", None, "tp", None),
        P(None, "req", "ctx", "tp", None),
        P("req", "ctx", None),
        P("req", None),
        P("req", None),
        P("req", "ctx", "tp"),
        P("req", None, "tp"),
        P(None, "tp"),
        P("tp"),
        P(None, "tp"),
        P("req", "ctx", "tp"),
        P(None, "tp"),
        P("tp"),
        P("req", None, "tp"),
        P("req", None),
    )
    out_specs = (P("req", "ctx", "tp", None), P("req", "ctx", "tp"))
    return jax.shard_map(
        per_device, mesh=mesh, in_specs=in_specs, out_specs=out_specs, check_vma=False
    )
```

```python
import functools
import math

import jax
import jax.numpy as jnp
from jax import lax
from jax.experimental import pallas as pl
from jax.experimental.pallas import tpu as pltpu
from jax.sharding import PartitionSpec as P

MESH = pl.DeviceIdType.MESH
F32 = jnp.float32
BF16 = jnp.bfloat16
LOG2E = math.log2(math.e)
NREQ, NCTX, NTP = 8, 16, 4
R, T, C, S = 8, 16, 2048, 16
HD = 128
PAGE, PAGES_REQ = 8, 6
SPAN = PAGE * PAGES_REQ
TILES = C // 128
RUNS, RUN = 4, 2 * T
PAD = T + 3
X, D, KV, QU = range(4)


def wrap(a, add, n=None):
    return lax.rem(a + add, add if n is None else n)


class Owners:
    def __init__(self, c, shift):
        self.shift = shift
        self.turn = shift * (NREQ // 2)
        self.x = c // 4
        self.ring = wrap(lax.rem(c, 4) - shift, 4)
        self.b = self.ring // 2
        self.slot = self.x * 2 + self.ring + self.b * (3 - 2 * self.ring)
        second = lax.rem(self.ring, 2)
        self.rank = wrap(self.x - shift * self.b * second, 4) * 2 + second
        self.partner = self.x * 4 + lax.rem(3 - self.ring + shift, 4)

    def owner(self, slot, b=None):
        b = self.b if b is None else b
        a = lax.rem(slot, 2)
        return (slot // 2) * 4 + lax.rem(a + b * (3 - 2 * a) + self.shift, 4)

    def block(self, rank, b=None):
        b = self.b if b is None else b
        second = lax.rem(rank, 2)
        x = lax.rem(rank // 2 + self.shift * b * second, 4)
        return x * 4 + lax.rem(2 * b + second + self.shift, 4)


def remote(device, src, dst, send_sem, recv_sem):
    return pltpu.make_async_remote_copy(
        src_ref=src,
        dst_ref=dst,
        send_sem=send_sem,
        recv_sem=recv_sem,
        device_id=device,
        device_id_type=MESH,
    )


def kernel(
    q_ref, pool, fresh, x_ref, dt_ref, taps_ref, bias, gains, a_log, old_x, xp, ssm,
    table, clens, nlens, target,
    att, mix,
    x_s, x_r, d_s, d_r, q_s, q_r, kv_s, kv_r, edge, edge_s, edge_r,
    taps, a2, xf, xc, dts, pp, pr, pj, sp, av, yl, s0, s1, st_s, st_r, y_s, o_s, order,
    in_send, in_recv, edge_send, edge_recv, pass_send, pass_recv, st_send, st_recv,
    tp_send, tp_recv, out_send, out_recv,
):
    g, c, p = lax.axis_index("req"), lax.axis_index("ctx"), lax.axis_index("tp")
    shift = lax.rem(g, 2)
    mine, heads = Owners(c, shift), Owners(c, 1 - shift)
    ends_run = lax.rem(mine.ring, 2)
    leads = mine.b == shift
    split = shift * mine.b

    barrier = pltpu.get_barrier_semaphore()

    def greet(device):
        pl.semaphore_signal(barrier, inc=1, device_id=device, device_id_type=MESH)

    for kind, who in enumerate((mine, heads)):

        def greet_set(k, carry, who=who):
            greet({"ctx": who.owner(lax.rem(who.slot + k, R))})
            return carry

        def greet_givers(k, carry, kind=kind):
            giver = Owners(c, kind + (1 - 2 * kind) * lax.rem(k, 2))
            greet({"req": k, "ctx": giver.owner(wrap(g - k - giver.turn, 2 * NREQ, NREQ))})
            return carry

        lax.fori_loop(1, R, greet_set, 0)
        greet({"ctx": who.partner})
        lax.fori_loop(0, NREQ, greet_givers, 0)
    for k in range(1, NTP):
        greet({"tp": wrap(p + k, NTP)})
    for k in range(RUNS):
        greet({"ctx": mine.block(2 * k + 1, 1 - mine.b)})

    for slot in range(NREQ):
        taker = lax.rem(g + slot, NREQ)
        found = jnp.int32(0)
        for i in range(1, R):
            found = jnp.where(target[i] == taker, i, found)
        order[slot] = found

    def fill_scan(o, carry):
        i = order[lax.rem(o + mine.turn, NREQ)]
        rows = x_ref[i]
        x_s[o] = rows
        d_s[o] = dt_ref[i]
        ends = rows.astype(F32)
        for j in range(TILES):
            for k in range(3):
                edge[k * TILES + j : k * TILES + j + 1, :] = ends[
                    T - 3 + k : T - 2 + k, j * 128 : j * 128 + 128
                ]
        edge_s[o] = edge[...].astype(BF16)
        return carry

    lax.fori_loop(0, R, fill_scan, 0)

    pl.semaphore_wait(barrier, 2 * (R - 1 + 1 + NREQ) + NTP - 1 + R * ends_run)

    def in_copy(kind, who, slot, src, dst):
        return remote(
            {"ctx": who.owner(slot)},
            src.at[slot],
            dst.at[who.rank],
            in_send.at[kind, slot],
            in_recv.at[kind, who.rank],
        )

    def in_wait(kind, who, rank, dst):
        @pl.when(rank != who.rank)
        def _():
            place = dst.at[rank]
            remote(
                {"ctx": who.partner}, place, place, in_send.at[kind, rank], in_recv.at[kind, rank]
            ).wait_recv()

    inputs = ((X, mine, x_s, x_r), (D, mine, d_s, d_r), (KV, heads, kv_s, kv_r), (QU, heads, q_s, q_r))

    def edge_copy(slot):
        return remote(
            {"ctx": mine.owner(slot, 1 - mine.b)},
            edge_s.at[slot],
            edge_r.at[mine.rank // 2],
            edge_send.at[slot],
            edge_recv.at[mine.rank // 2],
        )

    @pl.when(ends_run == 1)
    def _():
        def send_edge(o, carry):
            edge_copy(o).start()
            return carry

        lax.fori_loop(0, R, send_edge, 0)

    def send_in(k, carry, which):
        for kind, who, src, dst in which:
            in_copy(kind, who, lax.rem(who.slot + k, R), src, dst).start()
        return carry

    lax.fori_loop(1, R, functools.partial(send_in, which=inputs[:2]), 0)

    def fill_attention(o, carry):
        i = order[lax.rem(o + heads.turn, NREQ)]
        q_s[o] = q_ref[i].reshape(2 * T * 8, HD)
        parts = [[[], []], [[], []]]
        for n in range(PAGES_REQ):
            page = table[0, 0, i * PAGES_REQ + n]
            for head in range(2):
                both = pool[page, head].astype(F32)
                for kind in range(2):
                    parts[head][kind].append(both[kind * PAGE : kind * PAGE + PAGE])
        new = fresh[i]
        for head in range(2):
            for kind in range(2):
                at = head * 128 + kind * 64
                rows = jnp.concatenate(parts[head][kind], axis=0).astype(BF16)
                kv_s[o, at : at + SPAN] = rows
                kv_s[o, at + SPAN : at + 64] = new[head, kind]
        return carry

    lax.fori_loop(0, R, fill_attention, 0)

    lax.fori_loop(1, R, functools.partial(send_in, which=inputs[2:3]), 0)
    for kind, who, src, dst in inputs:
        dst[who.rank] = src[who.slot]

    def pass_copy(n):
        return remote(
            {"ctx": heads.partner},
            kv_r.at[n],
            kv_r.at[R + n],
            pass_send.at[n],
            pass_recv.at[n],
        )

    def pass_on(n, carry):
        in_wait(KV, heads, n, kv_r)
        pass_copy(n).start()

        @pl.when(n > 0)
        def _():
            send_in(n, 0, inputs[3:])

        return carry

    lax.fori_loop(0, R, pass_on, 0)

    for j in range(TILES):
        lanes = slice(j * 128, j * 128 + 128)
        for k in range(4):
            taps[k * TILES + j : k * TILES + j + 1, :] = taps_ref[k : k + 1, lanes]
        taps[4 * TILES + j : 4 * TILES + j + 1, :] = bias[0:1, lanes]
        taps[5 * TILES + j : 5 * TILES + j + 1, :] = gains[0:1, lanes]
        a2[pl.ds(j, S, stride=TILES), :] = jnp.exp(a_log[:, lanes]) * (-LOG2E)
    own = order[lax.rem(mine.slot + mine.turn, NREQ)]
    old_state = ssm[own].astype(F32)
    for j in range(TILES):
        s0[pl.ds(j, S, stride=TILES), :] = old_state[:, j * 128 : j * 128 + 128]

    request = lax.broadcasted_iota(jnp.int32, (R, C), 0)
    for k in range(3):
        row = jnp.sum(jnp.where(request == own, old_x[k].astype(F32), 0.0), axis=0, keepdims=True)
        for j in range(TILES):
            edge[k * TILES + j : k * TILES + j + 1, :] = row[:, j * 128 : j * 128 + 128]

    def land_edge(i, carry):
        place = edge_r.at[i]
        remote({"ctx": mine.partner}, place, place, edge_send.at[i], edge_recv.at[i]).wait_recv()
        return carry

    lax.fori_loop(0, RUNS, land_edge, 0)
    stored = edge[...]
    for i in range(RUNS):
        late, early = edge_r[i].astype(F32), edge_r[(i + RUNS - 1) % RUNS].astype(F32)
        if i == 0:
            early = jnp.where(shift == 0, stored, early)
        at = 2 * i * PAD * TILES
        xf[at : at + 3 * TILES, :] = jnp.where(mine.b == 0, early, late)

    def land_x(n, carry):
        in_wait(X, mine, n, x_r)
        rows = x_r[n].astype(F32)
        at = (n * PAD + 3) * TILES
        for j in range(TILES):
            xf[pl.ds(at + j, T, stride=TILES), :] = rows[:, j * 128 : j * 128 + 128]
        return carry

    lax.fori_loop(0, R, land_x, 0)
    for i in range(RUNS):
        at = (2 * i + 1) * PAD * TILES
        rows = xf[at - 3 * TILES : at, :]
        if i == RUNS - 1:
            rows = jnp.where(split == 1, stored, rows)
        xf[at : at + 3 * TILES, :] = rows

    def convolve(m, carry):
        at = (m * 8 + (m // 2) * 3) * TILES
        total = jnp.zeros((8, TILES, 128), F32)
        for k in range(4):
            rows = xf[pl.ds(pl.multiple_of(at + k * TILES, TILES), 8 * TILES), :]
            weight = taps[k * TILES : k * TILES + TILES, :]
            total = total + weight[None] * rows.reshape(8, TILES, 128)
        total = total + taps[4 * TILES : 5 * TILES, :][None]
        out = (total / (1.0 + jnp.exp(-total))).astype(BF16).astype(F32)
        xc[pl.ds(pl.multiple_of(m * 8 * TILES, TILES), 8 * TILES), :] = out.reshape(8 * TILES, 128)
        return carry

    lax.fori_loop(0, R * T // 8, convolve, 0)

    total = jnp.zeros((2 * S, R * T), F32)
    for j in range(TILES):
        rows = xc[pl.ds(j, R * T, stride=TILES), :].astype(BF16)
        total = total + lax.dot_general(
            xp[:, j * 128 : j * 128 + 128],
            rows,
            (((1,), (1,)), ((), ())),
            preferred_element_type=F32,
        )
    pp[...] = total

    def tp_copy(k):
        return remote(
            {"tp": wrap(p + k, NTP)}, pp, pr.at[k - 1], tp_send.at[k], tp_recv.at[k]
        )

    for k in range(1, NTP):
        tp_copy(k).start()

    def land_d(n, carry):
        in_wait(D, mine, n, d_r)
        rows = d_r[n].astype(F32)
        soft = jnp.maximum(rows, 0.0) + jnp.log1p(jnp.exp(-jnp.abs(rows)))
        for j in range(TILES):
            dts[pl.ds(n * T * TILES + j, T, stride=TILES), :] = soft[:, j * 128 : j * 128 + 128]
        return carry

    lax.fori_loop(0, R, land_d, 0)

    for k in range(1, NTP):
        tp_copy(k).wait()
    pj[...] = jnp.transpose((pp[...] + pr[0]) + (pr[1] + pr[2]), (1, 0))
    for s in range(2 * S):
        sp[s * R * T : (s + 1) * R * T, :] = jnp.broadcast_to(pj[:, s : s + 1], (R * T, 128))

    def position(at):
        return pl.ds(pl.multiple_of(at * TILES, TILES), TILES)

    def spread(s, at):
        return jnp.broadcast_to(sp[pl.ds(s * (R * T) + at, 1), :], (TILES, 128))

    def st_copy(i):
        return remote(
            {"ctx": mine.partner}, st_s.at[i], st_r.at[i], st_send.at[i], st_recv.at[i]
        )

    def scan_run(i, carry):
        def step(t, carry):
            elapsed, state = carry[0], carry[1:]
            at = i * RUN + t
            d, x = dts[position(at), :], xc[position(at), :]
            u = d * x
            parts = [taps[5 * TILES : 6 * TILES, :] * x, None]
            new = []
            for s in range(S):
                decay = jnp.exp2(d * a2[s * TILES : s * TILES + TILES, :])
                av[at * S + s] = decay
                h = decay * state[s] + u * spread(s, at)
                new.append(h)
                y = spread(S + s, at) * h
                parts[s % 2] = y if parts[s % 2] is None else parts[s % 2] + y
            yl[position(at), :] = parts[0] + parts[1]
            return (elapsed + d, *new)

        zero = jnp.zeros((TILES, 128), F32)

        def half(h, carry):
            apart = jnp.logical_and(split == 1, i * 2 + h == 2 * RUNS - 1)
            carry = tuple(jnp.where(apart, 0.0, v) for v in carry)
            return lax.fori_loop(h * T, h * T + T, step, carry)

        last = lax.fori_loop(0, 2, half, (zero,) * (S + 1))
        high = last[0].astype(BF16).astype(F32)
        st_s[i] = jnp.concatenate([*last[1:], high, last[0] - high], axis=0).astype(BF16)
        st_copy(i).start()
        return carry

    lax.fori_loop(0, RUNS, scan_run, 0)

    def out_copy(kind, who, rank, src, dst):
        return remote(
            {"req": lax.rem(g + who.slot + who.turn, NREQ), "ctx": who.block(rank)},
            src.at[rank],
            dst.at[g],
            out_send.at[kind, rank],
            out_recv.at[kind, g],
        )

    def stays(who, rank):
        return jnp.logical_and(lax.rem(who.slot + who.turn, NREQ) == 0, rank == who.rank)

    def give(kind, who, rank, src, dst):
        @pl.when(jnp.logical_not(stays(who, rank)))
        def _():
            out_copy(kind, who, rank, src, dst).start()

        @pl.when(stays(who, rank))
        def _():
            dst[g] = src[rank]

    def land_kv(n, carry):
        pass_copy(n).wait_recv()
        return carry

    lax.fori_loop(0, R, land_kv, 0)
    asked = order[lax.rem(heads.slot + heads.turn, NREQ)]
    cached_len, new_len = clens[asked], nlens[asked]
    factor = HD**-0.5 * LOG2E
    key = lax.broadcasted_iota(jnp.int32, (1, NCTX * 64), 1)
    place, spot = key // 64, lax.rem(key, 64)
    rank = lax.rem(place, R)
    side = jnp.where(place < R, heads.b, 1 - heads.b)
    block = heads.block(rank, side)
    never = jnp.int32(1 << 20)
    cached_from = jnp.where(block * SPAN + spot < cached_len, -1, never)
    fresh_at = block * T + spot - SPAN
    fresh_from = jnp.where(fresh_at < new_len, fresh_at, never)
    seen_from = jnp.where(spot < SPAN, cached_from, fresh_from)

    def attend(k, carry):
        pair = wrap(heads.x - k, 4)
        for half in range(2):
            in_wait(QU, heads, 2 * pair + half, q_r)
        q = q_r[pl.ds(2 * pair, 2)].astype(F32).reshape(2 * T, 16, HD)
        row = lax.broadcasted_iota(jnp.int32, (2 * T * 8, 1), 0) // 8
        first, second = heads.block(2 * pair), heads.block(2 * pair + 1)
        when = jnp.where(row < T, first * T + row, second * T + row - T)
        outs = []
        for head in range(2):
            rows = q[:, head * 8 : head * 8 + 8].reshape(2 * T * 8, HD).astype(BF16)
            at = head * 128
            keys = kv_r[:, at : at + 64, :].reshape(NCTX * 64, HD)
            values = kv_r[:, at + 64 : at + 128, :].reshape(NCTX * 64, HD)
            scores = lax.dot_general(
                rows, keys, (((1,), (1,)), ((), ())), preferred_element_type=F32
            )
            scores = jnp.where(when >= seen_from, scores, -1e30)
            top = jnp.max(scores, axis=1, keepdims=True)
            weight = jnp.exp2((scores - top) * factor)
            total = jnp.sum(weight, axis=1, keepdims=True)
            out = jnp.dot(weight.astype(BF16), values, preferred_element_type=F32) / total
            out = jnp.where(when < new_len, out, 0.0)
            outs.append(out.reshape(2 * T, 8, HD))
        both = jnp.concatenate(outs, axis=1).astype(BF16)
        for half in range(2):
            o_s[2 * pair + half] = both[half * T : half * T + T]
            give(1, heads, 2 * pair + half, o_s, att)
        return carry

    lax.fori_loop(0, 4, attend, 0)

    own_len = nlens[own]

    def land_state(i, carry):
        st_copy(i).wait_recv()
        return carry

    lax.fori_loop(0, RUNS, land_state, 0)
    s1[...] = s0[...]

    def finish_run(i, carry):
        own_item = st_s[lax.rem(i + 3 * split, RUNS)].astype(F32)
        other = st_r[lax.rem(i + 3 * shift * (1 - mine.b), RUNS)].astype(F32)

        def advance(item, state):
            elapsed = item[S * TILES : (S + 1) * TILES] + item[(S + 1) * TILES :]
            decay = jnp.exp2(a2[...] * jnp.concatenate([elapsed] * S, axis=0))
            return decay * state + item[: S * TILES]

        ahead = s0[...]
        middle = advance(jnp.where(leads, own_item, other), ahead)
        after = advance(jnp.where(leads, other, own_item), middle)
        s0[...] = after
        begin = jnp.where(split == 1, after, jnp.where(leads, ahead, middle))

        def half(h, state):
            rank = i * 2 + h
            first = mine.block(rank) * T
            apart = jnp.logical_and(split == 1, rank == 2 * RUNS - 1)
            state = tuple(
                jnp.where(apart, s1[s * TILES : (s + 1) * TILES, :], state[s]) for s in range(S)
            )

            def step(t, state):
                at = rank * T + t
                parts = [yl[position(at), :], None]
                new = []
                for s in range(S):
                    h = av[at * S + s] * state[s]
                    new.append(h)
                    y = spread(S + s, at) * h
                    parts[s % 2] = y if parts[s % 2] is None else parts[s % 2] + y
                live = jnp.full((TILES, 128), first + t, jnp.int32) < own_len
                yl[position(at), :] = jnp.where(live, parts[0] + parts[1], 0.0)
                return tuple(new)

            state = lax.fori_loop(0, T, step, state)
            rows = [
                yl[pl.ds(rank * T * TILES + j, T, stride=TILES), :] for j in range(TILES)
            ]
            y_s[rank] = jnp.concatenate(rows, axis=1).astype(BF16)
            give(0, mine, rank, y_s, mix)
            return state

        lax.fori_loop(
            0, 2, half, tuple(begin[s * TILES : (s + 1) * TILES] for s in range(S))
        )
        return carry

    lax.fori_loop(0, RUNS, finish_run, 0)

    for kind, who, dst in ((0, mine, mix), (1, heads, att)):

        def land_out(giver, carry, kind=kind, who=who, dst=dst):
            own_part = jnp.logical_and(giver == g, lax.rem(who.slot + who.turn, NREQ) == 0)

            @pl.when(jnp.logical_not(own_part))
            def _():
                place = dst.at[giver]
                remote(
                    {"ctx": who.partner},
                    place,
                    place,
                    out_send.at[kind, giver],
                    out_recv.at[kind, giver],
                ).wait_recv()

            return carry

        lax.fori_loop(0, NREQ, land_out, 0)

    @pl.when(ends_run == 1)
    def _():
        def sent_edge(o, carry):
            edge_copy(o).wait_send()
            return carry

        lax.fori_loop(0, R, sent_edge, 0)

    for kind, who, src, dst in inputs:

        def sent_in(k, carry, kind=kind, who=who, src=src, dst=dst):
            in_copy(kind, who, lax.rem(who.slot + k, R), src, dst).wait_send()
            return carry

        lax.fori_loop(1, R, sent_in, 0)

    def sent_rest(n, carry):
        pass_copy(n).wait_send()
        for kind, who, src, dst in ((0, mine, y_s, mix), (1, heads, o_s, att)):

            @pl.when(jnp.logical_not(stays(who, n)))
            def _():
                out_copy(kind, who, n, src, dst).wait_send()

        return carry

    lax.fori_loop(0, R, sent_rest, 0)

    def sent_state(i, carry):
        st_copy(i).wait_send()
        return carry

    lax.fori_loop(0, RUNS, sent_state, 0)


def per_device(
    queries,
    kv_pool,
    new_kv,
    block_table,
    cached_len,
    new_len,
    mamba_x,
    conv_state,
    conv_weight,
    conv_bias,
    x_proj,
    dt_raw,
    a_log,
    skip_gain,
    ssm_state,
    target_group,
):
    pool = kv_pool[:, 0].transpose(1, 3, 0, 2, 4).reshape(-1, 2, 2 * PAGE, HD)
    fresh = new_kv.transpose(1, 3, 0, 2, 4)
    vmem = pl.BlockSpec(memory_space=pltpu.VMEM)
    smem = pl.BlockSpec(memory_space=pltpu.SMEM)
    dma = pltpu.SemaphoreType.DMA
    att, mix = pl.pallas_call(
        kernel,
        out_shape=(
            jax.ShapeDtypeStruct((NREQ, T, 16, HD), BF16),
            jax.ShapeDtypeStruct((NREQ, T, C), BF16),
        ),
        in_specs=[vmem] * 12 + [smem] * 4,
        out_specs=(vmem, vmem),
        scratch_shapes=[
            pltpu.VMEM((R, T, C), BF16),
            pltpu.VMEM((R, T, C), BF16),
            pltpu.VMEM((R, T, C), BF16),
            pltpu.VMEM((R, T, C), BF16),
            pltpu.VMEM((R, 256, HD), BF16),
            pltpu.VMEM((R, 256, HD), BF16),
            pltpu.VMEM((R, 256, HD), BF16),
            pltpu.VMEM((2 * R, 256, HD), BF16),
            pltpu.VMEM((3 * TILES, 128), F32),
            pltpu.VMEM((R, 3 * TILES, 128), BF16),
            pltpu.VMEM((RUNS, 3 * TILES, 128), BF16),
            pltpu.VMEM((6 * TILES, 128), F32),
            pltpu.VMEM((S * TILES, 128), F32),
            pltpu.VMEM((R * PAD * TILES, 128), F32),
            pltpu.VMEM((R * T * TILES, 128), F32),
            pltpu.VMEM((R * T * TILES, 128), F32),
            pltpu.VMEM((2 * S, R * T), F32),
            pltpu.VMEM((NTP - 1, 2 * S, R * T), F32),
            pltpu.VMEM((R * T, 2 * S), F32),
            pltpu.VMEM((2 * S * R * T, 128), F32),
            pltpu.VMEM((R * T * S, TILES, 128), F32),
            pltpu.VMEM((R * T * TILES, 128), F32),
            pltpu.VMEM((S * TILES, 128), F32),
            pltpu.VMEM((S * TILES, 128), F32),
            pltpu.VMEM((RUNS, (S + 2) * TILES, 128), BF16),
            pltpu.VMEM((RUNS, (S + 2) * TILES, 128), BF16),
            pltpu.VMEM((R, T, C), BF16),
            pltpu.VMEM((R, T, 16, HD), BF16),
            pltpu.SMEM((NREQ,), jnp.int32),
            dma((4, R)),
            dma((4, R)),
            dma((R,)),
            dma((RUNS,)),
            dma((R,)),
            dma((R,)),
            dma((RUNS,)),
            dma((RUNS,)),
            dma((NTP,)),
            dma((NTP,)),
            dma((2, R)),
            dma((2, NREQ)),
        ],
        compiler_params=pltpu.CompilerParams(
            collective_id=0, has_side_effects=True, vmem_limit_bytes=56 << 20
        ),
    )(
        queries, pool, fresh, mamba_x, dt_raw, conv_weight, conv_bias[None], skip_gain[None],
        a_log, conv_state.transpose(1, 0, 2), x_proj, ssm_state,
        block_table, cached_len[0], new_len[0], target_group[0],
    )
    return att, mix


def solution(mesh):
    in_specs = (
        P("req", "ctx", "tp", None),
        P(None, "req", "ctx", None, "tp", None),
        P(None, "req", "ctx", "tp", None),
        P("req", "ctx", None),
        P("req", None),
        P("req", None),
        P("req", "ctx", "tp"),
        P("req", None, "tp"),
        P(None, "tp"),
        P("tp"),
        P(None, "tp"),
        P("req", "ctx", "tp"),
        P(None, "tp"),
        P("tp"),
        P("req", None, "tp"),
        P("req", None),
    )
    out_specs = (P("req", "ctx", "tp", None), P("req", "ctx", "tp"))
    return jax.shard_map(
        per_device, mesh=mesh, in_specs=in_specs, out_specs=out_specs, check_vma=False
    )
```
